32 devices in a mesh: group: 2 (over y), col: 8 (over z, x), batch: 2 (over core).
Axes of the slice: x: 2, y: 2, z: 4, core: 2. Of those that a mesh axis runs over, the one named last changes fastest.
Arguments:
- base_input: bfloat16 [1024, 131072], P(('group', 'batch'), 'col'), parts along dimension 0, may hold values from -6 to 6
- cotangent: bfloat16 [1024, 131072], P(('group', 'batch'), 'col'), parts along dimension 0, may hold values from -1.5 to 1.5
- u_factor: bfloat16 [131072, 1024], P(('col', 'batch')), may hold values from -0.1875 to 0.1875
- v_factor: bfloat16 [131072, 1024], P(('col', 'batch')), may hold values from -0.015625 to 0.015625
- bias: bfloat16 [131072], P('col'), may hold values from -4 to 4
Outputs:
- grad_input: bfloat16 [1024, 131072], P(('group', 'batch'), 'col'), parts along dimension 0
- grad_u: bfloat16 [262144, 1024], P(('group', 'col', 'batch')), parts along dimension 0
- grad_v: bfloat16 [262144, 1024], P(('group', 'col', 'batch')), parts along dimension 0
- grad_bias: float32 [262144], P(('group', 'col', 'batch')), parts along dimension 0
The draws below stay inside these ranges and needn't reach their ends.
There are 2 independent parts, one for each index of `group`. The reference program is written for one: setup_inputs(seed, part) draws one part's arguments, and reference() takes and returns one part's arrays. A program takes and returns all parts, laid end to end along the dimension named above; an argument that names none is the same for every part. Nothing has to cross between parts.
All inputs are finite; a program needn't handle non-finite values.
Results may differ from the reference program's by a relative error of at most 0.0058.
Values may be sent and summed in bfloat16 or wider, within the bound.
No kernel may reach another device: no remote copies, remote signals or barrier semaphores. Data moves between devices by JAX's collectives and lax.ppermute only.
A program may use at most 640 MiB of HBM per device.

```python
import jax
import jax.numpy as jnp

WIDTH = 131072
RANK = 1024
SAMPLES = 512


def levels(own_key, extent, pieces, smallest, high):
    level, own = 1.0, jax.random.fold_in(own_key, 6)
    for axis_at, shards_of in pieces:
        steps = jnp.exp(jax.random.uniform(jax.random.fold_in(own, axis_at), (shards_of,), jnp.float32, smallest / len(pieces), high / len(pieces)))
        level = level * jnp.repeat(steps, extent[axis_at] // shards_of).reshape([-1 if axis == axis_at else 1 for axis in range(len(extent))])
    return level


def scatter_about(own_key, dims, spread, most, cuts=(), held_as=jnp.bfloat16):
    entries = spread * jax.random.normal(own_key, dims, jnp.float32)
    if cuts:
        entries = entries * levels(own_key, dims, cuts, -0.22, 0.18)
    return jnp.clip(entries, -most, most).astype(held_as)


def setup_inputs(seed: int = 0, part: int = 0) -> dict:
    arg_keys = jax.random.split(jax.random.key(seed), 6)
    own_keys = jax.random.split(jax.random.fold_in(arg_keys[5], part), 6)
    return {
        "base_input": scatter_about(own_keys[0], (SAMPLES, WIDTH), 1.0, 6.0, ((0, 2), (1, 8))),
        "cotangent": scatter_about(own_keys[1], (SAMPLES, WIDTH), 0.25, 1.5, ((0, 2), (1, 8))),
        "u_factor": scatter_about(arg_keys[2], (WIDTH, RANK), RANK ** -0.5, 0.1875, ((0, 16),)),
        "v_factor": scatter_about(arg_keys[3], (WIDTH, RANK), WIDTH ** -0.5, 0.015625, ((0, 16),)),
        "bias": scatter_about(arg_keys[4], (WIDTH,), 1.0, 4.0, ((0, 8),)),
    }


def reference(base_input, cotangent, u_factor, v_factor, bias):
    projected = jnp.dot(base_input, v_factor, preferred_element_type=jnp.float32)
    proj_bf = projected.astype(jnp.bfloat16)
    expanded = jnp.dot(proj_bf, u_factor.T, preferred_element_type=jnp.float32)
    cot_f = cotangent.astype(jnp.float32)
    grad_hidden = (cot_f * base_input.astype(jnp.float32)).astype(jnp.bfloat16)
    grad_proj = jnp.dot(grad_hidden, u_factor, preferred_element_type=jnp.float32)
    gproj_bf = grad_proj.astype(jnp.bfloat16)
    back = jnp.dot(gproj_bf, v_factor.T, preferred_element_type=jnp.float32)
    grad_input = (cot_f * (expanded + bias.astype(jnp.float32)[None, :]) + cot_f + back).astype(jnp.bfloat16)
    grad_u = jnp.dot(grad_hidden.T, proj_bf, preferred_element_type=jnp.float32).astype(jnp.bfloat16)
    grad_v = jnp.dot(base_input.T, gproj_bf, preferred_element_type=jnp.float32).astype(jnp.bfloat16)
    grad_bias = jnp.sum(grad_hidden.astype(jnp.float32), axis=0)
    return (grad_input, grad_u, grad_v, grad_bias)
```

```python
import functools

import jax
import jax.numpy as jnp
from jax import lax
from jax.experimental import pallas as pl
from jax.experimental.pallas import tpu as pltpu
from jax.sharding import PartitionSpec as P

BF, F32 = jnp.bfloat16, jnp.float32
ANY = pl.BlockSpec(memory_space=pl.ANY)
MIB = 1 << 20


def params(mib=56):
    return pltpu.CompilerParams(vmem_limit_bytes=mib * MIB)


def cost(flops, nbytes):
    return pl.CostEstimate(flops=int(flops), bytes_accessed=int(nbytes), transcendentals=0)


def call(body, name, at, grid, ins, in_specs, outs, out_specs, scratch=(), flops=0, aliases=None, mib=56):
    nbytes = sum(a.size * a.dtype.itemsize for a in list(ins) + list(outs))
    return pl.pallas_call(
        body,
        out_shape=tuple(outs),
        grid_spec=pltpu.PrefetchScalarGridSpec(
            num_scalar_prefetch=1, grid=grid, in_specs=in_specs, out_specs=tuple(out_specs), scratch_shapes=list(scratch)
        ),
        input_output_aliases=aliases or {},
        compiler_params=params(mib),
        cost_estimate=cost(flops, nbytes),
        name=name,
    )(at, *ins)


def shape(dims, dtype):
    return jax.ShapeDtypeStruct(dims, dtype)


def cut_half(at, x, half):
    rows = x.shape[0]
    pieces = 4
    step = rows // pieces

    def body(at_ref, x_ref, o_ref, sems):
        start = pl.multiple_of((1 - at_ref[0]) * half, half)
        copies = [
            pltpu.make_async_copy(
                x_ref.at[pl.ds(i * step, step), pl.ds(start, half)], o_ref.at[pl.ds(i * step, step), :], sems.at[i]
            )
            for i in range(pieces)
        ]
        for c in copies:
            c.start()
        for c in copies:
            c.wait()

    return call(
        body, "cut_half", at, (1,), [x], [ANY], [shape((rows, half), x.dtype)], [ANY], [pltpu.SemaphoreType.DMA((pieces,))]
    )[0]


def put_half(at, part, out):
    rows, half = part.shape
    pieces = 4
    step = rows // pieces

    def body(at_ref, p_ref, i_ref, o_ref, sems):
        start = pl.multiple_of((1 - at_ref[0]) * half, half)
        copies = [
            pltpu.make_async_copy(
                p_ref.at[pl.ds(i * step, step), :], o_ref.at[pl.ds(i * step, step), pl.ds(start, half)], sems.at[i]
            )
            for i in range(pieces)
        ]
        for c in copies:
            c.start()
        for c in copies:
            c.wait()

    return call(
        body,
        "put_half",
        at,
        (1,),
        [part, out],
        [ANY, ANY],
        [shape(out.shape, out.dtype)],
        [ANY],
        [pltpu.SemaphoreType.DMA((pieces,))],
        aliases={2: 0},
    )[0]


def project(at, x, v, offset):
    rows, half, rank = x.shape[0], v.shape[0], v.shape[1]
    tk = min(1024, half)
    steps = half // tk

    def body(at_ref, x_ref, v_ref, o_ref, acc):
        k = pl.program_id(0)
        part = jnp.dot(x_ref[...], v_ref[...], preferred_element_type=F32)

        @pl.when(k == 0)
        def _():
            acc[...] = part

        @pl.when(k > 0)
        def _():
            acc[...] += part

        @pl.when(k == steps - 1)
        def _():
            o_ref[...] = acc[...].astype(BF)

    where = (lambda k, at: (0, at[0] * steps + k)) if offset else (lambda k, at: (0, k))
    return call(
        body,
        "project",
        at,
        (steps,),
        [x, v],
        [pl.BlockSpec((rows, tk), where), pl.BlockSpec((tk, rank), lambda k, at: (k, 0))],
        [shape((rows, rank), BF)],
        [pl.BlockSpec((rows, rank), lambda k, at: (0, 0))],
        [pltpu.VMEM((rows, rank), F32)],
        flops=2 * rows * half * rank,
    )[0]


def hidden(c, x):
    return (c.astype(F32) * x.astype(F32)).astype(BF)


def back_project(at, x, x_o, c, c_o, u):
    rows, half, rank = x.shape[0], u.shape[0], u.shape[1]
    tk = min(1024, half)
    steps = half // tk

    def body(at_ref, x_ref, xo_ref, c_ref, co_ref, u_ref, own_ref, oth_ref, b_ref, h, acc):
        k = pl.program_id(0)
        h[:rows, :] = hidden(c_ref[...], x_ref[...])
        h[rows:, :] = hidden(co_ref[...], xo_ref[...])
        b_ref[...] = jnp.sum(h[...].astype(F32), axis=0, keepdims=True)
        part = jnp.dot(h[...], u_ref[...], preferred_element_type=F32)

        @pl.when(k == 0)
        def _():
            acc[...] = part

        @pl.when(k > 0)
        def _():
            acc[...] += part

        @pl.when(k == steps - 1)
        def _():
            own_ref[...] = acc[:rows, :].astype(BF)
            oth_ref[...] = acc[rows:, :].astype(BF)

    own = pl.BlockSpec((rows, tk), lambda k, at: (0, at[0] * steps + k))
    oth = pl.BlockSpec((rows, tk), lambda k, at: (0, k))
    full = pl.BlockSpec((rows, rank), lambda k, at: (0, 0))
    return call(
        body,
        "back_project",
        at,
        (steps,),
        [x, x_o, c, c_o, u],
        [own, oth, own, oth, pl.BlockSpec((tk, rank), lambda k, at: (k, 0))],
        [shape((rows, rank), BF), shape((rows, rank), BF), shape((1, half), F32)],
        [full, full, pl.BlockSpec((1, tk), lambda k, at: (0, k))],
        [pltpu.VMEM((2 * rows, tk), BF), pltpu.VMEM((2 * rows, rank), F32)],
        flops=4 * rows * half * rank,
    )


def u_grad(at, x, x_o, c, c_o, p, p_o, half):
    rows, rank = p.shape
    tw = min(1024, half)
    steps = half // tw

    def body(at_ref, x_ref, xo_ref, c_ref, co_ref, p_ref, po_ref, o_ref):
        h = jnp.concatenate([hidden(c_ref[...], x_ref[...]), hidden(co_ref[...], xo_ref[...])], 0)
        pp = jnp.concatenate([p_ref[...], po_ref[...]], 0)
        o_ref[...] = lax.dot_general(h, pp, (((0,), (0,)), ((), ())), preferred_element_type=F32).astype(BF)

    own = pl.BlockSpec((rows, tw), lambda k, at: (0, at[0] * steps + k))
    oth = pl.BlockSpec((rows, tw), lambda k, at: (0, k))
    full = pl.BlockSpec((rows, rank), lambda k, at: (0, 0))
    return call(
        body,
        "u_grad",
        at,
        (steps,),
        [x, x_o, c, c_o, p, p_o],
        [own, oth, own, oth, full, full],
        [shape((half, rank), BF)],
        [pl.BlockSpec((tw, rank), lambda k, at: (k, 0))],
        flops=4 * rows * half * rank,
    )[0]


def v_grad(at, x, x_o, g, g_o, half):
    rows, rank = g.shape
    tw = min(1024, half)
    steps = half // tw

    def body(at_ref, x_ref, xo_ref, g_ref, go_ref, o_ref):
        xx = jnp.concatenate([x_ref[...], xo_ref[...]], 0)
        gg = jnp.concatenate([g_ref[...], go_ref[...]], 0)
        o_ref[...] = lax.dot_general(xx, gg, (((0,), (0,)), ((), ())), preferred_element_type=F32).astype(BF)

    own = pl.BlockSpec((rows, tw), lambda k, at: (0, at[0] * steps + k))
    oth = pl.BlockSpec((rows, tw), lambda k, at: (0, k))
    full = pl.BlockSpec((rows, rank), lambda k, at: (0, 0))
    return call(
        body,
        "v_grad",
        at,
        (steps,),
        [x, x_o, g, g_o],
        [own, oth, full, full],
        [shape((half, rank), BF)],
        [pl.BlockSpec((tw, rank), lambda k, at: (k, 0))],
        flops=4 * rows * half * rank,
    )[0]


def input_grad(at, c, c_o, u, v, bias, p, p_o, g, g_o):
    rows, rank = p.shape
    half, width = u.shape[0], c.shape[1]
    tw = min(1024, half)
    steps = half // tw

    def body(at_ref, c_ref, co_ref, u_ref, v_ref, b_ref, p_ref, po_ref, g_ref, go_ref, own_ref, oth_ref):
        pp = jnp.concatenate([p_ref[...], po_ref[...]], 0)
        gg = jnp.concatenate([g_ref[...], go_ref[...]], 0)
        nt = (((1,), (1,)), ((), ()))
        ex = lax.dot_general(pp, u_ref[...], nt, preferred_element_type=F32)
        bk = lax.dot_general(gg, v_ref[...], nt, preferred_element_type=F32)
        ex = ex + b_ref[...].astype(F32)
        cf, cof = c_ref[...].astype(F32), co_ref[...].astype(F32)
        own_ref[...] = (cf * ex[:rows] + cf + bk[:rows]).astype(BF)
        oth_ref[...] = (cof * ex[rows:] + cof + bk[rows:]).astype(BF)

    own = pl.BlockSpec((rows, tw), lambda k, at: (0, at[0] * steps + k))
    oth = pl.BlockSpec((rows, tw), lambda k, at: (0, k))
    full = pl.BlockSpec((rows, rank), lambda k, at: (0, 0))
    fac = pl.BlockSpec((tw, rank), lambda k, at: (k, 0))
    return call(
        body,
        "input_grad",
        at,
        (steps,),
        [c, c_o, u, v, bias, p, p_o, g, g_o],
        [own, oth, fac, fac, pl.BlockSpec((1, tw), lambda k, at: (0, at[0] * steps + k)), full, full, full, full],
        [shape((rows, width), BF), shape((rows, half), BF)],
        [own, oth],
        flops=8 * rows * half * rank,
    )


def pieces_of(at, a, b, n):
    rows, rank = a.shape
    each = rows // n

    def body(at_ref, a_ref, b_ref, *outs):
        for d in range(n):
            here = pl.ds(pl.multiple_of((at_ref[1] ^ d) * each, each), each)
            outs[d][...] = (a_ref[here, :].astype(F32) + b_ref[here, :].astype(F32)).astype(BF)

    full = pl.BlockSpec((rows, rank), lambda i, at: (0, 0))
    one = pl.BlockSpec((each, rank), lambda i, at: (0, 0))
    return call(body, "pieces_of", at, (1,), [a, b], [full, full], [shape((each, rank), BF)] * n, [one] * n, mib=16)


def add_pieces(at, parts):
    def body(at_ref, *refs):
        total = refs[0][...].astype(F32)
        for r in refs[1:-1]:
            total += r[...].astype(F32)
        refs[-1][...] = total.astype(BF)

    one = pl.BlockSpec(parts[0].shape, lambda i, at: (0, 0))
    return call(body, "add_pieces", at, (1,), parts, [one] * len(parts), [shape(parts[0].shape, BF)], [one], mib=16)[0]


def join_pieces(at, parts):
    n = len(parts)
    each, rank = parts[0].shape

    def body(at_ref, *refs):
        for d in range(n):
            here = pl.ds(pl.multiple_of((at_ref[1] ^ d) * each, each), each)
            refs[-1][here, :] = refs[d][...]

    one = pl.BlockSpec((each, rank), lambda i, at: (0, 0))
    full = pl.BlockSpec((n * each, rank), lambda i, at: (0, 0))
    return call(body, "join_pieces", at, (1,), parts, [one] * n, [shape((n * each, rank), BF)], [full], mib=16)[0]


def solution(mesh):
    n = mesh.shape["col"]
    swap = [(0, 1), (1, 0)]

    def trade(a):
        return lax.ppermute(a, "batch", swap)

    def to(a, d):
        return lax.ppermute(a, "col", [(i, i ^ d) for i in range(n)])

    def direct_sum(at, mine, theirs):
        parts = pieces_of(at, mine, theirs, n)
        parts = [parts[0]] + [to(parts[d], d) for d in range(1, n)]
        total = add_pieces(at, parts)
        return join_pieces(at, [total] + [to(total, d) for d in range(1, n)])

    def plain_sum(mine, theirs):
        both = mine.astype(F32) + theirs.astype(F32)
        if both.shape[0] % (16 * n):
            return lax.psum(both, "col").astype(BF)
        total = lax.psum_scatter(both.astype(BF), "col", scatter_dimension=0, tiled=True)
        return lax.all_gather(total, "col", axis=0, tiled=True)

    def local(x, c, u, v, bias):
        half = u.shape[0]
        core = lax.axis_index("batch")
        at = jnp.stack([core, lax.axis_index("col")]).astype(jnp.int32)
        direct = x.shape[0] % (16 * n) == 0 and n & (n - 1) == 0
        x_o = trade(cut_half(at, x, half))
        c_o = trade(cut_half(at, c, half))
        own = project(at, x, v, True)
        theirs = trade(own)
        mine = project(at, x_o, v, False)
        p_o = plain_sum(mine, theirs)
        p = trade(p_o)
        own_g, mine_g, b_sum = back_project(at, x, x_o, c, c_o, u)
        theirs_g = trade(own_g)
        g_o = direct_sum(at, mine_g, theirs_g) if direct else plain_sum(mine_g, theirs_g)
        g = trade(g_o)
        grad_u = u_grad(at, x, x_o, c, c_o, p, p_o, half)
        out, out_o = input_grad(at, c, c_o, u, v, bias[None, :], p, p_o, g, g_o)
        back = trade(out_o)
        grad_v = v_grad(at, x, x_o, g, g_o, half)
        return put_half(at, back, out), grad_u, grad_v, b_sum[0]

    return jax.shard_map(
        local,
        mesh=mesh,
        in_specs=(
            P(("group", "batch"), "col"),
            P(("group", "batch"), "col"),
            P(("col", "batch"), None),
            P(("col", "batch"), None),
            P("col"),
        ),
        out_specs=(
            P(("group", "batch"), "col"),
            P(("group", "col", "batch"), None),
            P(("group", "col", "batch"), None),
            P(("group", "col", "batch")),
        ),
        check_vma=False,
    )
```

```python
import jax
import jax.numpy as jnp
from jax import lax
from jax.experimental import pallas as pl
from jax.experimental.pallas import tpu as pltpu
from jax.sharding import PartitionSpec as P

BF, F32 = jnp.bfloat16, jnp.float32
MIB = 1 << 20
NT = (((1,), (1,)), ((), ()))
TN = (((0,), (0,)), ((), ()))


def call(body, name, at, ins, outs, scratch=(), flops=0, aliases=None, mib=4, after=()):
    specs = {"v": pl.BlockSpec(memory_space=pltpu.VMEM), "h": pl.BlockSpec(memory_space=pl.ANY)}
    spaces = {"v": pltpu.VMEM, "h": pltpu.HBM}
    nbytes = sum(a.size * a.dtype.itemsize for a, _ in ins)
    skip = 1 + len(ins)
    ins = list(ins) + [(a, "v") for a in after]
    args = [pltpu.with_memory_space_constraint(a, spaces[w]) for a, w in ins]
    return pl.pallas_call(
        lambda *refs: body(*refs[:skip], *refs[skip + len(after) :]),
        out_shape=tuple(spaces[w](dims, dtype) for dims, dtype, w in outs),
        in_specs=[pl.BlockSpec(memory_space=pltpu.SMEM)] + [specs[w] for _, w in ins],
        out_specs=tuple(specs[w] for _, _, w in outs),
        scratch_shapes=list(scratch),
        input_output_aliases=aliases or {},
        compiler_params=pltpu.CompilerParams(vmem_limit_bytes=mib * MIB),
        cost_estimate=pl.CostEstimate(flops=int(flops), bytes_accessed=int(nbytes), transcendentals=0),
        name=name,
    )(at, *args)


def at_block(i, size):
    return pl.ds(pl.multiple_of(i * size, size), size)


def dma(n):
    return pltpu.SemaphoreType.DMA((n,))


def cut_half(at, x, half, after=()):
    rows = x.shape[0]
    n = 4
    step = rows // n

    def body(at_ref, x_ref, o_ref, sems):
        copies = [
            pltpu.make_async_copy(
                x_ref.at[pl.ds(i * step, step), at_block(1 - at_ref[0], half)], o_ref.at[pl.ds(i * step, step), :], sems.at[i]
            )
            for i in range(n)
        ]
        for c in copies:
            c.start()
        for c in copies:
            c.wait()

    return call(body, "cut_half", at, [(x, "h")], [((rows, half), BF, "v")], [dma(n)], after=after)[0]


def put_half(at, part, out):
    rows, half = part.shape
    n = 4
    step = rows // n

    def body(at_ref, p_ref, i_ref, o_ref, sems):
        copies = [
            pltpu.make_async_copy(
                p_ref.at[pl.ds(i * step, step), :], o_ref.at[pl.ds(i * step, step), at_block(1 - at_ref[0], half)], sems.at[i]
            )
            for i in range(n)
        ]
        for c in copies:
            c.start()
        for c in copies:
            c.wait()

    return call(body, "put_half", at, [(part, "v"), (out, "h")], [(out.shape, BF, "h")], [dma(n)], aliases={2: 0}, mib=4)[0]


def project_own(at, x, v, after=()):
    rows, (half, rank) = x.shape[0], v.shape
    tk = min(1024, half)
    n = half // tk

    def body(at_ref, x_ref, v_ref, p_ref, xv_ref, vv_ref, acc, x_sem, v_sem):
        def x_copy(k):
            src = x_ref.at[:, pl.ds(pl.multiple_of(at_ref[0] * half + k * tk, tk), tk)]
            return pltpu.make_async_copy(src, xv_ref.at[:, at_block(k, tk)], x_sem.at[k])

        def v_copy(k):
            return pltpu.make_async_copy(v_ref.at[at_block(k, tk), :], vv_ref.at[at_block(k, tk), :], v_sem.at[k])

        for k in range(n):
            x_copy(k).start()
            v_copy(k).start()
        acc[...] = jnp.zeros_like(acc)

        @pl.loop(0, n)
        def _(k):
            x_copy(k).wait()
            v_copy(k).wait()
            acc[...] += jnp.dot(xv_ref[:, at_block(k, tk)], vv_ref[at_block(k, tk), :], preferred_element_type=F32)

        p_ref[...] = acc[...].astype(BF)

    return call(
        body,
        "project_own",
        at,
        [(x, "h"), (v, "h")],
        [((rows, rank), BF, "v"), ((rows, half), BF, "v"), ((half, rank), BF, "v")],
        [pltpu.VMEM((rows, rank), F32), dma(n), dma(n)],
        flops=2 * rows * half * rank,
        mib=5,
        after=after,
    )


def project_other(at, x_o, v):
    rows, (half, rank) = x_o.shape[0], v.shape
    tk = min(1024, half)

    def body(at_ref, x_ref, v_ref, p_ref):
        p_ref[...] = jnp.zeros_like(p_ref)

        @pl.loop(0, half // tk)
        def _(k):
            p_ref[...] += jnp.dot(x_ref[:, at_block(k, tk)], v_ref[at_block(k, tk), :], preferred_element_type=F32)

    return call(
        body, "project_other", at, [(x_o, "v"), (v, "v")], [((rows, rank), F32, "v")], flops=2 * rows * half * rank
    )[0]


def hidden(c, x):
    return (c.astype(F32) * x.astype(F32)).astype(BF)


def back_project(at, x, x_o, c, c_o, u, after=()):
    rows, (half, rank) = x.shape[0], u.shape
    tk = min(512, half)
    n = half // tk
    slots = min(4, n)

    def body(at_ref, x_ref, xo_ref, c_ref, co_ref, u_ref, own_ref, oth_ref, b_ref, cv_ref, uv, h, acc, c_sem, u_sem):
        def c_copy(k):
            src = c_ref.at[:, pl.ds(pl.multiple_of(at_ref[0] * half + k * tk, tk), tk)]
            return pltpu.make_async_copy(src, cv_ref.at[:, at_block(k, tk)], c_sem.at[k])

        def u_copy(k):
            slot = lax.rem(k, slots)
            return pltpu.make_async_copy(u_ref.at[at_block(k, tk), :], uv.at[slot], u_sem.at[slot])

        for k in range(n):
            c_copy(k).start()
            if k < slots:
                u_copy(k).start()
        acc[...] = jnp.zeros_like(acc)

        @pl.loop(0, n)
        def _(k):
            here = at_block(k, tk)
            c_copy(k).wait()
            h[:rows, :] = hidden(cv_ref[:, here], x_ref[:, here])
            h[rows:, :] = hidden(co_ref[:, here], xo_ref[:, here])
            b_ref[:, here] = jnp.sum(h[...].astype(F32), axis=0, keepdims=True)
            u_copy(k).wait()
            acc[...] += jnp.dot(h[...], uv[lax.rem(k, slots)], preferred_element_type=F32)

            @pl.when(k + slots < n)
            def _():
                u_copy(k + slots).start()

        own_ref[...] = acc[:rows, :].astype(BF)
        oth_ref[...] = acc[rows:, :]

    return call(
        body,
        "back_project",
        at,
        [(x, "v"), (x_o, "v"), (c, "h"), (c_o, "v"), (u, "h")],
        [((rows, rank), BF, "v"), ((rows, rank), F32, "v"), ((1, half), F32, "v"), ((rows, half), BF, "v")],
        [
            pltpu.VMEM((slots, tk, rank), BF),
            pltpu.VMEM((2 * rows, tk), BF),
            pltpu.VMEM((2 * rows, rank), F32),
            dma(n),
            dma(slots),
        ],
        flops=4 * rows * half * rank,
        mib=12,
        after=after,
    )


def factor_grad(at, name, ins, get, p, p_o, half):
    rows, rank = p.shape
    tw = min(512, half)
    n = half // tw
    m = len(ins)

    def body(at_ref, *refs):
        p_ref, po_ref, o_ref, stage, both, left, sems = refs[m:]
        both[:rows, :] = p_ref[...]
        both[rows:, :] = po_ref[...]

        def out(k, slot):
            return pltpu.make_async_copy(stage.at[slot], o_ref.at[at_block(k, tw), :], sems.at[slot])

        @pl.loop(0, n)
        def _(k):
            slot = lax.rem(k, 2)
            here = at_block(k, tw)
            own, oth = get([r[:, here] for r in refs[:m]])
            left[:rows, :] = own
            left[rows:, :] = oth

            @pl.when(k >= 2)
            def _():
                out(k, slot).wait()

            stage[slot] = lax.dot_general(left[...], both[...], TN, preferred_element_type=F32).astype(BF)
            out(k, slot).start()

        for k in range(max(0, n - 2), n):
            out(k, k % 2).wait()

    return call(
        body,
        name,
        at,
        [(a, "v") for a in ins] + [(p, "v"), (p_o, "v")],
        [((half, rank), BF, "h")],
        [pltpu.VMEM((2, tw, rank), BF), pltpu.VMEM((2 * rows, rank), BF), pltpu.VMEM((2 * rows, tw), BF), dma(2)],
        flops=4 * rows * half * rank,
        mib=8,
    )[0]


def input_grad(at, c, c_o, u, v, bias, p, p_o, g, g_o, width):
    rows, rank = p.shape
    half = u.shape[0]
    tw = min(512, half)
    n = half // tw
    slots = min(3, n)

    def body(
        at_ref, c_ref, co_ref, u_ref, v_ref, b_ref, p_ref, po_ref, g_ref, go_ref, own_ref, oth_ref, stage, uv, vv, pp, gg, sems, u_sem, v_sem
    ):
        def u_copy(k):
            slot = lax.rem(k, slots)
            return pltpu.make_async_copy(u_ref.at[at_block(k, tw), :], uv.at[slot], u_sem.at[slot])

        def v_copy(k):
            slot = lax.rem(k, slots)
            return pltpu.make_async_copy(v_ref.at[at_block(k, tw), :], vv.at[slot], v_sem.at[slot])

        for k in range(slots):
            u_copy(k).start()
            v_copy(k).start()
        pp[:rows, :] = p_ref[...]
        pp[rows:, :] = po_ref[...]
        gg[:rows, :] = g_ref[...]
        gg[rows:, :] = go_ref[...]

        def out(k, slot):
            there = pl.ds(pl.multiple_of(at_ref[0] * half + k * tw, tw), tw)
            return pltpu.make_async_copy(stage.at[slot], own_ref.at[:, there], sems.at[slot])

        @pl.loop(0, n)
        def _(k):
            slot = lax.rem(k, 2)
            here = at_block(k, tw)
            there = pl.ds(pl.multiple_of(at_ref[0] * half + k * tw, tw), tw)
            u_copy(k).wait()
            ex = lax.dot_general(pp[...], uv[lax.rem(k, slots)], NT, preferred_element_type=F32) + b_ref[:, there].astype(F32)
            v_copy(k).wait()
            bk = lax.dot_general(gg[...], vv[lax.rem(k, slots)], NT, preferred_element_type=F32)
            cf, cof = c_ref[:, here].astype(F32), co_ref[:, here].astype(F32)

            @pl.when(k >= 2)
            def _():
                out(k, slot).wait()

            stage[slot] = (cf * ex[:rows] + cf + bk[:rows]).astype(BF)
            oth_ref[:, here] = (cof * ex[rows:] + cof + bk[rows:]).astype(BF)
            out(k, slot).start()

            @pl.when(k + slots < n)
            def _():
                u_copy(k + slots).start()
                v_copy(k + slots).start()

        for k in range(max(0, n - 2), n):
            out(k, k % 2).wait()

    return call(
        body,
        "input_grad",
        at,
        [(a, "h" if a is u or a is v else "v") for a in (c, c_o, u, v, bias, p, p_o, g, g_o)],
        [((rows, width), BF, "h"), ((rows, half), BF, "v")],
        [
            pltpu.VMEM((2, rows, tw), BF),
            pltpu.VMEM((slots, tw, rank), BF),
            pltpu.VMEM((slots, tw, rank), BF),
            pltpu.VMEM((2 * rows, rank), BF),
            pltpu.VMEM((2 * rows, rank), BF),
            dma(2),
            dma(slots),
            dma(slots),
        ],
        flops=8 * rows * half * rank,
        mib=16,
    )


def plus(a, b):
    return (a.astype(F32) + b.astype(F32)).astype(BF)


def pair_pieces(at, a, b, n):
    rows, rank = a.shape
    each = rows // n

    def body(at_ref, a_ref, b_ref, o_ref):
        for j in range(n):
            here = slice(j * each, (j + 1) * each)
            o_ref[j] = plus(a_ref[here, :], b_ref[here, :])

    return call(body, "pair_pieces", at, [(a, "v"), (b, "v")], [((n, each, rank), BF, "v")], mib=4)[0]


def sum_spread(at, a):
    n = a.shape[0]

    def body(at_ref, a_ref, o_ref):
        total = a_ref[0].astype(F32)
        for j in range(1, n):
            total += a_ref[j].astype(F32)
        total = total.astype(BF)
        for j in range(n):
            o_ref[j] = total

    return call(body, "sum_spread", at, [(a, "v")], [(a.shape, BF, "v")], mib=4)[0]


def pair_halves(at, a, b):
    rows, rank = a.shape
    each = rows // 2

    def body(at_ref, a_ref, b_ref, keep_ref, send_ref):
        bit = at_ref[1] & 1
        for i, o_ref in ((bit, keep_ref), (1 - bit, send_ref)):
            here = at_block(i, each)
            o_ref[...] = plus(a_ref[here, :], b_ref[here, :])

    return call(body, "pair_halves", at, [(a, "v"), (b, "v")], [((each, rank), BF, "v")] * 2, mib=4)


def pieces_of(at, a, b, m):
    rows, rank = a.shape
    each = rows // m

    def body(at_ref, a_ref, b_ref, *outs):
        for d in range(m):
            here = at_block((at_ref[1] >> 1) ^ d, each)
            outs[d][...] = plus(a_ref[here, :], b_ref[here, :])

    return call(body, "pieces_of", at, [(a, "v"), (b, "v")], [((each, rank), BF, "v")] * m, mib=4)


def add_pieces(at, parts):
    def body(at_ref, *refs):
        total = refs[0][...].astype(F32)
        for r in refs[1:-1]:
            total += r[...].astype(F32)
        refs[-1][...] = total.astype(BF)

    return call(body, "add_pieces", at, [(a, "v") for a in parts], [(parts[0].shape, BF, "v")], mib=4)[0]


def join_pieces(at, parts, shift):
    n = len(parts)
    each, rank = parts[0].shape

    def body(at_ref, *refs):
        for d in range(n):
            refs[-1][at_block(((at_ref[1] >> shift) & (n - 1)) ^ d, each), :] = refs[d][...]

    return call(body, "join_pieces", at, [(a, "v") for a in parts], [((n * each, rank), BF, "v")], mib=4)[0]


def solution(mesh):
    n = mesh.shape["col"]
    swap = [(0, 1), (1, 0)]

    def trade(a):
        return lax.ppermute(a, "batch", swap)

    def to(a, d):
        return lax.ppermute(a, "col", [(i, i ^ d) for i in range(n)])

    def staged_sum(at, mine, theirs):
        m = n // 2
        keep, send = pair_halves(at, mine, theirs)
        parts = pieces_of(at, keep, to(send, 1), m)
        total = add_pieces(at, [parts[0]] + [to(parts[d], 2 * d) for d in range(1, m)])
        half = join_pieces(at, [total] + [to(total, 2 * d) for d in range(1, m)], 1)
        return join_pieces(at, [half, to(half, 1)], 0)

    def traded_sum(at, mine, theirs):
        def spread(a):
            return lax.all_to_all(a, "col", split_axis=0, concat_axis=0, tiled=True)

        return spread(sum_spread(at, spread(pair_pieces(at, mine, theirs, n)))).reshape(mine.shape)

    def plain_sum(mine, theirs):
        return lax.psum(mine.astype(F32) + theirs.astype(F32), "col").astype(BF)

    def local(x, c, u, v, bias):
        half, width = u.shape[0], x.shape[1]
        core = lax.axis_index("batch")
        at = jnp.stack([core, lax.axis_index("col")]).astype(jnp.int32)
        direct = x.shape[0] % (16 * n) == 0 and n & (n - 1) == 0 and n > 2
        x_s = cut_half(at, x, half)
        x_o = trade(x_s)
        c_s = cut_half(at, c, half, [x_s])
        c_o = trade(c_s)
        own, x_own, v_in = project_own(at, x, v, [c_s])
        theirs = trade(own)
        mine = project_other(at, x_o, v_in)
        p_o = staged_sum(at, mine, theirs) if direct else plain_sum(mine, theirs)
        p = trade(p_o)
        own_g, mine_g, b_sum, c_own = back_project(at, x_own, x_o, c, c_o, u, [mine])
        theirs_g = trade(own_g)
        g_o = traded_sum(at, mine_g, theirs_g) if direct else plain_sum(mine_g, theirs_g)
        g = trade(g_o)
        grad_u = factor_grad(
            at,
            "u_grad",
            [x_own, x_o, c_own, c_o],
            lambda t: (hidden(t[2], t[0]), hidden(t[3], t[1])),
            p,
            p_o,
            half,
        )
        out, out_o = input_grad(at, c_own, c_o, u, v, bias[None, :], p, p_o, g, g_o, width)
        back = trade(out_o)
        grad_v = factor_grad(at, "v_grad", [x_own, x_o], lambda t: (t[0], t[1]), g, g_o, half)
        return put_half(at, back, out), grad_u, grad_v, b_sum[0]

    return jax.shard_map(
        local,
        mesh=mesh,
        in_specs=(
            P(("group", "batch"), "col"),
            P(("group", "batch"), "col"),
            P(("col", "batch"), None),
            P(("col", "batch"), None),
            P("col"),
        ),
        out_specs=(
            P(("group", "batch"), "col"),
            P(("group", "col", "batch"), None),
            P(("group", "col", "batch"), None),
            P(("group", "col", "batch")),
        ),
        check_vma=False,
    )
```

```python
import jax
import jax.numpy as jnp
from jax import lax
from jax.experimental import pallas as pl
from jax.experimental.pallas import tpu as pltpu
from jax.sharding import PartitionSpec as P

BF, F32 = jnp.bfloat16, jnp.float32
MIB = 1 << 20
NT = (((1,), (1,)), ((), ()))


def call(body, name, at, ins, outs, scratch=(), flops=0, aliases=None, mib=4, after=()):
    specs = {"v": pl.BlockSpec(memory_space=pltpu.VMEM), "h": pl.BlockSpec(memory_space=pl.ANY)}
    spaces = {"v": pltpu.VMEM, "h": pltpu.HBM}
    nbytes = sum(a.size * a.dtype.itemsize for a, _ in ins)
    skip = 1 + len(ins)
    ins = list(ins) + [a if isinstance(a, tuple) else (a, "v") for a in after]
    args = [pltpu.with_memory_space_constraint(a, spaces[w]) for a, w in ins]
    return pl.pallas_call(
        lambda *refs: body(*refs[:skip], *refs[skip + len(after) :]),
        out_shape=tuple(spaces[w](dims, dtype) for dims, dtype, w in outs),
        in_specs=[pl.BlockSpec(memory_space=pltpu.SMEM)] + [specs[w] for _, w in ins],
        out_specs=tuple(specs[w] for _, _, w in outs),
        scratch_shapes=list(scratch),
        input_output_aliases=aliases or {},
        compiler_params=pltpu.CompilerParams(vmem_limit_bytes=mib * MIB),
        cost_estimate=pl.CostEstimate(flops=int(flops), bytes_accessed=int(nbytes), transcendentals=0),
        name=name,
    )(at, *args)


def at_block(i, size):
    return pl.ds(pl.multiple_of(i * size, size), size)


def dma(n):
    return pltpu.SemaphoreType.DMA((n,))


def copy(src, dst, sem):
    return pltpu.make_async_copy(src, dst, sem)


def cut_half(at, x, half):
    rows = x.shape[0]
    n = 8
    step = rows // n

    def body(at_ref, x_ref, o_ref, sems):
        def cut(i):
            here = pl.ds(i * step, step)
            return copy(x_ref.at[here, at_block(1 - at_ref[0], half)], o_ref.at[here, :], sems.at[i])

        for i in range(n):
            cut(i).start()
        for i in range(n):
            cut(i).wait()

    return call(body, "cut_half", at, [(x, "h")], [((rows, half), BF, "v")], [dma(n)])[0]


VPARTS = 4


def project_own(at, x, v, c, after=()):
    rows, (half, rank) = x.shape[0], v.shape
    tk = half // VPARTS

    def body(at_ref, x_ref, v_ref, c_ref, p_ref, xv_ref, cs_ref, *refs):
        vv, (acc, x_sem, v_sem, c_sem) = refs[:VPARTS], refs[VPARTS:]

        def cut(ref, dst, core, k, sem):
            src = ref.at[:, pl.ds(pl.multiple_of(core * half + k * tk, tk), tk)]
            return copy(src, dst.at[:, pl.ds(k * tk, tk)], sem.at[k])

        def x_copy(k):
            return cut(x_ref, xv_ref, at_ref[0], k, x_sem)

        def c_copy(k):
            return cut(c_ref, cs_ref, 1 - at_ref[0], k, c_sem)

        def v_copy(k):
            return copy(v_ref.at[pl.ds(k * tk, tk), :], vv[k], v_sem.at[k])

        for k in range(VPARTS):
            x_copy(k).start()
            v_copy(k).start()
        for k in range(VPARTS):
            c_copy(k).start()
        for k in range(VPARTS):
            x_copy(k).wait()
            v_copy(k).wait()
            part = jnp.dot(xv_ref[:, pl.ds(k * tk, tk)], vv[k][...], preferred_element_type=F32)
            if k == VPARTS - 1:
                p_ref[...] = (acc[...] + part).astype(BF)
            else:
                acc[...] = acc[...] + part if k else part
        for k in range(VPARTS):
            c_copy(k).wait()

    return call(
        body,
        "project_own",
        at,
        [(x, "h"), (v, "h"), (c, "h")],
        [((rows, rank), BF, "v"), ((rows, half), BF, "v"), ((rows, half), BF, "v")] + [((tk, rank), BF, "v")] * VPARTS,
        [pltpu.VMEM((rows, rank), F32)] + [dma(VPARTS)] * 3,
        flops=2 * rows * half * rank,
        mib=6,
        after=after,
    )


def write_halves(at_ref, total, outs):
    if len(outs) == 1:
        outs[0][...] = total(slice(None))
        return
    each = outs[0].shape[0]
    bit = at_ref[1] & 1
    for i, o_ref in ((bit, outs[0]), (1 - bit, outs[1])):
        o_ref[...] = total(at_block(i, each)).astype(BF)


def halves_of(rows, rank, direct):
    return [((rows // 2, rank), BF, "v")] * 2 if direct else [((rows, rank), F32, "v")]


def project_other(at, x_o, vs, theirs, direct):
    rows = x_o.shape[0]
    tk, rank = vs[0].shape

    def body(at_ref, x_ref, t_ref, *refs):
        vv, outs, acc = refs[:VPARTS], refs[VPARTS:-1], refs[-1]
        for k in range(VPARTS):
            part = jnp.dot(x_ref[:, pl.ds(k * tk, tk)], vv[k][...], preferred_element_type=F32)
            acc[...] = part + (acc[...] if k else t_ref[...].astype(F32))
        write_halves(at_ref, lambda here: acc[here, :], outs)

    return call(
        body,
        "project_other",
        at,
        [(x_o, "v"), (theirs, "v")] + [(a, "v") for a in vs],
        halves_of(rows, rank, direct),
        [pltpu.VMEM((rows, rank), F32)],
        flops=2 * rows * tk * VPARTS * rank,
        mib=6,
    )


def hidden(c, x):
    return (c.astype(F32) * x.astype(F32)).astype(BF)


def back_project(at, s, x, x_o, c, c_o, u, so_far, after=()):
    rows, (half, rank) = x.shape[0], u.shape
    part = half // 2
    tk = min(512, part)
    n = part // tk
    slots = min(4, n)
    first = so_far is None

    def body(at_ref, x_ref, xo_ref, c_ref, co_ref, u_ref, *rest):
        if first:
            acc, b_ref, cv_ref, uv, h, c_sem, u_sem = rest
        else:
            so_ref, own_ref, oth_ref, b_ref, cv_ref, uv, h, acc, c_sem, u_sem = rest

        def c_copy(k):
            src = c_ref.at[:, pl.ds(pl.multiple_of(at_ref[0] * half + s * part + k * tk, tk), tk)]
            return copy(src, cv_ref.at[:, at_block(k, tk)], c_sem.at[k])

        def u_copy(k):
            slot = lax.rem(k, slots)
            return copy(u_ref.at[pl.ds(pl.multiple_of(s * part + k * tk, tk), tk), :], uv.at[slot], u_sem.at[slot])

        def make(k, slot):
            here = at_block(k, tk)
            there = pl.ds(pl.multiple_of(s * part + k * tk, tk), tk)
            own = hidden(cv_ref[:, here], x_ref[:, there])
            oth = hidden(co_ref[:, there], xo_ref[:, there])
            h[slot, :rows, :] = own
            h[slot, rows:, :] = oth
            b_ref[:, here] = jnp.sum(own.astype(F32), axis=0, keepdims=True) + jnp.sum(oth.astype(F32), axis=0, keepdims=True)

        def add(slot, k):
            acc[...] += jnp.dot(h[slot], uv[lax.rem(k, slots)], preferred_element_type=F32)

        for k in range(n):
            c_copy(k).start()
            if k < slots:
                u_copy(k).start()
        acc[...] = jnp.zeros_like(acc) if first else so_ref[...]
        c_copy(0).wait()
        make(0, 0)

        @pl.loop(0, n - 1)
        def _(k):
            c_copy(k + 1).wait()
            u_copy(k).wait()
            make(k + 1, lax.rem(k + 1, 2))
            add(lax.rem(k, 2), k)

            @pl.when(k + slots < n)
            def _():
                u_copy(k + slots).start()

        u_copy(n - 1).wait()
        add((n - 1) % 2, n - 1)
        if not first:
            own_ref[...] = acc[:rows, :].astype(BF)
            oth_ref[...] = acc[rows:, :]

    ends = [((1, part), F32, "v"), ((rows, part), BF, "v")]
    whole = pltpu.VMEM((2 * rows, rank), F32)
    return call(
        body,
        "back_project",
        at,
        [(x, "v"), (x_o, "v"), (c, "h"), (c_o, "v"), (u, "h")] + ([] if first else [(so_far, "v")]),
        ([((2 * rows, rank), F32, "v")] if first else [((rows, rank), BF, "v"), ((rows, rank), F32, "v")]) + ends,
        [pltpu.VMEM((slots, tk, rank), BF), pltpu.VMEM((2, 2 * rows, tk), BF)]
        + ([] if first else [whole])
        + [dma(n), dma(slots)],
        flops=2 * rows * half * rank,
        mib=12,
        after=after,
    )


def turn_x(at, x, x_o, after=()):
    rows, half = x.shape
    tw = min(512, half)

    def body(at_ref, x_ref, xo_ref, o_ref):
        @pl.loop(0, half // tw)
        def _(k):
            here = at_block(k, tw)
            o_ref[here, :rows] = x_ref[:, here].T
            o_ref[here, rows:] = xo_ref[:, here].T

    return call(body, "turn_x", at, [(x, "v"), (x_o, "v")], [((half, 2 * rows), BF, "v")], mib=6, after=after)[0]


def turn_hidden(at, x, x_o, cs, c_o, after=()):
    rows, half = x.shape
    part = half // 2
    tw = min(512, part)

    def body(at_ref, x_ref, xo_ref, c0_ref, c1_ref, co_ref, o_ref):
        for s, c_ref in enumerate((c0_ref, c1_ref)):

            @pl.loop(0, part // tw)
            def _(k):
                here = at_block(k, tw)
                there = pl.ds(pl.multiple_of(s * part + k * tw, tw), tw)
                o_ref[there, :rows] = hidden(c_ref[:, here], x_ref[:, there]).T
                o_ref[there, rows:] = hidden(co_ref[:, there], xo_ref[:, there]).T

    return call(
        body,
        "turn_hidden",
        at,
        [(a, "v") for a in (x, x_o, *cs, c_o)],
        [((half, 2 * rows), BF, "v")],
        mib=6,
        after=after,
    )[0]


def fill(at_ref, both, refs):
    if len(refs) == 2:
        rows = refs[0].shape[0]
        both[:rows, :] = refs[0][...]
        both[rows:, :] = refs[1][...]
        return
    each = refs[0].shape[0]
    bit = at_ref[1] & 1
    for i, (keep, other) in enumerate((refs[:2], refs[2:])):
        both[at_block(2 * i + bit, each), :] = keep[...]
        both[at_block(2 * i + 1 - bit, each), :] = other[...]


def factor_grad(at, name, s, turned, p, so_far, placed=None, after=()):
    half, rows2 = turned.shape
    rank = p[0].shape[1]
    part = half // 2
    tw = min(1024, part)
    n = part // tw
    np_ = len(p)
    recv, full = placed or ((), None)
    nr = len(recv)
    ins = [(turned, "v")] + [(a, "v") for a in p]
    aliases = {}
    if so_far is not None:
        aliases[1 + len(ins)] = 0
        ins.append((so_far, "h"))
    if placed:
        ins += [(a, "v") for a in recv]
        aliases[1 + len(ins)] = 1
        ins.append((full, "h"))

    def body(at_ref, t_ref, *refs):
        p_refs, refs = refs[:np_], refs[np_ + (so_far is not None) :]
        r_refs, refs = refs[:nr], refs[nr + (nr > 0) :]
        o_ref, refs = refs[0], refs[1:]
        if nr:
            f_ref, refs = refs[0], refs[1:]
        stage, both, sems, put_sem = refs

        def put(i):
            w = recv[i].shape[1]
            there = pl.ds(pl.multiple_of((1 - at_ref[0]) * half + i * w, w), w)
            return copy(r_refs[i], f_ref.at[:, there], put_sem.at[i])

        def out(k, slot):
            there = pl.ds(pl.multiple_of(s * part + k * tw, tw), tw)
            return copy(stage.at[slot], o_ref.at[there, :], sems.at[slot])

        for i in range(nr):
            put(i).start()
        fill(at_ref, both, p_refs)

        @pl.loop(0, n)
        def _(k):
            slot = lax.rem(k, 2)

            @pl.when(k >= 2)
            def _():
                out(k, slot).wait()

            left = t_ref[pl.ds(pl.multiple_of(s * part + k * tw, tw), tw), :]
            stage[slot] = jnp.dot(left, both[...], preferred_element_type=F32).astype(BF)
            out(k, slot).start()

        for k in range(max(0, n - 2), n):
            out(k, k % 2).wait()
        for i in range(nr):
            put(i).wait()

    outs = [((half, rank), BF, "h")] + ([(full.shape, BF, "h")] if placed else [])
    return call(
        body,
        name,
        at,
        ins,
        outs,
        [pltpu.VMEM((2, tw, rank), BF), pltpu.VMEM((rows2, rank), BF), dma(2), dma(max(1, nr))],
        flops=rows2 * half * rank,
        aliases=aliases,
        mib=12,
        after=after,
    )


def expand(at, s, u, p, after=()):
    half, rank = u.shape
    rows2 = sum(a.shape[0] for a in p)
    part = half // 2
    tw = min(1024, part)
    n = part // tw
    slots = min(3, n)

    def body(at_ref, u_ref, *refs):
        o_ref, uv, both, u_sem = refs[len(p) :]

        def u_copy(k):
            slot = lax.rem(k, slots)
            return copy(u_ref.at[pl.ds(pl.multiple_of(s * part + k * tw, tw), tw), :], uv.at[slot], u_sem.at[slot])

        for k in range(slots):
            u_copy(k).start()
        fill(at_ref, both, refs[: len(p)])

        @pl.loop(0, n)
        def _(k):
            u_copy(k).wait()
            o_ref[:, at_block(k, tw)] = lax.dot_general(both[...], uv[lax.rem(k, slots)], NT, preferred_element_type=F32)

            @pl.when(k + slots < n)
            def _():
                u_copy(k + slots).start()

    return call(
        body,
        "expand",
        at,
        [(u, "h")] + [(a, "v") for a in p],
        [((rows2, part), F32, "v")],
        [pltpu.VMEM((slots, tw, rank), BF), pltpu.VMEM((rows2, rank), BF), dma(slots)],
        flops=rows2 * half * rank,
        mib=10,
        after=after,
    )[0]


def input_grad(at, s, c, c_o, ex, v, bias, g, so_far, width, after=()):
    rows, half = c_o.shape
    rank = v.shape[1]
    part = half // 2
    tw = min(512, part)
    n = part // tw
    slots = min(4, n)
    ng = len(g)

    def body(at_ref, c_ref, co_ref, ex_ref, v_ref, b_ref, *refs):
        g_refs, refs = refs[:ng], refs[ng + (so_far is not None) :]
        own_ref, oth_ref, stage, vv, bk, both, sems, v_sem = refs

        def v_copy(k):
            slot = lax.rem(k, slots)
            return copy(v_ref.at[pl.ds(pl.multiple_of(s * part + k * tw, tw), tw), :], vv.at[slot], v_sem.at[slot])

        def columns(k):
            return pl.ds(pl.multiple_of(at_ref[0] * half + s * part + k * tw, tw), tw)

        def out(k, slot):
            return copy(stage.at[slot], own_ref.at[:, columns(k)], sems.at[slot])

        def finish(k, slot):
            here = at_block(k, tw)
            there = pl.ds(pl.multiple_of(s * part + k * tw, tw), tw)
            b = b_ref[:, columns(k)].astype(F32)
            cf, cof = c_ref[:, here].astype(F32), co_ref[:, there].astype(F32)
            stage[slot] = (cf * (ex_ref[:rows, here] + b) + cf + bk[slot, :rows, :]).astype(BF)
            oth_ref[:, here] = (cof * (ex_ref[rows:, here] + b) + cof + bk[slot, rows:, :]).astype(BF)

        def product(k, slot):
            bk[slot] = lax.dot_general(both[...], vv[lax.rem(k, slots)], NT, preferred_element_type=F32)

        for k in range(slots):
            v_copy(k).start()
        fill(at_ref, both, g_refs)
        v_copy(0).wait()
        product(0, 0)

        @pl.loop(1, n)
        def _(k):
            now, last = lax.rem(k, 2), lax.rem(k + 1, 2)
            v_copy(k).wait()

            @pl.when(k >= 3)
            def _():
                out(k - 1, last).wait()

            finish(k - 1, last)
            product(k, now)
            out(k - 1, last).start()

            @pl.when(k - 1 + slots < n)
            def _():
                v_copy(k - 1 + slots).start()

        if n >= 3:
            out(n - 1, (n - 1) % 2).wait()
        finish(n - 1, (n - 1) % 2)
        out(n - 1, (n - 1) % 2).start()
        for k in range(max(0, n - 2), n):
            out(k, k % 2).wait()

    ins = [(c, "v"), (c_o, "v"), (ex, "v"), (v, "h"), (bias, "v")] + [(a, "v") for a in g]
    aliases = {}
    if so_far is not None:
        aliases = {1 + len(ins): 0}
        ins.append((so_far, "h"))
    return call(
        body,
        "input_grad",
        at,
        ins,
        [((rows, width), BF, "h"), ((rows, part), BF, "v")],
        [
            pltpu.VMEM((2, rows, tw), BF),
            pltpu.VMEM((slots, tw, rank), BF),
            pltpu.VMEM((2, 2 * rows, tw), F32),
            pltpu.VMEM((2 * rows, rank), BF),
            dma(2),
            dma(slots),
        ],
        flops=2 * rows * half * rank,
        aliases=aliases,
        mib=12,
        after=after,
    )


def plus(a, b):
    return a.astype(F32) + b.astype(F32)


def pair_halves(at, a, b, direct, after=()):
    rows, rank = a.shape

    def body(at_ref, a_ref, b_ref, *outs):
        write_halves(at_ref, lambda here: plus(a_ref[here, :], b_ref[here, :]), outs)

    return call(body, "pair_halves", at, [(a, "v"), (b, "v")], halves_of(rows, rank, direct), after=after)


def pieces_of(at, a, b, m, after=()):
    rows, rank = a.shape
    each = rows // m

    def body(at_ref, a_ref, b_ref, *outs):
        for d in range(m):
            here = at_block((at_ref[1] >> 1) ^ d, each)
            outs[d][...] = plus(a_ref[here, :], b_ref[here, :]).astype(BF)

    return call(body, "pieces_of", at, [(a, "v"), (b, "v")], [((each, rank), BF, "v")] * m, after=after)


def add_pieces(at, parts, after=()):
    def body(at_ref, *refs):
        total = refs[0][...].astype(F32)
        for r in refs[1:-1]:
            total += r[...].astype(F32)
        refs[-1][...] = total.astype(BF)

    return call(body, "add_pieces", at, [(a, "v") for a in parts], [(parts[0].shape, BF, "v")], after=after)[0]


def join_pieces(at, parts, after=()):
    m = len(parts)
    each, rank = parts[0].shape

    def body(at_ref, *refs):
        for d in range(m):
            refs[-1][at_block((at_ref[1] >> 1) ^ d, each), :] = refs[d][...]

    return call(body, "join_pieces", at, [(a, "v") for a in parts], [((m * each, rank), BF, "v")], after=after)[0]


def solution(mesh):
    n = mesh.shape["col"]
    m = n // 2
    swap = [(0, 1), (1, 0)]

    def trade(a):
        return lax.ppermute(a, "batch", swap)

    def to(a, d):
        return lax.ppermute(a, "col", [(i, i ^ d) for i in range(n)])

    def spread(parts):
        return [parts[0]] + [to(parts[d], 2 * d) for d in range(1, m)]

    def ends(half):
        other = to(half, 1)
        return [trade(half), trade(other), half, other]

    def local(x, c, u, v, bias):
        half, width = u.shape[0], x.shape[1]
        core = lax.axis_index("batch")
        at = jnp.stack([core, lax.axis_index("col")]).astype(jnp.int32)
        direct = x.shape[0] % (16 * n) == 0 and n & (n - 1) == 0 and n > 2

        def plain(total):
            total = lax.psum(total, "col").astype(BF)
            return [trade(total), total]

        x_s = cut_half(at, x, half)
        x_o = trade(x_s)
        own, x_own, c_s, *v_in = project_own(at, x, v, c, [x_s])
        theirs = trade(own)
        c_o = trade(c_s)
        sums = project_other(at, x_o, v_in, theirs, direct)
        acc, b0, c0 = back_project(at, 0, x_own, x_o, c, c_o, u, None, [sums[0]])
        if direct:
            parts = pieces_of(at, sums[0], to(sums[1], 1), m, [acc])
            own_g, mine_g, b1, c1 = back_project(at, 1, x_own, x_o, c, c_o, u, acc, [parts[0]])
            parts = spread(parts)
            theirs_g = trade(own_g)
            total = add_pieces(at, parts, [own_g])
            sums_g = pair_halves(at, mine_g, theirs_g, direct, [total])
            x_t = turn_x(at, x_own, x_o, [sums_g[0]])
            p = ends(join_pieces(at, spread([total] * m), [x_t]))
            parts_g = pieces_of(at, sums_g[0], to(sums_g[1], 1), m, [p[2]])
            h_t = turn_hidden(at, x_own, x_o, (c0, c1), c_o, [parts_g[0]])
            total_g = add_pieces(at, spread(parts_g), [h_t])
            (grad_u,) = factor_grad(at, "u_grad", 0, h_t, p, None, after=[total_g])
            (grad_u,) = factor_grad(at, "u_grad", 1, h_t, p, grad_u)
            half_g = join_pieces(at, spread([total_g] * m), [(grad_u, "h")])
            g = ends(half_g)
            ex0 = expand(at, 0, u, p, [half_g])
            ex1 = expand(at, 1, u, p, [ex0])
        else:
            own_g, mine_g, b1, c1 = back_project(at, 1, x_own, x_o, c, c_o, u, acc)
            (sums_g,) = pair_halves(at, mine_g, trade(own_g), direct)
            p, g = plain(sums[0]), plain(sums_g)
            x_t = turn_x(at, x_own, x_o)
            h_t = turn_hidden(at, x_own, x_o, (c0, c1), c_o)
            (grad_u,) = factor_grad(at, "u_grad", 0, h_t, p, None)
            (grad_u,) = factor_grad(at, "u_grad", 1, h_t, p, grad_u)
            ex0, ex1 = expand(at, 0, u, p), expand(at, 1, u, p)
        bias = bias[None, :]
        out, oth0 = input_grad(at, 0, c0, c_o, ex0, v, bias, g, None, width, [ex1])
        out, oth1 = input_grad(at, 1, c1, c_o, ex1, v, bias, g, out, width)
        back = [trade(oth0), trade(oth1)]
        (grad_v,) = factor_grad(at, "v_grad", 0, x_t, g, None, after=[oth1])
        grad_v, out = factor_grad(at, "v_grad", 1, x_t, g, grad_v, (back, out))
        return out, grad_u, grad_v, jnp.concatenate([b0[0], b1[0]])

    return jax.shard_map(
        local,
        mesh=mesh,
        in_specs=(
            P(("group", "batch"), "col"),
            P(("group", "batch"), "col"),
            P(("col", "batch"), None),
            P(("col", "batch"), None),
            P("col"),
        ),
        out_specs=(
            P(("group", "batch"), "col"),
            P(("group", "col", "batch"), None),
            P(("group", "col", "batch"), None),
            P(("group", "col", "batch")),
        ),
        check_vma=False,
    )
```

```python
import jax
import jax.numpy as jnp
from jax import lax
from jax.experimental import pallas as pl
from jax.experimental.pallas import tpu as pltpu
from jax.sharding import PartitionSpec as P

BF, F32 = jnp.bfloat16, jnp.float32
MIB = 1 << 20
NT = (((1,), (1,)), ((), ()))


def call(body, name, at, ins, outs, scratch=(), flops=0, aliases=None, mib=4, after=()):
    specs = {"v": pl.BlockSpec(memory_space=pltpu.VMEM), "h": pl.BlockSpec(memory_space=pl.ANY)}
    spaces = {"v": pltpu.VMEM, "h": pltpu.HBM}
    nbytes = sum(a.size * a.dtype.itemsize for a, _ in ins)
    skip = 1 + len(ins)
    ins = list(ins) + [a if isinstance(a, tuple) else (a, "v") for a in after]
    args = [pltpu.with_memory_space_constraint(a, spaces[w]) for a, w in ins]
    return pl.pallas_call(
        lambda *refs: body(*refs[:skip], *refs[skip + len(after) :]),
        out_shape=tuple(spaces[w](dims, dtype) for dims, dtype, w in outs),
        in_specs=[pl.BlockSpec(memory_space=pltpu.SMEM)] + [specs[w] for _, w in ins],
        out_specs=tuple(specs[w] for _, _, w in outs),
        scratch_shapes=list(scratch),
        input_output_aliases=aliases or {},
        compiler_params=pltpu.CompilerParams(vmem_limit_bytes=mib * MIB),
        cost_estimate=pl.CostEstimate(flops=int(flops), bytes_accessed=int(nbytes), transcendentals=0),
        name=name,
    )(at, *args)


def at_block(i, size):
    return pl.ds(pl.multiple_of(i * size, size), size)


def dma(n):
    return pltpu.SemaphoreType.DMA((n,))


def copy(src, dst, sem):
    return pltpu.make_async_copy(src, dst, sem)


def cut_half(at, x, half):
    rows = x.shape[0]
    n = 8
    step = rows // n

    def body(at_ref, x_ref, o_ref, sems):
        def cut(i):
            here = pl.ds(i * step, step)
            return copy(x_ref.at[here, at_block(1 - at_ref[0], half)], o_ref.at[here, :], sems.at[i])

        for i in range(n):
            cut(i).start()
        for i in range(n):
            cut(i).wait()

    return call(body, "cut_half", at, [(x, "h")], [((rows, half), BF, "v")], [dma(n)])[0]


VPARTS = 4


def project_own(at, x, v, c, after=()):
    rows, (half, rank) = x.shape[0], v.shape
    tk = half // VPARTS

    def body(at_ref, x_ref, v_ref, c_ref, p_ref, xv_ref, cs_ref, *refs):
        vv, (acc, x_sem, v_sem, c_sem) = refs[:VPARTS], refs[VPARTS:]

        def cut(ref, dst, core, k, sem):
            src = ref.at[:, pl.ds(pl.multiple_of(core * half + k * tk, tk), tk)]
            return copy(src, dst.at[:, pl.ds(k * tk, tk)], sem.at[k])

        def x_copy(k):
            return cut(x_ref, xv_ref, at_ref[0], k, x_sem)

        def c_copy(k):
            return cut(c_ref, cs_ref, 1 - at_ref[0], k, c_sem)

        def v_copy(k):
            return copy(v_ref.at[pl.ds(k * tk, tk), :], vv[k], v_sem.at[k])

        for k in range(VPARTS):
            x_copy(k).start()
            v_copy(k).start()
        for k in range(VPARTS):
            c_copy(k).start()
        for k in range(VPARTS):
            x_copy(k).wait()
            v_copy(k).wait()
            part = jnp.dot(xv_ref[:, pl.ds(k * tk, tk)], vv[k][...], preferred_element_type=F32)
            if k == VPARTS - 1:
                p_ref[...] = (acc[...] + part).astype(BF)
            else:
                acc[...] = acc[...] + part if k else part
        for k in range(VPARTS):
            c_copy(k).wait()

    return call(
        body,
        "project_own",
        at,
        [(x, "h"), (v, "h"), (c, "h")],
        [((rows, rank), BF, "v"), ((rows, half), BF, "v"), ((rows, half), BF, "v")] + [((tk, rank), BF, "v")] * VPARTS,
        [pltpu.VMEM((rows, rank), F32)] + [dma(VPARTS)] * 3,
        flops=2 * rows * half * rank,
        mib=6,
        after=after,
    )


def write_halves(at_ref, total, outs):
    if len(outs) == 1:
        outs[0][...] = total(slice(None))
        return
    each = outs[0].shape[0]
    bit = at_ref[1] & 1
    for i, o_ref in ((bit, outs[0]), (1 - bit, outs[1])):
        o_ref[...] = total(at_block(i, each)).astype(BF)


def halves_of(rows, rank, direct):
    return [((rows // 2, rank), BF, "v")] * 2 if direct else [((rows, rank), F32, "v")]


def project_other(at, x_o, vs, theirs, direct):
    rows = x_o.shape[0]
    tk, rank = vs[0].shape

    def body(at_ref, x_ref, t_ref, *refs):
        vv, outs, acc = refs[:VPARTS], refs[VPARTS:-1], refs[-1]
        for k in range(VPARTS):
            part = jnp.dot(x_ref[:, pl.ds(k * tk, tk)], vv[k][...], preferred_element_type=F32)
            acc[...] = part + (acc[...] if k else t_ref[...].astype(F32))
        write_halves(at_ref, lambda here: acc[here, :], outs)

    return call(
        body,
        "project_other",
        at,
        [(x_o, "v"), (theirs, "v")] + [(a, "v") for a in vs],
        halves_of(rows, rank, direct),
        [pltpu.VMEM((rows, rank), F32)],
        flops=2 * rows * tk * VPARTS * rank,
        mib=6,
    )


def hidden(c, x):
    return (c.astype(F32) * x.astype(F32)).astype(BF)


def back_project(at, s, x, x_o, c, c_o, u, so_far, after=(), tk=1024):
    rows, (half, rank) = x.shape[0], u.shape
    part = half // 2
    tk = min(tk, part)
    n = part // tk
    slots = min(2, n)
    first = so_far is None

    def body(at_ref, x_ref, xo_ref, c_ref, co_ref, u_ref, *rest):
        if first:
            acc, b_ref, cv_ref, uv, h, c_sem, u_sem = rest
        else:
            so_ref, own_ref, oth_ref, b_ref, cv_ref, uv, h, acc, c_sem, u_sem = rest

        def c_copy(k):
            src = c_ref.at[:, pl.ds(pl.multiple_of(at_ref[0] * half + s * part + k * tk, tk), tk)]
            return copy(src, cv_ref.at[:, at_block(k, tk)], c_sem.at[k])

        def u_copy(k):
            slot = lax.rem(k, slots)
            return copy(u_ref.at[pl.ds(pl.multiple_of(s * part + k * tk, tk), tk), :], uv.at[slot], u_sem.at[slot])

        def make(k, slot):
            here = at_block(k, tk)
            there = pl.ds(pl.multiple_of(s * part + k * tk, tk), tk)
            own = hidden(cv_ref[:, here], x_ref[:, there])
            oth = hidden(co_ref[:, there], xo_ref[:, there])
            h[slot, :rows, :] = own
            h[slot, rows:, :] = oth
            b_ref[:, here] = jnp.sum(own.astype(F32), axis=0, keepdims=True) + jnp.sum(oth.astype(F32), axis=0, keepdims=True)

        def add(slot, k):
            acc[...] += jnp.dot(h[slot], uv[lax.rem(k, slots)], preferred_element_type=F32)

        for k in range(n):
            c_copy(k).start()
            if k < slots:
                u_copy(k).start()
        acc[...] = jnp.zeros_like(acc) if first else so_ref[...]
        c_copy(0).wait()
        make(0, 0)

        @pl.loop(0, n - 1)
        def _(k):
            c_copy(k + 1).wait()
            u_copy(k).wait()
            make(k + 1, lax.rem(k + 1, 2))
            add(lax.rem(k, 2), k)

            @pl.when(k + slots < n)
            def _():
                u_copy(k + slots).start()

        u_copy(n - 1).wait()
        add((n - 1) % 2, n - 1)
        if not first:
            own_ref[...] = acc[:rows, :].astype(BF)
            oth_ref[...] = acc[rows:, :]

    ends = [((1, part), F32, "v"), ((rows, part), BF, "v")]
    whole = pltpu.VMEM((2 * rows, rank), F32)
    return call(
        body,
        "back_project",
        at,
        [(x, "v"), (x_o, "v"), (c, "h"), (c_o, "v"), (u, "h")] + ([] if first else [(so_far, "v")]),
        ([((2 * rows, rank), F32, "v")] if first else [((rows, rank), BF, "v"), ((rows, rank), F32, "v")]) + ends,
        [pltpu.VMEM((slots, tk, rank), BF), pltpu.VMEM((2, 2 * rows, tk), BF)]
        + ([] if first else [whole])
        + [dma(n), dma(slots)],
        flops=2 * rows * half * rank,
        mib=16,
        after=after,
    )


def turn_x(at, x, x_o, after=()):
    rows, half = x.shape
    tw = min(512, half)

    def body(at_ref, x_ref, xo_ref, o_ref):
        @pl.loop(0, half // tw)
        def _(k):
            here = at_block(k, tw)
            o_ref[here, :rows] = x_ref[:, here].T
            o_ref[here, rows:] = xo_ref[:, here].T

    return call(body, "turn_x", at, [(x, "v"), (x_o, "v")], [((half, 2 * rows), BF, "v")], mib=6, after=after)[0]


def turn_hidden(at, x, x_o, cs, c_o, after=()):
    rows, half = x.shape
    part = half // 2
    tw = min(512, part)

    def body(at_ref, x_ref, xo_ref, c0_ref, c1_ref, co_ref, o_ref):
        for s, c_ref in enumerate((c0_ref, c1_ref)):

            @pl.loop(0, part // tw)
            def _(k):
                here = at_block(k, tw)
                there = pl.ds(pl.multiple_of(s * part + k * tw, tw), tw)
                o_ref[there, :rows] = hidden(c_ref[:, here], x_ref[:, there]).T
                o_ref[there, rows:] = hidden(co_ref[:, there], xo_ref[:, there]).T

    return call(
        body,
        "turn_hidden",
        at,
        [(a, "v") for a in (x, x_o, *cs, c_o)],
        [((half, 2 * rows), BF, "v")],
        mib=6,
        after=after,
    )[0]


def fill(at_ref, both, refs):
    if len(refs) == 2:
        rows = refs[0].shape[0]
        both[:rows, :] = refs[0][...]
        both[rows:, :] = refs[1][...]
        return
    each = refs[0].shape[0]
    bit = at_ref[1] & 1
    for i, (keep, other) in enumerate((refs[:2], refs[2:])):
        both[at_block(2 * i + bit, each), :] = keep[...]
        both[at_block(2 * i + 1 - bit, each), :] = other[...]


def factor_grad(at, name, s, turned, p, so_far, placed=None, after=(), tw=1024):
    half, rows2 = turned.shape
    rank = p[0].shape[1]
    part = half // 2
    tw = min(tw, part)
    n = part // tw
    np_ = len(p)
    recv, full = placed or ((), None)
    nr = len(recv)
    ins = [(turned, "v")] + [(a, "v") for a in p]
    aliases = {}
    if so_far is not None:
        aliases[1 + len(ins)] = 0
        ins.append((so_far, "h"))
    if placed:
        ins += [(a, "v") for a in recv]
        aliases[1 + len(ins)] = 1
        ins.append((full, "h"))

    def body(at_ref, t_ref, *refs):
        p_refs, refs = refs[:np_], refs[np_ + (so_far is not None) :]
        r_refs, refs = refs[:nr], refs[nr + (nr > 0) :]
        o_ref, refs = refs[0], refs[1:]
        if nr:
            f_ref, refs = refs[0], refs[1:]
        stage, both, sems, put_sem = refs

        def put(i):
            w = recv[i].shape[1]
            there = pl.ds(pl.multiple_of((1 - at_ref[0]) * half + i * w, w), w)
            return copy(r_refs[i], f_ref.at[:, there], put_sem.at[i])

        def out(k, slot):
            there = pl.ds(pl.multiple_of(s * part + k * tw, tw), tw)
            return copy(stage.at[slot], o_ref.at[there, :], sems.at[slot])

        for i in range(nr):
            put(i).start()
        fill(at_ref, both, p_refs)

        @pl.loop(0, n)
        def _(k):
            slot = lax.rem(k, 2)

            @pl.when(k >= 2)
            def _():
                out(k, slot).wait()

            left = t_ref[pl.ds(pl.multiple_of(s * part + k * tw, tw), tw), :]
            stage[slot] = jnp.dot(left, both[...], preferred_element_type=F32).astype(BF)
            out(k, slot).start()

        for k in range(max(0, n - 2), n):
            out(k, k % 2).wait()
        for i in range(nr):
            put(i).wait()

    outs = [((half, rank), BF, "h")] + ([(full.shape, BF, "h")] if placed else [])
    return call(
        body,
        name,
        at,
        ins,
        outs,
        [pltpu.VMEM((2, tw, rank), BF), pltpu.VMEM((rows2, rank), BF), dma(2), dma(max(1, nr))],
        flops=rows2 * half * rank,
        aliases=aliases,
        mib=16,
        after=after,
    )


def expand(at, s, u, p, after=(), tw=1024):
    half, rank = u.shape
    rows2 = sum(a.shape[0] for a in p)
    part = half // 2
    tw = min(tw, part)
    n = part // tw
    slots = min(3, n)

    def body(at_ref, u_ref, *refs):
        o_ref, uv, both, u_sem = refs[len(p) :]

        def u_copy(k):
            slot = lax.rem(k, slots)
            return copy(u_ref.at[pl.ds(pl.multiple_of(s * part + k * tw, tw), tw), :], uv.at[slot], u_sem.at[slot])

        for k in range(slots):
            u_copy(k).start()
        fill(at_ref, both, refs[: len(p)])

        @pl.loop(0, n)
        def _(k):
            u_copy(k).wait()
            o_ref[:, at_block(k, tw)] = lax.dot_general(both[...], uv[lax.rem(k, slots)], NT, preferred_element_type=F32)

            @pl.when(k + slots < n)
            def _():
                u_copy(k + slots).start()

    return call(
        body,
        "expand",
        at,
        [(u, "h")] + [(a, "v") for a in p],
        [((rows2, part), F32, "v")],
        [pltpu.VMEM((slots, tw, rank), BF), pltpu.VMEM((rows2, rank), BF), dma(slots)],
        flops=rows2 * half * rank,
        mib=10,
        after=after,
    )[0]


def input_grad(at, s, c, c_o, ex, v, bias, g, so_far, width, after=(), tw=1024):
    rows, half = c_o.shape
    rank = v.shape[1]
    part = half // 2
    tw = min(tw, part)
    n = part // tw
    slots = min(2, n)
    ng = len(g)

    def body(at_ref, c_ref, co_ref, ex_ref, v_ref, b_ref, *refs):
        g_refs, refs = refs[:ng], refs[ng + (so_far is not None) :]
        own_ref, oth_ref, stage, vv, both, sems, v_sem = refs

        def v_copy(k):
            slot = lax.rem(k, slots)
            return copy(v_ref.at[pl.ds(pl.multiple_of(s * part + k * tw, tw), tw), :], vv.at[slot], v_sem.at[slot])

        def columns(k):
            return pl.ds(pl.multiple_of(at_ref[0] * half + s * part + k * tw, tw), tw)

        def out(k, slot):
            return copy(stage.at[slot], own_ref.at[:, columns(k)], sems.at[slot])

        for k in range(slots):
            v_copy(k).start()
        fill(at_ref, both, g_refs)

        @pl.loop(0, n)
        def _(k):
            slot = lax.rem(k, 2)
            here = at_block(k, tw)
            there = pl.ds(pl.multiple_of(s * part + k * tw, tw), tw)
            v_copy(k).wait()

            @pl.when(k >= 2)
            def _():
                out(k, slot).wait()

            bk = lax.dot_general(both[...], vv[lax.rem(k, slots)], NT, preferred_element_type=F32)
            b = b_ref[:, columns(k)].astype(F32)
            cf, cof = c_ref[:, here].astype(F32), co_ref[:, there].astype(F32)
            stage[slot] = (cf * (ex_ref[:rows, here] + b) + cf + bk[:rows]).astype(BF)
            oth_ref[:, here] = (cof * (ex_ref[rows:, here] + b) + cof + bk[rows:]).astype(BF)
            out(k, slot).start()

            @pl.when(k + slots < n)
            def _():
                v_copy(k + slots).start()

        for k in range(max(0, n - 2), n):
            out(k, k % 2).wait()

    ins = [(c, "v"), (c_o, "v"), (ex, "v"), (v, "h"), (bias, "v")] + [(a, "v") for a in g]
    aliases = {}
    if so_far is not None:
        aliases = {1 + len(ins): 0}
        ins.append((so_far, "h"))
    return call(
        body,
        "input_grad",
        at,
        ins,
        [((rows, width), BF, "h"), ((rows, part), BF, "v")],
        [
            pltpu.VMEM((2, rows, tw), BF),
            pltpu.VMEM((slots, tw, rank), BF),
            pltpu.VMEM((2 * rows, rank), BF),
            dma(2),
            dma(slots),
        ],
        flops=2 * rows * half * rank,
        aliases=aliases,
        mib=16,
        after=after,
    )


def plus(a, b):
    return a.astype(F32) + b.astype(F32)


def pair_halves(at, a, b, direct, after=()):
    rows, rank = a.shape

    def body(at_ref, a_ref, b_ref, *outs):
        write_halves(at_ref, lambda here: plus(a_ref[here, :], b_ref[here, :]), outs)

    return call(body, "pair_halves", at, [(a, "v"), (b, "v")], halves_of(rows, rank, direct), after=after)


def pieces_of(at, a, b, m, after=()):
    rows, rank = a.shape
    each = rows // m

    def body(at_ref, a_ref, b_ref, o_ref):
        for j in range(m):
            here = slice(j * each, (j + 1) * each)
            o_ref[j] = plus(a_ref[here, :], b_ref[here, :]).astype(BF)

    return call(body, "pieces_of", at, [(a, "v"), (b, "v")], [((m, each, rank), BF, "v")], after=after)[0]


def add_pieces(at, parts, after=()):
    m = parts.shape[0]

    def body(at_ref, a_ref, o_ref):
        total = a_ref[0].astype(F32)
        for j in range(1, m):
            total += a_ref[j].astype(F32)
        total = total.astype(BF)
        for j in range(m):
            o_ref[j] = total

    return call(body, "add_pieces", at, [(parts, "v")], [(parts.shape, BF, "v")], after=after)[0]


def hold(at, a, after):
    def body(at_ref, a_ref, o_ref):
        pass

    return call(body, "hold", at, [(a, "v")], [(a.shape, a.dtype, "v")], aliases={1: 0}, after=after)[0]


def solution(mesh):
    n = mesh.shape["col"]
    m = n // 2
    swap = [(0, 1), (1, 0)]

    def trade(a):
        return lax.ppermute(a, "batch", swap)

    def to(a, d):
        return lax.ppermute(a, "col", [(i, i ^ d) for i in range(n)])

    def spread(parts):
        groups = [[bit + 2 * j for j in range(m)] for bit in range(2)]
        return lax.all_to_all(parts, "col", split_axis=0, concat_axis=0, axis_index_groups=groups, tiled=True)

    def whole(parts):
        return parts.reshape(-1, parts.shape[-1])

    def ends(half):
        other = to(half, 1)
        return [trade(half), trade(other), half, other]

    def local(x, c, u, v, bias):
        half, width = u.shape[0], x.shape[1]
        core = lax.axis_index("batch")
        at = jnp.stack([core, lax.axis_index("col")]).astype(jnp.int32)
        direct = x.shape[0] % (16 * n) == 0 and n & (n - 1) == 0 and n > 2

        def plain(total):
            total = lax.psum(total, "col").astype(BF)
            return [trade(total), total]

        x_s = cut_half(at, x, half)
        x_o = trade(x_s)
        own, x_own, c_s, *v_in = project_own(at, x, v, c, [x_s])
        theirs = trade(own)
        c_o = trade(hold(at, c_s, [theirs]))
        sums = project_other(at, x_o, v_in, theirs, direct)
        acc, b0, c0 = back_project(at, 0, x_own, x_o, c, c_o, u, None, [sums[0]])
        if direct:
            parts = pieces_of(at, sums[0], to(sums[1], 1), m, [acc])
            own_g, mine_g, b1, c1 = back_project(at, 1, x_own, x_o, c, c_o, u, acc, [parts])
            theirs_g = trade(own_g)
            total = add_pieces(at, spread(parts), [own_g])
            x_t = turn_x(at, x_own, x_o, [total])
            sums_g = pair_halves(at, mine_g, theirs_g, direct, [x_t])
            half_p = hold(at, whole(spread(total)), [sums_g[0]])
            p = ends(half_p)
            h_t = turn_hidden(at, x_own, x_o, (c0, c1), c_o, [half_p])
            parts_g = pieces_of(at, sums_g[0], to(sums_g[1], 1), m, [h_t])
            (grad_u,) = factor_grad(at, "u_grad", 0, h_t, p, None, after=[parts_g], tw=512)
            total_g = add_pieces(at, spread(parts_g), [(grad_u, "h")])
            (grad_u,) = factor_grad(at, "u_grad", 1, h_t, p, grad_u, after=[total_g])
            half_g = hold(at, whole(spread(total_g)), [(grad_u, "h")])
            g = ends(half_g)
            ex0 = expand(at, 0, u, p, [half_g])
            ex1 = expand(at, 1, u, p, [ex0], tw=512)
        else:
            own_g, mine_g, b1, c1 = back_project(at, 1, x_own, x_o, c, c_o, u, acc)
            (sums_g,) = pair_halves(at, mine_g, trade(own_g), direct)
            p, g = plain(sums[0]), plain(sums_g)
            x_t = turn_x(at, x_own, x_o)
            h_t = turn_hidden(at, x_own, x_o, (c0, c1), c_o)
            (grad_u,) = factor_grad(at, "u_grad", 0, h_t, p, None)
            (grad_u,) = factor_grad(at, "u_grad", 1, h_t, p, grad_u)
            ex0, ex1 = expand(at, 0, u, p), expand(at, 1, u, p)
        bias = bias[None, :]
        out, oth0 = input_grad(at, 0, c0, c_o, ex0, v, bias, g, None, width, [ex1])
        out, oth1 = input_grad(at, 1, c1, c_o, ex1, v, bias, g, out, width, tw=512)
        back = [trade(oth0), trade(oth1)]
        (grad_v,) = factor_grad(at, "v_grad", 0, x_t, g, None, after=[oth1])
        grad_v, out = factor_grad(at, "v_grad", 1, x_t, g, grad_v, (back, out))
        return out, grad_u, grad_v, jnp.concatenate([b0[0], b1[0]])

    return jax.shard_map(
        local,
        mesh=mesh,
        in_specs=(
            P(("group", "batch"), "col"),
            P(("group", "batch"), "col"),
            P(("col", "batch"), None),
            P(("col", "batch"), None),
            P("col"),
        ),
        out_specs=(
            P(("group", "batch"), "col"),
            P(("group", "col", "batch"), None),
            P(("group", "col", "batch"), None),
            P(("group", "col", "batch")),
        ),
        check_vma=False,
    )
```

```python
import jax
import jax.numpy as jnp
from jax import lax
from jax.experimental import pallas as pl
from jax.experimental.pallas import tpu as pltpu
from jax.sharding import PartitionSpec as P

BF, F32 = jnp.bfloat16, jnp.float32
MIB = 1 << 20
NT = (((1,), (1,)), ((), ()))


def call(body, name, at, ins, outs, scratch=(), flops=0, aliases=None, mib=4, after=(), us=0.6, carry=()):
    specs = {"v": pl.BlockSpec(memory_space=pltpu.VMEM), "h": pl.BlockSpec(memory_space=pl.ANY)}
    spaces = {"v": pltpu.VMEM, "h": pltpu.HBM}
    skip, n_outs = 1 + len(ins), len(outs)
    ins = list(ins) + [(a, "v") for a in carry] + [a if isinstance(a, tuple) else (a, "v") for a in after]
    outs = list(outs) + [(a.shape, a.dtype, "v") for a in carry]
    aliases = dict(aliases or {})
    aliases.update({skip + i: n_outs + i for i in range(len(carry))})
    args = [pltpu.with_memory_space_constraint(a, spaces[w]) for a, w in ins]
    first = skip + len(carry) + len(after)
    return pl.pallas_call(
        lambda *refs: body(*refs[:skip], *refs[first : first + n_outs], *refs[first + len(outs) :]),
        out_shape=tuple(spaces[w](dims, dtype) for dims, dtype, w in outs),
        in_specs=[pl.BlockSpec(memory_space=pltpu.SMEM)] + [specs[w] for _, w in ins],
        out_specs=tuple(specs[w] for _, _, w in outs),
        scratch_shapes=list(scratch),
        input_output_aliases=aliases,
        compiler_params=pltpu.CompilerParams(vmem_limit_bytes=mib * MIB),
        cost_estimate=pl.CostEstimate(flops=int(1.7 * flops + us * 1.15e9), bytes_accessed=0, transcendentals=0),
        name=name,
    )(at, *args)


def at_block(i, size):
    return pl.ds(pl.multiple_of(i * size, size), size)


def dma(n):
    return pltpu.SemaphoreType.DMA((n,))


def copy(src, dst, sem):
    return pltpu.make_async_copy(src, dst, sem)


def cut_half(at, x, half):
    rows = x.shape[0]
    n = 8
    step = rows // n

    def body(at_ref, x_ref, o_ref, sems):
        def cut(i):
            here = pl.ds(i * step, step)
            return copy(x_ref.at[here, at_block(1 - at_ref[0], half)], o_ref.at[here, :], sems.at[i])

        for i in range(n):
            cut(i).start()
        for i in range(n):
            cut(i).wait()

    return call(body, "cut_half", at, [(x, "h")], [((rows, half), BF, "v")], [dma(n)])[0]


VPARTS = 4


def project_own(at, x, v, c, after=()):
    rows, (half, rank) = x.shape[0], v.shape
    tk = half // VPARTS

    def body(at_ref, x_ref, v_ref, c_ref, p_ref, xv_ref, cs_ref, *refs):
        vv, (acc, x_sem, v_sem, c_sem) = refs[:VPARTS], refs[VPARTS:]

        def cut(ref, dst, core, k, sem):
            src = ref.at[:, pl.ds(pl.multiple_of(core * half + k * tk, tk), tk)]
            return copy(src, dst.at[:, pl.ds(k * tk, tk)], sem.at[k])

        def x_copy(k):
            return cut(x_ref, xv_ref, at_ref[0], k, x_sem)

        def c_copy(k):
            return cut(c_ref, cs_ref, 1 - at_ref[0], k, c_sem)

        def v_copy(k):
            return copy(v_ref.at[pl.ds(k * tk, tk), :], vv[k], v_sem.at[k])

        for k in range(VPARTS):
            x_copy(k).start()
            v_copy(k).start()
        for k in range(VPARTS):
            c_copy(k).start()
        for k in range(VPARTS):
            x_copy(k).wait()
            v_copy(k).wait()
            part = jnp.dot(xv_ref[:, pl.ds(k * tk, tk)], vv[k][...], preferred_element_type=F32)
            if k == VPARTS - 1:
                p_ref[...] = (acc[...] + part).astype(BF)
            else:
                acc[...] = acc[...] + part if k else part
        for k in range(VPARTS):
            c_copy(k).wait()

    return call(
        body,
        "project_own",
        at,
        [(x, "h"), (v, "h"), (c, "h")],
        [((rows, rank), BF, "v"), ((rows, half), BF, "v"), ((rows, half), BF, "v")] + [((tk, rank), BF, "v")] * VPARTS,
        [pltpu.VMEM((rows, rank), F32)] + [dma(VPARTS)] * 3,
        flops=2 * rows * half * rank,
        mib=6,
        after=after,
    )


def write_halves(at_ref, total, outs):
    if len(outs) == 1:
        outs[0][...] = total(slice(None))
        return
    each = outs[0].shape[0]
    bit = at_ref[1] & 1
    for i, o_ref in ((bit, outs[0]), (1 - bit, outs[1])):
        o_ref[...] = total(at_block(i, each)).astype(BF)


def halves_of(rows, rank, direct):
    return [((rows // 2, rank), BF, "v")] * 2 if direct else [((rows, rank), F32, "v")]


def project_other(at, x_o, vs, theirs, direct):
    rows = x_o.shape[0]
    tk, rank = vs[0].shape

    def body(at_ref, x_ref, t_ref, *refs):
        vv, outs, acc = refs[:VPARTS], refs[VPARTS:-1], refs[-1]
        for k in range(VPARTS):
            part = jnp.dot(x_ref[:, pl.ds(k * tk, tk)], vv[k][...], preferred_element_type=F32)
            acc[...] = part + (acc[...] if k else t_ref[...].astype(F32))
        write_halves(at_ref, lambda here: acc[here, :], outs)

    return call(
        body,
        "project_other",
        at,
        [(x_o, "v"), (theirs, "v")] + [(a, "v") for a in vs],
        halves_of(rows, rank, direct),
        [pltpu.VMEM((rows, rank), F32)],
        flops=2 * rows * tk * VPARTS * rank,
        mib=6,
    )


def hidden(c, x):
    return (c.astype(F32) * x.astype(F32)).astype(BF)


def back_project(at, s, x, x_o, c, c_o, u, so_far, after=(), tk=512):
    rows, (half, rank) = x.shape[0], u.shape
    part = half // 2
    tk = min(tk, part)
    n = part // tk
    slots = min(4, n)
    first = so_far is None

    def body(at_ref, x_ref, xo_ref, c_ref, co_ref, u_ref, *rest):
        if first:
            acc, b_ref, cv_ref, uv, h, c_sem, u_sem = rest
        else:
            so_ref, own_ref, oth_ref, b_ref, cv_ref, uv, h, acc, c_sem, u_sem = rest

        def c_copy(k):
            src = c_ref.at[:, pl.ds(pl.multiple_of(at_ref[0] * half + s * part + k * tk, tk), tk)]
            return copy(src, cv_ref.at[:, at_block(k, tk)], c_sem.at[k])

        def u_copy(k):
            slot = lax.rem(k, slots)
            return copy(u_ref.at[pl.ds(pl.multiple_of(s * part + k * tk, tk), tk), :], uv.at[slot], u_sem.at[slot])

        def make(k, slot):
            here = at_block(k, tk)
            there = pl.ds(pl.multiple_of(s * part + k * tk, tk), tk)
            own = hidden(cv_ref[:, here], x_ref[:, there])
            oth = hidden(co_ref[:, there], xo_ref[:, there])
            h[slot, :rows, :] = own
            h[slot, rows:, :] = oth
            b_ref[:, here] = jnp.sum(own.astype(F32), axis=0, keepdims=True) + jnp.sum(oth.astype(F32), axis=0, keepdims=True)

        def add(slot, k):
            acc[...] += jnp.dot(h[slot], uv[lax.rem(k, slots)], preferred_element_type=F32)

        for k in range(n):
            c_copy(k).start()
            if k < slots:
                u_copy(k).start()
        acc[...] = jnp.zeros_like(acc) if first else so_ref[...]
        c_copy(0).wait()
        make(0, 0)

        @pl.loop(0, n - 1)
        def _(k):
            c_copy(k + 1).wait()
            u_copy(k).wait()
            make(k + 1, lax.rem(k + 1, 2))
            add(lax.rem(k, 2), k)

            @pl.when(k + slots < n)
            def _():
                u_copy(k + slots).start()

        u_copy(n - 1).wait()
        add((n - 1) % 2, n - 1)
        if not first:
            own_ref[...] = acc[:rows, :].astype(BF)
            oth_ref[...] = acc[rows:, :]

    ends = [((1, part), F32, "v"), ((rows, part), BF, "v")]
    whole = pltpu.VMEM((2 * rows, rank), F32)
    return call(
        body,
        "back_project",
        at,
        [(x, "v"), (x_o, "v"), (c, "h"), (c_o, "v"), (u, "h")] + ([] if first else [(so_far, "v")]),
        ([((2 * rows, rank), F32, "v")] if first else [((rows, rank), BF, "v"), ((rows, rank), F32, "v")]) + ends,
        [pltpu.VMEM((slots, tk, rank), BF), pltpu.VMEM((2, 2 * rows, tk), BF)]
        + ([] if first else [whole])
        + [dma(n), dma(slots)],
        flops=2 * rows * half * rank,
        mib=12,
        after=after,
    )


def turn_x(at, x, after=()):
    rows, half = x.shape
    tw = min(512, half)

    def body(at_ref, x_ref, o_ref):
        @pl.loop(0, half // tw)
        def _(k):
            here = at_block(k, tw)
            o_ref[here, :] = x_ref[:, here].T

    return call(body, "turn_x", at, [(x, "v")], [((half, rows), BF, "v")], after=after, us=1.8)[0]


def turn_hidden(at, s, x, x_o, c, c_o, after=(), carry=()):
    rows, half = x.shape
    part = half // 2
    tw = min(512, part)

    def body(at_ref, x_ref, xo_ref, c_ref, co_ref, o_ref):
        @pl.loop(0, part // tw)
        def _(k):
            here = at_block(k, tw)
            there = pl.ds(pl.multiple_of(s * part + k * tw, tw), tw)
            o_ref[here, :rows] = hidden(c_ref[:, here], x_ref[:, there]).T
            o_ref[here, rows:] = hidden(co_ref[:, there], xo_ref[:, there]).T

    return call(
        body,
        "turn_hidden",
        at,
        [(a, "v") for a in (x, x_o, c, c_o)],
        [((part, 2 * rows), BF, "v")],
        mib=6,
        after=after,
        us=1.8,
        carry=carry,
    )


def fill(at_ref, both, refs):
    if len(refs) == 2:
        rows = refs[0].shape[0]
        both[:rows, :] = refs[0][...]
        both[rows:, :] = refs[1][...]
        return
    each = refs[0].shape[0]
    bit = at_ref[1] & 1
    for i, (keep, other) in enumerate((refs[:2], refs[2:])):
        both[at_block(2 * i + bit, each), :] = keep[...]
        both[at_block(2 * i + 1 - bit, each), :] = other[...]


def factor_grad(at, name, s, half, turned, p, so_far, placed=None, after=(), tw=1024):
    rows2, rank = sum(a.shape[0] for a in p), p[0].shape[1]
    part = half // 2
    shift = s * part if turned[0].shape[0] == half else 0
    nt = len(turned)
    tw = min(tw, part)
    n = part // tw
    np_ = len(p)
    recv, full = placed or ((), None)
    nr = len(recv)
    ins = [(a, "v") for a in (*turned, *p)]
    aliases = {}
    if so_far is not None:
        aliases[1 + len(ins)] = 0
        ins.append((so_far, "h"))
    if placed:
        ins += [(a, "v") for a in recv]
        aliases[1 + len(ins)] = 1
        ins.append((full, "h"))

    def body(at_ref, *refs):
        t_refs, refs = refs[:nt], refs[nt:]
        p_refs, refs = refs[:np_], refs[np_ + (so_far is not None) :]
        r_refs, refs = refs[:nr], refs[nr + (nr > 0) :]
        o_ref, refs = refs[0], refs[1:]
        if nr:
            f_ref, refs = refs[0], refs[1:]
        stage, both, sems, put_sem = refs

        def put(i):
            w = recv[i].shape[1]
            there = pl.ds(pl.multiple_of((1 - at_ref[0]) * half + i * w, w), w)
            return copy(r_refs[i], f_ref.at[:, there], put_sem.at[i])

        def out(k, slot):
            there = pl.ds(pl.multiple_of(s * part + k * tw, tw), tw)
            return copy(stage.at[slot], o_ref.at[there, :], sems.at[slot])

        for i in range(nr):
            put(i).start()
        fill(at_ref, both, p_refs)

        @pl.loop(0, n)
        def _(k):
            slot = lax.rem(k, 2)

            @pl.when(k >= 2)
            def _():
                out(k, slot).wait()

            here = pl.ds(pl.multiple_of(shift + k * tw, tw), tw)
            each = rows2 // nt
            parts = [
                jnp.dot(t_refs[i][here, :], both[i * each : (i + 1) * each, :], preferred_element_type=F32) for i in range(nt)
            ]
            stage[slot] = sum(parts[1:], parts[0]).astype(BF)
            out(k, slot).start()

        for k in range(max(0, n - 2), n):
            out(k, k % 2).wait()
        for i in range(nr):
            put(i).wait()

    outs = [((half, rank), BF, "h")] + ([(full.shape, BF, "h")] if placed else [])
    return call(
        body,
        name,
        at,
        ins,
        outs,
        [pltpu.VMEM((2, tw, rank), BF), pltpu.VMEM((rows2, rank), BF), dma(2), dma(max(1, nr))],
        flops=rows2 * half * rank,
        aliases=aliases,
        mib=12,
        after=after,
    )


def expand(at, s, u, p, after=(), tw=1024):
    half, rank = u.shape
    rows2 = sum(a.shape[0] for a in p)
    part = half // 2
    tw = min(tw, part)
    n = part // tw
    slots = min(3, n)

    def body(at_ref, u_ref, *refs):
        o_ref, uv, both, u_sem = refs[len(p) :]

        def u_copy(k):
            slot = lax.rem(k, slots)
            return copy(u_ref.at[pl.ds(pl.multiple_of(s * part + k * tw, tw), tw), :], uv.at[slot], u_sem.at[slot])

        for k in range(slots):
            u_copy(k).start()
        fill(at_ref, both, refs[: len(p)])

        @pl.loop(0, n)
        def _(k):
            u_copy(k).wait()
            o_ref[:, at_block(k, tw)] = lax.dot_general(both[...], uv[lax.rem(k, slots)], NT, preferred_element_type=F32)

            @pl.when(k + slots < n)
            def _():
                u_copy(k + slots).start()

    return call(
        body,
        "expand",
        at,
        [(u, "h")] + [(a, "v") for a in p],
        [((rows2, part), F32, "v")],
        [pltpu.VMEM((slots, tw, rank), BF), pltpu.VMEM((rows2, rank), BF), dma(slots)],
        flops=rows2 * half * rank,
        mib=10,
        after=after,
    )[0]


def input_grad(at, s, c, c_o, ex, v, bias, g, so_far, width, after=(), tw=1024):
    rows, half = c_o.shape
    rank = v.shape[1]
    part = half // 2
    tw = min(tw, part)
    n = part // tw
    slots = min(2, n)
    ng = len(g)

    def body(at_ref, c_ref, co_ref, ex_ref, v_ref, b_ref, *refs):
        g_refs, refs = refs[:ng], refs[ng + (so_far is not None) :]
        own_ref, oth_ref, stage, vv, both, sems, v_sem = refs

        def v_copy(k):
            slot = lax.rem(k, slots)
            return copy(v_ref.at[pl.ds(pl.multiple_of(s * part + k * tw, tw), tw), :], vv.at[slot], v_sem.at[slot])

        def columns(k):
            return pl.ds(pl.multiple_of(at_ref[0] * half + s * part + k * tw, tw), tw)

        def out(k, slot):
            return copy(stage.at[slot], own_ref.at[:, columns(k)], sems.at[slot])

        for k in range(slots):
            v_copy(k).start()
        fill(at_ref, both, g_refs)

        @pl.loop(0, n)
        def _(k):
            slot = lax.rem(k, 2)
            here = at_block(k, tw)
            there = pl.ds(pl.multiple_of(s * part + k * tw, tw), tw)
            v_copy(k).wait()

            @pl.when(k >= 2)
            def _():
                out(k, slot).wait()

            bk = lax.dot_general(both[...], vv[lax.rem(k, slots)], NT, preferred_element_type=F32)
            b = b_ref[:, columns(k)].astype(F32)
            cf, cof = c_ref[:, here].astype(F32), co_ref[:, there].astype(F32)
            stage[slot] = (cf * (ex_ref[:rows, here] + b) + cf + bk[:rows]).astype(BF)
            oth_ref[:, here] = (cof * (ex_ref[rows:, here] + b) + cof + bk[rows:]).astype(BF)
            out(k, slot).start()

            @pl.when(k + slots < n)
            def _():
                v_copy(k + slots).start()

        for k in range(max(0, n - 2), n):
            out(k, k % 2).wait()

    ins = [(c, "v"), (c_o, "v"), (ex, "v"), (v, "h"), (bias, "v")] + [(a, "v") for a in g]
    aliases = {}
    if so_far is not None:
        aliases = {1 + len(ins): 0}
        ins.append((so_far, "h"))
    return call(
        body,
        "input_grad",
        at,
        ins,
        [((rows, width), BF, "h"), ((rows, part), BF, "v")],
        [
            pltpu.VMEM((2, rows, tw), BF),
            pltpu.VMEM((slots, tw, rank), BF),
            pltpu.VMEM((2 * rows, rank), BF),
            dma(2),
            dma(slots),
        ],
        flops=2 * rows * half * rank,
        aliases=aliases,
        mib=12,
        after=after,
    )


def plus(a, b):
    return a.astype(F32) + b.astype(F32)


def pair_halves(at, a, b, direct, after=()):
    rows, rank = a.shape

    def body(at_ref, a_ref, b_ref, *outs):
        write_halves(at_ref, lambda here: plus(a_ref[here, :], b_ref[here, :]), outs)

    return call(body, "pair_halves", at, [(a, "v"), (b, "v")], halves_of(rows, rank, direct), after=after)


def pieces_of(at, a, b, m, after=(), carry=()):
    rows, rank = a.shape
    each = rows // m

    def body(at_ref, a_ref, b_ref, *outs):
        for d in range(m):
            here = at_block((at_ref[1] >> 1) ^ d, each)
            outs[d][...] = plus(a_ref[here, :], b_ref[here, :]).astype(BF)

    return call(body, "pieces_of", at, [(a, "v"), (b, "v")], [((each, rank), BF, "v")] * m, after=after, carry=carry)


def add_pieces(at, parts, after=(), carry=()):
    def body(at_ref, *refs):
        total = refs[0][...].astype(F32)
        for r in refs[1:-1]:
            total += r[...].astype(F32)
        refs[-1][...] = total.astype(BF)

    return call(body, "add_pieces", at, [(a, "v") for a in parts], [(parts[0].shape, BF, "v")], after=after, carry=carry)


def join_pieces(at, parts, after=()):
    m = len(parts)
    each, rank = parts[0].shape

    def body(at_ref, *refs):
        for d in range(m):
            refs[-1][at_block((at_ref[1] >> 1) ^ d, each), :] = refs[d][...]

    return call(body, "join_pieces", at, [(a, "v") for a in parts], [((m * each, rank), BF, "v")], after=after)[0]


def hold(at, a, after):
    def body(at_ref, a_ref, o_ref):
        pass

    return call(body, "hold", at, [(a, "v")], [(a.shape, a.dtype, "v")], aliases={1: 0}, after=after)[0]


def solution(mesh):
    n = mesh.shape["col"]
    m = n // 2
    swap = [(0, 1), (1, 0)]

    def trade(a):
        return lax.ppermute(a, "batch", swap)

    def to(a, d):
        return lax.ppermute(a, "col", [(i, i ^ d) for i in range(n)])

    def spread(parts):
        return [parts[0]] + [to(parts[d], 2 * d) for d in range(1, m)]

    def local(x, c, u, v, bias):
        half, width = u.shape[0], x.shape[1]
        core = lax.axis_index("batch")
        at = jnp.stack([core, lax.axis_index("col")]).astype(jnp.int32)
        direct = x.shape[0] % (16 * n) == 0 and n & (n - 1) == 0 and n > 2

        def plain(total):
            total = lax.psum(total, "col").astype(BF)
            return [trade(total), total]

        x_s = cut_half(at, x, half)
        x_o = trade(x_s)
        own, x_own, c_s, *v_in = project_own(at, x, v, c, [x_s])
        theirs = trade(own)
        x_t = turn_x(at, x_own)
        c_o = trade(hold(at, c_s, [theirs, x_t]))
        sums = project_other(at, x_o, v_in, theirs, direct)
        x_t = [x_t, turn_x(at, x_o, [sums[0]])]
        acc, b0, c0 = back_project(at, 0, x_own, x_o, c, c_o, u, None, x_t)
        if direct:
            parts = pieces_of(at, sums[0], to(sums[1], 1), m, [acc])
            own_g, mine_g, b1, c1 = back_project(at, 1, x_own, x_o, c, c_o, u, acc, [parts[0]])
            total, own_g = add_pieces(at, spread(parts), carry=[own_g])
            (h_t0,) = turn_hidden(at, 0, x_own, x_o, c0, c_o, [total])
            sums_g = pair_halves(at, mine_g, trade(own_g), direct, [h_t0])
            half_p = join_pieces(at, spread([total] * m), [sums_g[0]])
            other_p = to(half_p, 1)
            *parts_g, other_p = pieces_of(at, sums_g[0], to(sums_g[1], 1), m, [half_p], carry=[other_p])
            (h_t1,) = turn_hidden(at, 1, x_own, x_o, c1, c_o, [parts_g[0]])
            p = [trade(half_p), trade(other_p), half_p, other_p]
            (grad_u,) = factor_grad(at, "u_grad", 0, half, [h_t0], p, None, after=[h_t1])
            (total_g,) = add_pieces(at, spread(parts_g), [(grad_u, "h")])
            (grad_u,) = factor_grad(at, "u_grad", 1, half, [h_t1], p, grad_u, after=[total_g])
            half_g = join_pieces(at, spread([total_g] * m), [(grad_u, "h")])
            other_g = to(half_g, 1)
            ex0 = expand(at, 0, u, p, [half_g])
            g = [trade(half_g), trade(other_g), half_g, other_g]
            ex1 = expand(at, 1, u, p, [ex0])
        else:
            own_g, mine_g, b1, c1 = back_project(at, 1, x_own, x_o, c, c_o, u, acc)
            (sums_g,) = pair_halves(at, mine_g, trade(own_g), direct)
            p, g = plain(sums[0]), plain(sums_g)
            (h_t0,) = turn_hidden(at, 0, x_own, x_o, c0, c_o)
            (h_t1,) = turn_hidden(at, 1, x_own, x_o, c1, c_o)
            (grad_u,) = factor_grad(at, "u_grad", 0, half, [h_t0], p, None)
            (grad_u,) = factor_grad(at, "u_grad", 1, half, [h_t1], p, grad_u)
            ex0, ex1 = expand(at, 0, u, p), expand(at, 1, u, p)
        bias = bias[None, :]
        out, oth0 = input_grad(at, 0, c0, c_o, ex0, v, bias, g, None, width, [ex1])
        out, oth1 = input_grad(at, 1, c1, c_o, ex1, v, bias, g, out, width)
        back = [trade(oth0), trade(oth1)]
        (grad_v,) = factor_grad(at, "v_grad", 0, half, x_t, g, None, after=[oth1])
        grad_v, out = factor_grad(at, "v_grad", 1, half, x_t, g, grad_v, (back, out))
        return out, grad_u, grad_v, jnp.concatenate([b0[0], b1[0]])

    return jax.shard_map(
        local,
        mesh=mesh,
        in_specs=(
            P(("group", "batch"), "col"),
            P(("group", "batch"), "col"),
            P(("col", "batch"), None),
            P(("col", "batch"), None),
            P("col"),
        ),
        out_specs=(
            P(("group", "batch"), "col"),
            P(("group", "col", "batch"), None),
            P(("group", "col", "batch"), None),
            P(("group", "col", "batch")),
        ),
        check_vma=False,
    )
```

```python
import jax
import jax.numpy as jnp
from jax import lax
from jax.experimental import pallas as pl
from jax.experimental.pallas import tpu as pltpu
from jax.sharding import PartitionSpec as P

BF, F32 = jnp.bfloat16, jnp.float32
MIB = 1 << 20
NT = (((1,), (1,)), ((), ()))


class Place:
    def __getitem__(self, i):
        return lax.axis_index(("batch", "col")[i])


def call(body, name, ins, outs, scratch=(), flops=0, aliases=None, mib=4, after=(), us=0.3, carry=(), ahead=()):
    specs = {"v": pl.BlockSpec(memory_space=pltpu.VMEM), "h": pl.BlockSpec(memory_space=pl.ANY)}
    spaces = {"v": pltpu.VMEM, "h": pltpu.HBM}
    n_ins, n_ahead, n_outs, n_after = len(ins), len(ahead), len(outs), len(after)
    aliases = dict(aliases or {})
    aliases.update({n_ins + n_ahead + i: n_outs + n_ahead + i for i in range(len(carry))})
    ins = list(ins) + [(a, "h") for a, _, _ in ahead] + [(a, "v") for a in carry]
    ins += [a if isinstance(a, tuple) else (a, "v") for a in after]
    outs = list(outs) + [((rows, a.shape[1]), a.dtype, "v") for a, _, rows in ahead] + [(a.shape, a.dtype, "v") for a in carry]
    args = [pltpu.with_memory_space_constraint(a, spaces[w]) for a, w in ins]

    def whole(*refs):
        first = len(ins)
        sems = refs[-1] if n_ahead else None
        scratch_refs = refs[first + len(outs) : len(refs) - (n_ahead > 0)]
        fetches = [
            pltpu.make_async_copy(refs[n_ins + i].at[pl.ds(row, rows), :], refs[first + n_outs + i], sems.at[i])
            for i, (_, row, rows) in enumerate(ahead)
        ]
        body(Place(), *refs[:n_ins], *refs[first : first + n_outs], *scratch_refs, fetch=lambda: [f.start() for f in fetches])
        for f in fetches:
            f.wait()

    return pl.pallas_call(
        whole if n_ahead else lambda *refs: body(Place(), *refs[:n_ins], *refs[len(ins) : len(ins) + n_outs], *refs[len(ins) + len(outs) :]),
        out_shape=tuple(spaces[w](dims, dtype) for dims, dtype, w in outs),
        in_specs=[specs[w] for _, w in ins],
        out_specs=tuple(specs[w] for _, _, w in outs),
        scratch_shapes=list(scratch) + ([pltpu.SemaphoreType.DMA((n_ahead,))] if n_ahead else []),
        input_output_aliases=aliases,
        compiler_params=pltpu.CompilerParams(vmem_limit_bytes=mib * MIB),
        cost_estimate=pl.CostEstimate(flops=int(1.7 * flops + us * 1.15e9), bytes_accessed=0, transcendentals=0),
        name=name,
    )(*args)


def nothing():
    pass


def at_block(i, size):
    return pl.ds(pl.multiple_of(i * size, size), size)


def dma(n):
    return pltpu.SemaphoreType.DMA((n,))


def copy(src, dst, sem):
    return pltpu.make_async_copy(src, dst, sem)


def cut_half(x, half):
    rows = x.shape[0]
    n = 8
    step = rows // n

    def body(at_ref, x_ref, o_ref, sems):
        def cut(i):
            here = pl.ds(i * step, step)
            return copy(x_ref.at[here, at_block(1 - at_ref[0], half)], o_ref.at[here, :], sems.at[i])

        for i in range(n):
            cut(i).start()
        for i in range(n):
            cut(i).wait()

    return call(body, "cut_half", [(x, "h")], [((rows, half), BF, "v")], [dma(n)])[0]


VPARTS = 4


def project_own(x, v, c, after=()):
    rows, (half, rank) = x.shape[0], v.shape
    tk = half // VPARTS

    def body(at_ref, x_ref, v_ref, c_ref, p_ref, xv_ref, cs_ref, *refs):
        vv, (acc, x_sem, v_sem, c_sem) = refs[:VPARTS], refs[VPARTS:]

        def cut(ref, dst, core, k, sem):
            src = ref.at[:, pl.ds(pl.multiple_of(core * half + k * tk, tk), tk)]
            return copy(src, dst.at[:, pl.ds(k * tk, tk)], sem.at[k])

        def x_copy(k):
            return cut(x_ref, xv_ref, at_ref[0], k, x_sem)

        def c_copy(k):
            return cut(c_ref, cs_ref, 1 - at_ref[0], k, c_sem)

        def v_copy(k):
            return copy(v_ref.at[pl.ds(k * tk, tk), :], vv[k], v_sem.at[k])

        for k in range(VPARTS):
            x_copy(k).start()
            v_copy(k).start()
        for k in range(VPARTS):
            c_copy(k).start()
        for k in range(VPARTS):
            x_copy(k).wait()
            v_copy(k).wait()
            part = jnp.dot(xv_ref[:, pl.ds(k * tk, tk)], vv[k][...], preferred_element_type=F32)
            if k == VPARTS - 1:
                p_ref[...] = (acc[...] + part).astype(BF)
            else:
                acc[...] = acc[...] + part if k else part
        for k in range(VPARTS):
            c_copy(k).wait()

    return call(
        body,
        "project_own",
        [(x, "h"), (v, "h"), (c, "h")],
        [((rows, rank), BF, "v"), ((rows, half), BF, "v"), ((rows, half), BF, "v")] + [((tk, rank), BF, "v")] * VPARTS,
        [pltpu.VMEM((rows, rank), F32)] + [dma(VPARTS)] * 3,
        flops=2 * rows * half * rank,
        mib=6,
        after=after,
    )


def write_halves(at_ref, total, outs):
    if len(outs) == 1:
        outs[0][...] = total(slice(None))
        return
    each = outs[0].shape[0]
    bit = at_ref[1] & 1
    for i, o_ref in ((bit, outs[0]), (1 - bit, outs[1])):
        o_ref[...] = total(at_block(i, each)).astype(BF)


def halves_of(rows, rank, direct):
    return [((rows // 2, rank), BF, "v")] * 2 if direct else [((rows, rank), F32, "v")]


def project_other(x_o, vs, theirs, direct):
    rows = x_o.shape[0]
    tk, rank = vs[0].shape

    def body(at_ref, x_ref, t_ref, *refs):
        vv, outs, acc = refs[:VPARTS], refs[VPARTS:-1], refs[-1]
        for k in range(VPARTS):
            part = jnp.dot(x_ref[:, pl.ds(k * tk, tk)], vv[k][...], preferred_element_type=F32)
            acc[...] = part + (acc[...] if k else t_ref[...].astype(F32))
        write_halves(at_ref, lambda here: acc[here, :], outs)

    return call(
        body,
        "project_other",
        [(x_o, "v"), (theirs, "v")] + [(a, "v") for a in vs],
        halves_of(rows, rank, direct),
        [pltpu.VMEM((rows, rank), F32)],
        flops=2 * rows * tk * VPARTS * rank,
        mib=6,
    )


def hidden(c, x):
    return (c.astype(F32) * x.astype(F32)).astype(BF)


def back_project(s, x, x_o, c, c_o, u, u_first, so_far, c_all=None, after=()):
    rows, (half, rank) = x.shape[0], u.shape
    part = half // 2
    tk = u_first.shape[0]
    n = part // tk
    first = so_far is None
    n_outs = 2 if first else 3

    def body(at_ref, x_ref, xo_ref, c_ref, co_ref, u_ref, uf_ref, *refs, fetch=nothing):
        if first:
            all_ref, acc_ref, b_ref, next_ref, uv, h, u_sem, c_sem = refs
            src = all_ref.at[:, pl.ds(pl.multiple_of(at_ref[0] * half + part, part), part)]
            next_c = copy(src, next_ref, c_sem.at[0])
        else:
            so_ref, own_ref, oth_ref, b_ref, uv, h, u_sem = refs

        def u_copy(k):
            return copy(u_ref.at[pl.ds(s * part + k * tk, tk), :], uv.at[k - 1], u_sem.at[k - 1])

        for k in range(1, n):
            u_copy(k).start()
        if first:
            next_c.start()
        fetch()
        for k in range(n):
            here = pl.ds(k * tk, tk)
            there = pl.ds(s * part + k * tk, tk)
            own = hidden(c_ref[:, here], x_ref[:, there])
            oth = hidden(co_ref[:, there], xo_ref[:, there])
            h[k, :rows, :] = own
            h[k, rows:, :] = oth
            b_ref[:, here] = jnp.sum(own.astype(F32), axis=0, keepdims=True) + jnp.sum(oth.astype(F32), axis=0, keepdims=True)
        for i in range(2):
            at_rows = slice(i * rows, (i + 1) * rows)
            total = None if first else so_ref[at_rows, :]
            for k in range(n):
                if k and not i:
                    u_copy(k).wait()
                term = jnp.dot(h[k, at_rows, :], uv[k - 1] if k else uf_ref[...], preferred_element_type=F32)
                total = term if total is None else total + term
            if first:
                acc_ref[at_rows, :] = total
            elif i:
                oth_ref[...] = total
            else:
                own_ref[...] = total.astype(BF)
        if first:
            next_c.wait()

    outs = [((2 * rows, rank), F32, "v")] if first else [((rows, rank), BF, "v"), ((rows, rank), F32, "v")]
    outs += [((1, part), F32, "v")] + ([((rows, part), BF, "v")] if first else [])
    return call(
        body,
        "back_project",
        [(x, "v"), (x_o, "v"), (c, "v"), (c_o, "v"), (u, "h"), (u_first, "v"), (c_all, "h") if first else (so_far, "v")],
        outs,
        [pltpu.VMEM((max(1, n - 1), tk, rank), BF), pltpu.VMEM((n, 2 * rows, tk), BF), dma(max(1, n - 1))]
        + ([dma(1)] if first else []),
        flops=2 * rows * half * rank,
        mib=13,
        after=after,
        ahead=[(u, part, tk)] if first else [],
    )


def turn_x(x, c=None, u=None, after=()):
    rows, half = x.shape
    tw = min(512, half)
    part = half // 2
    n = half // tw
    slots = min(4, n)

    def body(at_ref, x_ref, *refs, fetch=nothing):
        fetch()
        if c is None:
            o_ref, stage, sems = refs
        else:
            c_ref, o_ref, cv_ref, stage, sems, c_sem = refs
            first_c = copy(c_ref.at[:, at_block(2 * at_ref[0], part)], cv_ref, c_sem.at[0])
            first_c.start()

        def out(k):
            return copy(stage.at[k % slots], o_ref.at[pl.ds(k * tw, tw), :], sems.at[k % slots])

        for k in range(n):
            if k >= slots:
                out(k - slots).wait()
            stage[k % slots] = x_ref[:, k * tw : (k + 1) * tw].T
            out(k).start()
        for k in range(n - slots, n):
            out(k).wait()
        if c is not None:
            first_c.wait()

    out_x = ((half, rows), BF, "h")
    scratch = [pltpu.VMEM((slots, tw, rows), BF), dma(slots)]
    if c is None:
        return call(body, "turn_x", [(x, "v")], [out_x], scratch, after=after, us=1.8)
    return call(
        body,
        "turn_x",
        [(x, "v"), (c, "h")],
        [out_x, ((rows, part), BF, "v")],
        scratch + [dma(1)],
        after=after,
        us=1.8,
        ahead=[(u, 0, part // 2)],
    )


def turn_hidden(s, x, x_o, c, c_o, after=(), carry=()):
    rows, half = x.shape
    part = half // 2
    tw = min(512, part)

    def body(at_ref, x_ref, xo_ref, c_ref, co_ref, o_ref):
        @pl.loop(0, part // tw)
        def _(k):
            here = at_block(k, tw)
            there = pl.ds(pl.multiple_of(s * part + k * tw, tw), tw)
            o_ref[here, :rows] = hidden(c_ref[:, here], x_ref[:, there]).T
            o_ref[here, rows:] = hidden(co_ref[:, there], xo_ref[:, there]).T

    return call(
        body,
        "turn_hidden",
        [(a, "v") for a in (x, x_o, c, c_o)],
        [((part, 2 * rows), BF, "v")],
        mib=6,
        after=after,
        us=1.8,
        carry=carry,
    )


def fill(at_ref, both, refs):
    if len(refs) == 2:
        rows = refs[0].shape[0]
        both[:rows, :] = refs[0][...]
        both[rows:, :] = refs[1][...]
        return
    each = refs[0].shape[0]
    bit = at_ref[1] & 1
    for i, (keep, other) in enumerate((refs[:2], refs[2:])):
        both[at_block(2 * i + bit, each), :] = keep[...]
        both[at_block(2 * i + 1 - bit, each), :] = other[...]


def factor_grad(name, s, half, turned, p, so_far, placed=None, after=(), tw=1024, ahead=()):
    rows2, rank = sum(a.shape[0] for a in p), p[0].shape[1]
    part = half // 2
    shift = s * part if turned[0].shape[0] == half else 0
    nt = len(turned)
    tw = min(tw, part)
    n = part // tw
    slots = min(n, max(2, 2048 // tw))
    np_ = len(p)
    recv, full = placed or ((), None)
    nr = len(recv)
    far = nt > 1
    ins = [(a, "h" if far else "v") for a in turned] + [(a, "v") for a in p]
    aliases = {}
    if so_far is not None:
        aliases[len(ins)] = 0
        ins.append((so_far, "h"))
    if placed:
        ins += [(a, "v") for a in recv]
        aliases[len(ins)] = 1
        ins.append((full, "h"))

    def body(at_ref, *refs, fetch=nothing):
        t_refs, refs = refs[:nt], refs[nt:]
        p_refs, refs = refs[:np_], refs[np_ + (so_far is not None) :]
        r_refs, refs = refs[:nr], refs[nr + (nr > 0) :]
        o_ref, refs = refs[0], refs[1:]
        if nr:
            f_ref, refs = refs[0], refs[1:]
        stage, both, sems, put_sem, *refs = refs

        def left_copy(i, k):
            here = pl.ds(k * tw, tw)
            return copy(t_refs[i].at[pl.ds(shift + k * tw, tw), :], refs[0].at[i, here, :], refs[1].at[i, k])

        if far:
            for k in range(n):
                for i in range(nt):
                    left_copy(i, k).start()

        def left(i, k):
            if not far:
                return t_refs[i][pl.ds(shift + k * tw, tw), :]
            left_copy(i, k).wait()
            return refs[0][i, pl.ds(k * tw, tw), :]

        def put(i):
            w = recv[i].shape[1]
            there = pl.ds(pl.multiple_of((1 - at_ref[0]) * half + i * w, w), w)
            return copy(r_refs[i], f_ref.at[:, there], put_sem.at[i])

        def out(k):
            return copy(stage.at[k % slots], o_ref.at[pl.ds(s * part + k * tw, tw), :], sems.at[k % slots])

        for i in range(nr):
            put(i).start()
        fetch()
        fill(at_ref, both, p_refs)
        each = rows2 // nt
        for k in range(n):
            parts = [
                jnp.dot(left(i, k), both[i * each : (i + 1) * each, :], preferred_element_type=F32) for i in range(nt)
            ]
            if k >= slots:
                out(k - slots).wait()
            stage[k % slots] = sum(parts[1:], parts[0]).astype(BF)
            out(k).start()
        for k in range(max(0, n - slots), n):
            out(k).wait()
        for i in range(nr):
            put(i).wait()

    outs = [((half, rank), BF, "h")] + ([(full.shape, BF, "h")] if placed else [])
    return call(
        body,
        name,
        ins,
        outs,
        [pltpu.VMEM((slots, tw, rank), BF), pltpu.VMEM((rows2, rank), BF), dma(slots), dma(max(1, nr))]
        + ([pltpu.VMEM((nt, part, rows2 // nt), BF), pltpu.SemaphoreType.DMA((nt, n))] if far else []),
        flops=rows2 * half * rank,
        aliases=aliases,
        mib=16 if far else 12,
        after=after,
        ahead=ahead,
    )


def expand(s, u, u_first, p, after=(), ahead=()):
    half, rank = u.shape
    rows2 = sum(a.shape[0] for a in p)
    part = half // 2
    tw = u_first.shape[0]
    n = part // tw

    def body(at_ref, u_ref, uf_ref, *refs, fetch=nothing):
        o_ref, uv, both, u_sem = refs[len(p) :]

        def u_copy(k):
            return copy(u_ref.at[pl.ds(s * part + k * tw, tw), :], uv.at[k - 1], u_sem.at[k - 1])

        for k in range(1, n):
            u_copy(k).start()
        fetch()
        fill(at_ref, both, refs[: len(p)])
        for k in range(n):
            if k:
                u_copy(k).wait()
            block = uv[k - 1] if k else uf_ref[...]
            o_ref[:, k * tw : (k + 1) * tw] = lax.dot_general(both[...], block, NT, preferred_element_type=F32)

    return call(
        body,
        "expand",
        [(u, "h"), (u_first, "v")] + [(a, "v") for a in p],
        [((rows2, part), F32, "v")],
        [pltpu.VMEM((max(1, n - 1), tw, rank), BF), pltpu.VMEM((rows2, rank), BF), dma(max(1, n - 1))],
        flops=rows2 * half * rank,
        mib=10,
        after=after,
        ahead=ahead,
    )


def input_grad(s, c, c_o, ex, v, v_first, bias, g, so_far, width, after=(), ahead=()):
    rows, half = c_o.shape
    rank = v.shape[1]
    part = half // 2
    tw = v_first.shape[0]
    n = part // tw
    ng = len(g)

    def body(at_ref, c_ref, co_ref, ex_ref, v_ref, vf_ref, b_ref, *refs, fetch=nothing):
        g_refs, refs = refs[:ng], refs[ng + (so_far is not None) :]
        own_ref, oth_ref, stage, vv, both, sems, v_sem = refs

        def v_copy(k):
            return copy(v_ref.at[pl.ds(s * part + k * tw, tw), :], vv.at[k - 1], v_sem.at[k - 1])

        def columns(k):
            return pl.ds(pl.multiple_of(at_ref[0] * half + s * part + k * tw, tw), tw)

        def out(k):
            return copy(stage.at[k % 2], own_ref.at[:, columns(k)], sems.at[k % 2])

        for k in range(1, n):
            v_copy(k).start()
        fetch()
        fill(at_ref, both, g_refs)
        for k in range(n):
            here = pl.ds(k * tw, tw)
            there = pl.ds(s * part + k * tw, tw)
            if k:
                v_copy(k).wait()
            if k >= 2:
                out(k - 2).wait()
            bk = lax.dot_general(both[...], vv[k - 1] if k else vf_ref[...], NT, preferred_element_type=F32)
            b = b_ref[:, columns(k)].astype(F32)
            cf, cof = c_ref[:, here].astype(F32), co_ref[:, there].astype(F32)
            stage[k % 2] = (cf * (ex_ref[:rows, here] + b) + cf + bk[:rows]).astype(BF)
            oth_ref[:, here] = (cof * (ex_ref[rows:, here] + b) + cof + bk[rows:]).astype(BF)
            out(k).start()
        for k in range(max(0, n - 2), n):
            out(k).wait()

    ins = [(c, "v"), (c_o, "v"), (ex, "v"), (v, "h"), (v_first, "v"), (bias, "v")] + [(a, "v") for a in g]
    aliases = {}
    if so_far is not None:
        aliases = {len(ins): 0}
        ins.append((so_far, "h"))
    return call(
        body,
        "input_grad",
        ins,
        [((rows, width), BF, "h"), ((rows, part), BF, "v")],
        [
            pltpu.VMEM((2, rows, tw), BF),
            pltpu.VMEM((max(1, n - 1), tw, rank), BF),
            pltpu.VMEM((2 * rows, rank), BF),
            dma(2),
            dma(max(1, n - 1)),
        ],
        flops=2 * rows * half * rank,
        aliases=aliases,
        mib=12,
        after=after,
        ahead=ahead,
    )


def plus(a, b):
    return a.astype(F32) + b.astype(F32)


def pair_halves(a, b, direct, after=()):
    rows, rank = a.shape

    def body(at_ref, a_ref, b_ref, *outs):
        write_halves(at_ref, lambda here: plus(a_ref[here, :], b_ref[here, :]), outs)

    return call(body, "pair_halves", [(a, "v"), (b, "v")], halves_of(rows, rank, direct), after=after)


def pieces_of(a, b, m, after=(), carry=()):
    rows, rank = a.shape
    each = rows // m

    def body(at_ref, a_ref, b_ref, *outs):
        for d in range(m):
            here = at_block((at_ref[1] >> 1) ^ d, each)
            outs[d][...] = plus(a_ref[here, :], b_ref[here, :]).astype(BF)

    return call(body, "pieces_of", [(a, "v"), (b, "v")], [((each, rank), BF, "v")] * m, after=after, carry=carry)


def add_pieces(parts, after=(), carry=()):
    def body(at_ref, *refs):
        total = refs[0][...].astype(F32)
        for r in refs[1:-1]:
            total += r[...].astype(F32)
        refs[-1][...] = total.astype(BF)

    return call(body, "add_pieces", [(a, "v") for a in parts], [(parts[0].shape, BF, "v")], after=after, carry=carry)


def join_pieces(parts, after=()):
    m = len(parts)
    each, rank = parts[0].shape

    def body(at_ref, *refs):
        for d in range(m):
            refs[-1][at_block((at_ref[1] >> 1) ^ d, each), :] = refs[d][...]

    return call(body, "join_pieces", [(a, "v") for a in parts], [((m * each, rank), BF, "v")], after=after)[0]


def hold(a, after):
    def body(at_ref, a_ref, o_ref):
        pass

    return call(body, "hold", [(a, "v")], [(a.shape, a.dtype, "v")], aliases={0: 0}, after=after)[0]


def solution(mesh):
    n = mesh.shape["col"]
    m = n // 2
    swap = [(0, 1), (1, 0)]

    def trade(a):
        return lax.ppermute(a, "batch", swap)

    def to(a, d):
        return lax.ppermute(a, "col", [(i, i ^ d) for i in range(n)])

    def spread(parts):
        return [parts[0]] + [to(parts[d], 2 * d) for d in range(1, m)]

    def local(x, c, u, v, bias):
        half, width = u.shape[0], x.shape[1]
        direct = x.shape[0] % (16 * n) == 0 and n & (n - 1) == 0 and n > 2

        def plain(total):
            total = lax.psum(total, "col").astype(BF)
            return [trade(total), total]

        part = half // 2
        tw = min(1024, part)
        x_s = cut_half(x, half)
        x_o = trade(x_s)
        own, x_own, c_s, *v_in = project_own(x, v, c, [x_s])
        theirs = trade(own)
        (x_t,) = turn_x(x_own)
        c_o = trade(hold(c_s, [theirs, (x_t, "h")]))
        sums = project_other(x_o, v_in, theirs, direct)
        x_to, c0, u0 = turn_x(x_o, c, u, [sums[0]])
        x_t = [x_t, x_to]
        acc, b0, c1, u1 = back_project(0, x_own, x_o, c0, c_o, u, u0, None, c, [(x_to, "h")])
        if direct:
            parts = pieces_of(sums[0], to(sums[1], 1), m, [acc])
            own_g, mine_g, b1 = back_project(1, x_own, x_o, c1, c_o, u, u1, acc, after=[parts[0]])
            total, own_g = add_pieces(spread(parts), carry=[own_g])
            (h_t0,) = turn_hidden(0, x_own, x_o, c0, c_o, [total])
            sums_g = pair_halves(mine_g, trade(own_g), direct, [h_t0])
            half_p = join_pieces(spread([total] * m), [sums_g[0]])
            other_p = to(half_p, 1)
            (h_t1,) = turn_hidden(1, x_own, x_o, c1, c_o, [half_p])
            other_p = hold(other_p, [h_t1])
            p = [trade(half_p), trade(other_p), half_p, other_p]
            (grad_u,) = factor_grad("u_grad", 0, half, [h_t0], p, None, after=[h_t1], tw=512)
            parts_g = pieces_of(sums_g[0], to(sums_g[1], 1), m, [(grad_u, "h")])
            grad_u, u0 = factor_grad("u_grad", 1, half, [h_t1], p, grad_u, after=[parts_g[0]], tw=512, ahead=[(u, 0, tw)])
            (total_g,) = add_pieces(spread(parts_g), [(grad_u, "h")])
            ex0, u1 = expand(0, u, u0, p, [total_g], [(u, part, tw)])
            half_g = join_pieces(spread([total_g] * m), [ex0])
            other_g = to(half_g, 1)
            ex1, v0 = expand(1, u, u1, p, [half_g], [(v, 0, tw)])
            other_g = hold(other_g, [ex1])
            g = [trade(half_g), trade(other_g), half_g, other_g]
        else:
            own_g, mine_g, b1 = back_project(1, x_own, x_o, c1, c_o, u, u1, acc)
            (sums_g,) = pair_halves(mine_g, trade(own_g), direct)
            p, g = plain(sums[0]), plain(sums_g)
            (h_t0,) = turn_hidden(0, x_own, x_o, c0, c_o)
            (h_t1,) = turn_hidden(1, x_own, x_o, c1, c_o)
            (grad_u,) = factor_grad("u_grad", 0, half, [h_t0], p, None)
            grad_u, u0 = factor_grad("u_grad", 1, half, [h_t1], p, grad_u, ahead=[(u, 0, tw)])
            ex0, u1 = expand(0, u, u0, p, ahead=[(u, part, tw)])
            ex1, v0 = expand(1, u, u1, p, ahead=[(v, 0, tw)])
        bias = bias[None, :]
        out, oth0, v1 = input_grad(0, c0, c_o, ex0, v, v0, bias, g, None, width, [ex1], [(v, part, tw)])
        out, oth1 = input_grad(1, c1, c_o, ex1, v, v1, bias, g, out, width)
        back = [trade(oth0), trade(oth1)]
        (grad_v,) = factor_grad("v_grad", 0, half, x_t, g, None, after=[oth1])
        grad_v, out = factor_grad("v_grad", 1, half, x_t, g, grad_v, (back, out))
        return out, grad_u, grad_v, jnp.concatenate([b0[0], b1[0]])

    return jax.shard_map(
        local,
        mesh=mesh,
        in_specs=(
            P(("group", "batch"), "col"),
            P(("group", "batch"), "col"),
            P(("col", "batch"), None),
            P(("col", "batch"), None),
            P("col"),
        ),
        out_specs=(
            P(("group", "batch"), "col"),
            P(("group", "col", "batch"), None),
            P(("group", "col", "batch"), None),
            P(("group", "col", "batch")),
        ),
        check_vma=False,
    )
```

```python
import jax
import jax.numpy as jnp
from jax import lax
from jax.experimental import pallas as pl
from jax.experimental.pallas import tpu as pltpu
from jax.sharding import PartitionSpec as P

BF, F32 = jnp.bfloat16, jnp.float32
MIB = 1 << 20
NT = (((1,), (1,)), ((), ()))


class Place:
    def __getitem__(self, i):
        return lax.axis_index(("batch", "col")[i])


def call(body, name, ins, outs, scratch=(), flops=0, aliases=None, mib=4, after=(), us=0.3, carry=(), ahead=()):
    specs = {"v": pl.BlockSpec(memory_space=pltpu.VMEM), "h": pl.BlockSpec(memory_space=pl.ANY)}
    spaces = {"v": pltpu.VMEM, "h": pltpu.HBM}
    n_ins, n_ahead, n_outs, n_after = len(ins), len(ahead), len(outs), len(after)
    aliases = dict(aliases or {})
    aliases.update({n_ins + n_ahead + i: n_outs + n_ahead + i for i in range(len(carry))})
    ins = list(ins) + [(a, "h") for a, _, _ in ahead] + [(a, "v") for a in carry]
    ins += [a if isinstance(a, tuple) else (a, "v") for a in after]
    outs = list(outs) + [((rows, a.shape[1]), a.dtype, "v") for a, _, rows in ahead] + [(a.shape, a.dtype, "v") for a in carry]
    args = [pltpu.with_memory_space_constraint(a, spaces[w]) for a, w in ins]

    def whole(*refs):
        first = len(ins)
        sems = refs[-1] if n_ahead else None
        scratch_refs = refs[first + len(outs) : len(refs) - (n_ahead > 0)]
        fetches = [
            pltpu.make_async_copy(refs[n_ins + i].at[pl.ds(row, rows), :], refs[first + n_outs + i], sems.at[i])
            for i, (_, row, rows) in enumerate(ahead)
        ]
        body(Place(), *refs[:n_ins], *refs[first : first + n_outs], *scratch_refs, fetch=lambda: [f.start() for f in fetches])
        for f in fetches:
            f.wait()

    return pl.pallas_call(
        whole if n_ahead else lambda *refs: body(Place(), *refs[:n_ins], *refs[len(ins) : len(ins) + n_outs], *refs[len(ins) + len(outs) :]),
        out_shape=tuple(spaces[w](dims, dtype) for dims, dtype, w in outs),
        in_specs=[specs[w] for _, w in ins],
        out_specs=tuple(specs[w] for _, _, w in outs),
        scratch_shapes=list(scratch) + ([pltpu.SemaphoreType.DMA((n_ahead,))] if n_ahead else []),
        input_output_aliases=aliases,
        compiler_params=pltpu.CompilerParams(vmem_limit_bytes=mib * MIB),
        cost_estimate=pl.CostEstimate(flops=int(1.7 * flops + us * 1.15e9), bytes_accessed=0, transcendentals=0),
        name=name,
    )(*args)


def nothing():
    pass


def at_block(i, size):
    return pl.ds(pl.multiple_of(i * size, size), size)


def dma(n):
    return pltpu.SemaphoreType.DMA((n,))


def copy(src, dst, sem):
    return pltpu.make_async_copy(src, dst, sem)


def cut_half(x, half, after=()):
    rows = x.shape[0]
    n = 8
    step = rows // n

    def body(at_ref, x_ref, o_ref, sems):
        def cut(i):
            here = pl.ds(i * step, step)
            return copy(x_ref.at[here, at_block(1 - at_ref[0], half)], o_ref.at[here, :], sems.at[i])

        for i in range(n):
            cut(i).start()
        for i in range(n):
            cut(i).wait()

    return call(body, "cut_half", [(x, "h")], [((rows, half), BF, "v")], [dma(n)], us=2.2, after=after)[0]


VPARTS = 4


def project_own(x, v, c, after=()):
    rows, (half, rank) = x.shape[0], v.shape
    part = half // VPARTS
    tk = min(1024, part)
    n = half // tk
    each = part // tk

    def body(at_ref, x_ref, v_ref, c_ref, p_ref, xv_ref, cs_ref, *refs):
        vv, (acc, x_sem, v_sem, c_sem) = refs[:VPARTS], refs[VPARTS:]

        def cut(ref, dst, core, k, sem):
            src = ref.at[:, pl.ds(pl.multiple_of(core * half + k * tk, tk), tk)]
            return copy(src, dst.at[:, at_block(k, tk)], sem.at[k])

        def x_copy(k):
            return cut(x_ref, xv_ref, at_ref[0], k, x_sem)

        def c_copy(k):
            return cut(c_ref, cs_ref, 1 - at_ref[0], k, c_sem)

        def v_copy(k, i, j):
            return copy(v_ref.at[at_block(k, tk), :], vv[i].at[at_block(j, tk), :], v_sem.at[k])

        for k in range(n):
            x_copy(k).start()
            v_copy(k, k // each, k % each).start()
        for k in range(n):
            c_copy(k).start()
        acc[...] = jnp.zeros_like(acc)
        for i in range(VPARTS):

            @pl.loop(0, each)
            def _(j):
                k = i * each + j
                x_copy(k).wait()
                v_copy(k, i, j).wait()
                acc[...] += jnp.dot(xv_ref[:, at_block(k, tk)], vv[i][at_block(j, tk), :], preferred_element_type=F32)

        p_ref[...] = acc[...].astype(BF)
        for k in range(n):
            c_copy(k).wait()

    return call(
        body,
        "project_own",
        [(x, "h"), (v, "h"), (c, "h")],
        [((rows, rank), BF, "v"), ((rows, half), BF, "v"), ((rows, half), BF, "v")] + [((part, rank), BF, "v")] * VPARTS,
        [pltpu.VMEM((rows, rank), F32)] + [dma(n)] * 3,
        flops=2 * rows * half * rank,
        mib=8,
        after=after,
    )


def write_halves(at_ref, total, outs):
    if len(outs) == 1:
        outs[0][...] = total(slice(None))
        return
    each = outs[0].shape[0]
    bit = at_ref[1] & 1
    for i, o_ref in ((bit, outs[0]), (1 - bit, outs[1])):
        o_ref[...] = total(at_block(i, each)).astype(BF)


def halves_of(rows, rank, direct):
    return [((rows // 2, rank), BF, "v")] * 2 if direct else [((rows, rank), F32, "v")]


def project_other(x_o, vs, theirs, direct):
    rows, half = x_o.shape
    part, rank = vs[0].shape
    tk = min(1024, part)
    each = part // tk

    def body(at_ref, x_ref, t_ref, *refs):
        vv, outs, acc = refs[:VPARTS], refs[VPARTS:-1], refs[-1]
        acc[...] = t_ref[...].astype(F32)
        for i in range(VPARTS):

            @pl.loop(0, each)
            def _(j):
                acc[...] += jnp.dot(x_ref[:, at_block(i * each + j, tk)], vv[i][at_block(j, tk), :], preferred_element_type=F32)

        write_halves(at_ref, lambda here: acc[here, :], outs)

    return call(
        body,
        "project_other",
        [(x_o, "v"), (theirs, "v")] + [(a, "v") for a in vs],
        halves_of(rows, rank, direct),
        [pltpu.VMEM((rows, rank), F32)],
        flops=2 * rows * half * rank,
        mib=8,
    )


def fetch_first(c, u, after=()):
    rows, part = c.shape[0], u.shape[0] // 2

    def body(at_ref, c_ref, cv_ref, c_sem, fetch):
        first_c = copy(c_ref.at[:, at_block(2 * at_ref[0], part)], cv_ref, c_sem.at[0])
        fetch()
        first_c.start()
        first_c.wait()

    return call(
        body, "fetch_first", [(c, "h")], [((rows, part), BF, "v")], [dma(1)], ahead=[(u, 0, part // 2)], after=after, us=2.8
    )


def hidden(c, x):
    return (c.astype(F32) * x.astype(F32)).astype(BF)


def back_project(s, x, x_o, c, c_o, u, u_first, so_far, c_all=None, after=()):
    rows, (half, rank) = x.shape[0], u.shape
    part = half // 2
    tk = u_first.shape[0]
    n = part // tk
    first = so_far is None
    n_outs = 2 if first else 3

    def body(at_ref, x_ref, xo_ref, c_ref, co_ref, u_ref, uf_ref, *refs, fetch=nothing):
        if first:
            all_ref, acc_ref, b_ref, next_ref, uv, h, u_sem, c_sem = refs
            src = all_ref.at[:, pl.ds(pl.multiple_of(at_ref[0] * half + part, part), part)]
            next_c = copy(src, next_ref, c_sem.at[0])
        else:
            so_ref, own_ref, oth_ref, b_ref, uv, h, u_sem = refs

        def u_copy(k):
            return copy(u_ref.at[pl.ds(s * part + k * tk, tk), :], uv.at[k - 1], u_sem.at[k - 1])

        for k in range(1, n):
            u_copy(k).start()
        if first:
            next_c.start()
        fetch()
        for k in range(n):
            here = pl.ds(k * tk, tk)
            there = pl.ds(s * part + k * tk, tk)
            own = hidden(c_ref[:, here], x_ref[:, there])
            oth = hidden(co_ref[:, there], xo_ref[:, there])
            h[k, :rows, :] = own
            h[k, rows:, :] = oth
            b_ref[:, here] = jnp.sum(own.astype(F32), axis=0, keepdims=True) + jnp.sum(oth.astype(F32), axis=0, keepdims=True)
        for k in range(1, n):
            u_copy(k).wait()

        @pl.loop(0, 2)
        def _(i):
            at_rows = at_block(i, rows)
            total = None if first else so_ref[at_rows, :]
            for k in range(n):
                term = jnp.dot(h[k, at_rows, :], uv[k - 1] if k else uf_ref[...], preferred_element_type=F32)
                total = term if total is None else total + term
            if first:
                acc_ref[at_rows, :] = total
            else:

                @pl.when(i == 0)
                def _():
                    own_ref[...] = total.astype(BF)

                @pl.when(i == 1)
                def _():
                    oth_ref[...] = total

        if first:
            next_c.wait()

    outs = [((2 * rows, rank), F32, "v")] if first else [((rows, rank), BF, "v"), ((rows, rank), F32, "v")]
    outs += [((1, part), F32, "v")] + ([((rows, part), BF, "v")] if first else [])
    return call(
        body,
        "back_project",
        [(x, "v"), (x_o, "v"), (c, "v"), (c_o, "v"), (u, "h"), (u_first, "v"), (c_all, "h") if first else (so_far, "v")],
        outs,
        [pltpu.VMEM((max(1, n - 1), tk, rank), BF), pltpu.VMEM((n, 2 * rows, tk), BF), dma(max(1, n - 1))]
        + ([dma(1)] if first else []),
        flops=2 * rows * half * rank,
        mib=16,
        after=after,
        ahead=[(u, part, tk)] if first else [],
    )


def turn_x(x, x_o, after=()):
    rows, half = x.shape
    tw = min(512, half)
    n = half // tw

    def body(at_ref, x_ref, xo_ref, o_ref, stage, sems):
        def out(k):
            slot = lax.rem(k, 2)
            return copy(stage.at[slot], o_ref.at[at_block(k, tw), :], sems.at[slot])

        @pl.loop(0, n)
        def _(k):
            here = at_block(k, tw)
            slot = lax.rem(k, 2)

            @pl.when(k >= 2)
            def _():
                out(k).wait()

            stage[slot, :, :rows] = x_ref[:, here].T
            stage[slot, :, rows:] = xo_ref[:, here].T
            out(k).start()

        for k in range(max(0, n - 2), n):
            out(k).wait()

    return call(
        body,
        "turn_x",
        [(x, "v"), (x_o, "v")],
        [((half, 2 * rows), BF, "h")],
        [pltpu.VMEM((2, tw, 2 * rows), BF), dma(2)],
        after=after,
        us=3.6,
    )[0]


def turn_hidden(s, x, x_o, c, c_o, after=(), carry=()):
    rows, half = x.shape
    part = half // 2
    tw = min(512, part)

    def body(at_ref, x_ref, xo_ref, c_ref, co_ref, o_ref):
        @pl.loop(0, part // tw)
        def _(k):
            here = at_block(k, tw)
            there = pl.ds(pl.multiple_of(s * part + k * tw, tw), tw)
            o_ref[here, :rows] = hidden(c_ref[:, here], x_ref[:, there]).T
            o_ref[here, rows:] = hidden(co_ref[:, there], xo_ref[:, there]).T

    return call(
        body,
        "turn_hidden",
        [(a, "v") for a in (x, x_o, c, c_o)],
        [((part, 2 * rows), BF, "v")],
        mib=6,
        after=after,
        us=1.8,
        carry=carry,
    )


def fill(at_ref, both, refs):
    if len(refs) == 2:
        rows = refs[0].shape[0]
        both[:rows, :] = refs[0][...]
        both[rows:, :] = refs[1][...]
        return
    each = refs[0].shape[0]
    bit = at_ref[1] & 1
    for i, (keep, other) in enumerate((refs[:2], refs[2:])):
        both[at_block(2 * i + bit, each), :] = keep[...]
        both[at_block(2 * i + 1 - bit, each), :] = other[...]


def factor_grad(name, s, half, turned, p, so_far, placed=None, after=(), ahead=()):
    rows2, rank = turned.shape[1], p[0].shape[1]
    part = half // 2
    tw = min(512, part // 2)
    n = part // tw
    far = turned.shape[0] == half
    np_ = len(p)
    recv, full = placed or ((), None)
    nr = len(recv)
    ins = [(turned, "h" if far else "v")] + [(a, "v") for a in p]
    aliases = {}
    if so_far is not None:
        aliases[len(ins)] = 0
        ins.append((so_far, "h"))
    if placed:
        ins += [(a, "v") for a in recv]
        aliases[len(ins)] = 1
        ins.append((full, "h"))

    def body(at_ref, t_ref, *refs, fetch=nothing):
        p_refs, refs = refs[:np_], refs[np_ + (so_far is not None) :]
        r_refs, refs = refs[:nr], refs[nr + (nr > 0) :]
        o_ref, refs = refs[0], refs[1:]
        if nr:
            f_ref, refs = refs[0], refs[1:]
        stage, both, sems, put_sem, *refs = refs

        def left_copy(k):
            src = t_ref.at[pl.ds(pl.multiple_of(s * part + k * tw, tw), tw), :]
            return copy(src, refs[0].at[at_block(k, tw), :], refs[1].at[k])

        def put(i):
            w = recv[i].shape[1]
            there = pl.ds(pl.multiple_of((1 - at_ref[0]) * half + i * w, w), w)
            return copy(r_refs[i], f_ref.at[:, there], put_sem.at[i])

        def out(k, slot):
            there = pl.ds(pl.multiple_of(s * part + k * tw, tw), tw)
            return copy(stage.at[slot], o_ref.at[there, :], sems.at[slot])

        if far:
            for k in range(n):
                left_copy(k).start()
        for i in range(nr):
            put(i).start()
        fetch()
        fill(at_ref, both, p_refs)

        @pl.loop(0, n // 2)
        def _(kk):
            if far:
                left_copy(2 * kk).wait()
                left_copy(2 * kk + 1).wait()

            @pl.when(kk >= 1)
            def _():
                out(2 * kk - 2, 0).wait()
                out(2 * kk - 1, 1).wait()

            for i in range(2):
                k = 2 * kk + i
                left = refs[0][at_block(k, tw), :] if far else t_ref[at_block(k, tw), :]
                stage[i] = jnp.dot(left, both[...], preferred_element_type=F32).astype(BF)
                out(k, i).start()

        for i in range(2):
            out(n - 2 + i, i).wait()
        for i in range(nr):
            put(i).wait()

    outs = [((half, rank), BF, "h")] + ([(full.shape, BF, "h")] if placed else [])
    return call(
        body,
        name,
        ins,
        outs,
        [pltpu.VMEM((2, tw, rank), BF), pltpu.VMEM((rows2, rank), BF), dma(2), dma(max(1, nr))]
        + ([pltpu.VMEM((part, rows2), BF), dma(n)] if far else []),
        flops=rows2 * half * rank,
        aliases=aliases,
        mib=16 if far else 12,
        after=after,
        ahead=ahead,
    )


def expand(s, u, u_first, p, after=(), ahead=()):
    half, rank = u.shape
    rows2 = sum(a.shape[0] for a in p)
    part = half // 2
    tw = u_first.shape[0]
    n = part // tw

    def body(at_ref, u_ref, uf_ref, *refs, fetch=nothing):
        o_ref, uv, both, u_sem = refs[len(p) :]

        def u_copy(k):
            src = u_ref.at[pl.ds(pl.multiple_of(s * part + k * tw, tw), tw), :]
            return copy(src, uv.at[k - 1], u_sem.at[k - 1])

        for k in range(1, n):
            u_copy(k).start()
        fetch()
        fill(at_ref, both, refs[: len(p)])
        o_ref[:, :tw] = lax.dot_general(both[...], uf_ref[...], NT, preferred_element_type=F32)

        @pl.loop(1, n)
        def _(k):
            u_copy(k).wait()
            o_ref[:, at_block(k, tw)] = lax.dot_general(both[...], uv[k - 1], NT, preferred_element_type=F32)

    return call(
        body,
        "expand",
        [(u, "h"), (u_first, "v")] + [(a, "v") for a in p],
        [((rows2, part), F32, "v")],
        [pltpu.VMEM((max(1, n - 1), tw, rank), BF), pltpu.VMEM((rows2, rank), BF), dma(max(1, n - 1))],
        flops=rows2 * half * rank,
        mib=11,
        after=after,
        ahead=ahead,
    )


def input_grad(s, c, c_o, ex, v, v_first, bias, g, so_far, width, after=(), ahead=()):
    rows, half = c_o.shape
    rank = v.shape[1]
    part = half // 2
    tw = v_first.shape[0]
    n = part // tw
    slots = max(1, min(2, n - 1))
    ng = len(g)

    def body(at_ref, c_ref, co_ref, ex_ref, v_ref, vf_ref, b_ref, *refs, fetch=nothing):
        g_refs, refs = refs[:ng], refs[ng + (so_far is not None) :]
        own_ref, oth_ref, stage, vv, both, sems, v_sem = refs

        def v_copy(k):
            src = v_ref.at[pl.ds(pl.multiple_of(s * part + k * tw, tw), tw), :]
            slot = lax.rem(k - 1, slots)
            return copy(src, vv.at[slot], v_sem.at[slot])

        def columns(k):
            return pl.ds(pl.multiple_of(at_ref[0] * half + s * part + k * tw, tw), tw)

        def out(k):
            slot = lax.rem(k, 2)
            return copy(stage.at[slot], own_ref.at[:, columns(k)], sems.at[slot])

        def block(k, v_block):
            here = at_block(k, tw)
            there = pl.ds(pl.multiple_of(s * part + k * tw, tw), tw)
            bk = lax.dot_general(both[...], v_block, NT, preferred_element_type=F32)
            b = b_ref[:, columns(k)].astype(F32)
            cf, cof = c_ref[:, here].astype(F32), co_ref[:, there].astype(F32)
            stage[lax.rem(k, 2)] = (cf * (ex_ref[:rows, here] + b) + cf + bk[:rows]).astype(BF)
            oth_ref[:, here] = (cof * (ex_ref[rows:, here] + b) + cof + bk[rows:]).astype(BF)
            out(k).start()

        for k in range(1, min(n, slots + 1)):
            v_copy(k).start()
        fetch()
        fill(at_ref, both, g_refs)
        block(0, vf_ref[...])

        @pl.loop(1, n)
        def _(k):
            v_copy(k).wait()

            @pl.when(k >= 2)
            def _():
                out(k - 2).wait()

            block(k, vv[lax.rem(k - 1, slots)])

            @pl.when(k + slots < n)
            def _():
                v_copy(k + slots).start()

        for k in range(max(0, n - 2), n):
            out(k).wait()

    ins = [(c, "v"), (c_o, "v"), (ex, "v"), (v, "h"), (v_first, "v"), (bias, "v")] + [(a, "v") for a in g]
    aliases = {}
    if so_far is not None:
        aliases = {len(ins): 0}
        ins.append((so_far, "h"))
    return call(
        body,
        "input_grad",
        ins,
        [((rows, width), BF, "h"), ((rows, part), BF, "v")],
        [
            pltpu.VMEM((2, rows, tw), BF),
            pltpu.VMEM((slots, tw, rank), BF),
            pltpu.VMEM((2 * rows, rank), BF),
            dma(2),
            dma(slots),
        ],
        flops=2 * rows * half * rank,
        aliases=aliases,
        mib=14,
        after=after,
        ahead=ahead,
    )


def plus(a, b):
    return a.astype(F32) + b.astype(F32)


def pair_halves(a, b, direct, after=()):
    rows, rank = a.shape

    def body(at_ref, a_ref, b_ref, *outs):
        write_halves(at_ref, lambda here: plus(a_ref[here, :], b_ref[here, :]), outs)

    return call(body, "pair_halves", [(a, "v"), (b, "v")], halves_of(rows, rank, direct), after=after)


def pieces_of(a, b, m, after=(), carry=()):
    rows, rank = a.shape
    each = rows // m

    def body(at_ref, a_ref, b_ref, *outs):
        for d in range(m):
            here = at_block((at_ref[1] >> 1) ^ d, each)
            outs[d][...] = plus(a_ref[here, :], b_ref[here, :]).astype(BF)

    return call(body, "pieces_of", [(a, "v"), (b, "v")], [((each, rank), BF, "v")] * m, after=after, carry=carry)


def add_pieces(parts, after=(), carry=()):
    def body(at_ref, *refs):
        total = refs[0][...].astype(F32)
        for r in refs[1:-1]:
            total += r[...].astype(F32)
        refs[-1][...] = total.astype(BF)

    return call(body, "add_pieces", [(a, "v") for a in parts], [(parts[0].shape, BF, "v")], after=after, carry=carry)


def join_pieces(parts, after=()):
    m = len(parts)
    each, rank = parts[0].shape

    def body(at_ref, *refs):
        for d in range(m):
            refs[-1][at_block((at_ref[1] >> 1) ^ d, each), :] = refs[d][...]

    return call(body, "join_pieces", [(a, "v") for a in parts], [((m * each, rank), BF, "v")], after=after)[0]


def hold(a, after):
    def body(at_ref, a_ref, o_ref):
        pass

    return call(body, "hold", [(a, "v")], [(a.shape, a.dtype, "v")], aliases={0: 0}, after=after, mib=9)[0]


def solution(mesh):
    n = mesh.shape["col"]
    m = n // 2
    swap = [(0, 1), (1, 0)]

    def trade(a):
        return lax.ppermute(a, "batch", swap)

    def to(a, d):
        return lax.ppermute(a, "col", [(i, i ^ d) for i in range(n)])

    def spread(parts):
        return [parts[0]] + [to(parts[d], 2 * d) for d in range(1, m)]

    def local(x, c, u, v, bias):
        half, width = u.shape[0], x.shape[1]
        direct = x.shape[0] % (16 * n) == 0 and n & (n - 1) == 0 and n > 2

        def plain(total):
            total = lax.psum(total, "col").astype(BF)
            return [trade(total), total]

        part = half // 2
        tw = min(1024, part)
        x_s = cut_half(x, half)
        x_o = trade(x_s)
        own, x_own, c_s, *v_in = project_own(x, v, c, [x_s])
        theirs = trade(own)
        c_o = trade(hold(c_s, [theirs]))
        sums = project_other(x_o, v_in, theirs, direct)
        c0, u0 = fetch_first(c, u, [sums[0]])
        acc, b0, c1, u1 = back_project(0, x_own, x_o, c0, c_o, u, u0, None, c)
        if direct:
            parts = pieces_of(sums[0], to(sums[1], 1), m, [acc])
            own_g, mine_g, b1 = back_project(1, x_own, x_o, c1, c_o, u, u1, acc, after=[parts[0]])
            total, own_g = add_pieces(spread(parts), carry=[own_g])
            (h_t0,) = turn_hidden(0, x_own, x_o, c0, c_o, [total])
            sums_g = pair_halves(mine_g, trade(own_g), direct, [h_t0])
            (h_t1,) = turn_hidden(1, x_own, x_o, c1, c_o, [sums_g[0]])
            half_p = join_pieces(spread([total] * m), [h_t1])
            other_p = to(half_p, 1)
            x_t = turn_x(x_own, x_o, [half_p])
            other_p = hold(other_p, [(x_t, "h")])
            p = [trade(half_p), trade(other_p), half_p, other_p]
            (grad_u,) = factor_grad("u_grad", 0, half, h_t0, p, None, after=[(x_t, "h")])
            parts_g = pieces_of(sums_g[0], to(sums_g[1], 1), m, [(grad_u, "h")])
            grad_u, u0 = factor_grad("u_grad", 1, half, h_t1, p, grad_u, after=[parts_g[0]], ahead=[(u, 0, tw)])
            (total_g,) = add_pieces(spread(parts_g), [(grad_u, "h")])
            ex0, u1 = expand(0, u, u0, p, [total_g], [(u, part, tw)])
            half_g = join_pieces(spread([total_g] * m), [ex0])
            other_g = to(half_g, 1)
            ex1, v0 = expand(1, u, u1, p, [half_g], [(v, 0, tw)])
            other_g = hold(other_g, [ex1])
            g = [trade(half_g), trade(other_g), half_g, other_g]
        else:
            own_g, mine_g, b1 = back_project(1, x_own, x_o, c1, c_o, u, u1, acc)
            (sums_g,) = pair_halves(mine_g, trade(own_g), direct)
            p, g = plain(sums[0]), plain(sums_g)
            x_t = turn_x(x_own, x_o)
            (h_t0,) = turn_hidden(0, x_own, x_o, c0, c_o)
            (h_t1,) = turn_hidden(1, x_own, x_o, c1, c_o)
            (grad_u,) = factor_grad("u_grad", 0, half, h_t0, p, None)
            grad_u, u0 = factor_grad("u_grad", 1, half, h_t1, p, grad_u, ahead=[(u, 0, tw)])
            ex0, u1 = expand(0, u, u0, p, ahead=[(u, part, tw)])
            ex1, v0 = expand(1, u, u1, p, ahead=[(v, 0, tw)])
        bias = bias[None, :]
        out, oth0, v1 = input_grad(0, c0, c_o, ex0, v, v0, bias, g, None, width, [ex1], [(v, part, tw)])
        out, oth1 = input_grad(1, c1, c_o, ex1, v, v1, bias, g, out, width)
        back = [trade(oth0), trade(oth1)]
        (grad_v,) = factor_grad("v_grad", 0, half, x_t, g, None, after=[oth1])
        grad_v, out = factor_grad("v_grad", 1, half, x_t, g, grad_v, (back, out))
        return out, grad_u, grad_v, jnp.concatenate([b0[0], b1[0]])

    return jax.shard_map(
        local,
        mesh=mesh,
        in_specs=(
            P(("group", "batch"), "col"),
            P(("group", "batch"), "col"),
            P(("col", "batch"), None),
            P(("col", "batch"), None),
            P("col"),
        ),
        out_specs=(
            P(("group", "batch"), "col"),
            P(("group", "col", "batch"), None),
            P(("group", "col", "batch"), None),
            P(("group", "col", "batch")),
        ),
        check_vma=False,
    )
```

```python
import jax
import jax.numpy as jnp
from jax import lax
from jax.experimental import pallas as pl
from jax.experimental.pallas import tpu as pltpu
from jax.sharding import PartitionSpec as P

BF, F32 = jnp.bfloat16, jnp.float32
MIB = 1 << 20
NT = (((1,), (1,)), ((), ()))


class Place:
    def __getitem__(self, i):
        return lax.axis_index(("batch", "col")[i])


def call(body, name, ins, outs, scratch=(), flops=0, aliases=None, mib=4, after=(), us=0.3, carry=(), ahead=()):
    specs = {"v": pl.BlockSpec(memory_space=pltpu.VMEM), "h": pl.BlockSpec(memory_space=pl.ANY)}
    spaces = {"v": pltpu.VMEM, "h": pltpu.HBM}
    n_ins, n_ahead, n_outs, n_after = len(ins), len(ahead), len(outs), len(after)
    aliases = dict(aliases or {})
    aliases.update({n_ins + n_ahead + i: n_outs + n_ahead + i for i in range(len(carry))})
    ins = list(ins) + [(a, "h") for a, _, _ in ahead] + [(a, "v") for a in carry]
    ins += [a if isinstance(a, tuple) else (a, "v") for a in after]
    outs = list(outs) + [((rows, a.shape[1]), a.dtype, "v") for a, _, rows in ahead] + [(a.shape, a.dtype, "v") for a in carry]
    args = [pltpu.with_memory_space_constraint(a, spaces[w]) for a, w in ins]

    def whole(*refs):
        first = len(ins)
        sems = refs[-1] if n_ahead else None
        scratch_refs = refs[first + len(outs) : len(refs) - (n_ahead > 0)]
        fetches = [
            pltpu.make_async_copy(refs[n_ins + i].at[pl.ds(row, rows), :], refs[first + n_outs + i], sems.at[i])
            for i, (_, row, rows) in enumerate(ahead)
        ]
        body(Place(), *refs[:n_ins], *refs[first : first + n_outs], *scratch_refs, fetch=lambda: [f.start() for f in fetches])
        for f in fetches:
            f.wait()

    return pl.pallas_call(
        whole if n_ahead else lambda *refs: body(Place(), *refs[:n_ins], *refs[len(ins) : len(ins) + n_outs], *refs[len(ins) + len(outs) :]),
        out_shape=tuple(spaces[w](dims, dtype) for dims, dtype, w in outs),
        in_specs=[specs[w] for _, w in ins],
        out_specs=tuple(specs[w] for _, _, w in outs),
        scratch_shapes=list(scratch) + ([pltpu.SemaphoreType.DMA((n_ahead,))] if n_ahead else []),
        input_output_aliases=aliases,
        compiler_params=pltpu.CompilerParams(vmem_limit_bytes=mib * MIB),
        cost_estimate=pl.CostEstimate(flops=int(1.7 * flops + us * 1.15e9), bytes_accessed=0, transcendentals=0),
        name=name,
    )(*args)


def nothing():
    pass


def at_block(i, size):
    return pl.ds(pl.multiple_of(i * size, size), size)


def dma(n):
    return pltpu.SemaphoreType.DMA((n,))


def copy(src, dst, sem):
    return pltpu.make_async_copy(src, dst, sem)


def cut_half(x, half, after=()):
    rows = x.shape[0]
    n = 8
    step = rows // n

    def body(at_ref, x_ref, o_ref, sems):
        def cut(i):
            here = pl.ds(i * step, step)
            return copy(x_ref.at[here, at_block(1 - at_ref[0], half)], o_ref.at[here, :], sems.at[i])

        for i in range(n):
            cut(i).start()
        for i in range(n):
            cut(i).wait()

    return call(body, "cut_half", [(x, "h")], [((rows, half), BF, "v")], [dma(n)], us=2.2, after=after)[0]


VPARTS = 4


def project_own(x, v, c, after=()):
    rows, (half, rank) = x.shape[0], v.shape
    part = half // VPARTS
    tk = min(1024, part)
    n = half // tk
    each = part // tk

    def body(at_ref, x_ref, v_ref, c_ref, p_ref, xv_ref, cs_ref, *refs):
        vv, (acc, x_sem, v_sem, c_sem) = refs[:VPARTS], refs[VPARTS:]

        def cut(ref, dst, core, k, sem):
            src = ref.at[:, pl.ds(pl.multiple_of(core * half + k * tk, tk), tk)]
            return copy(src, dst.at[:, at_block(k, tk)], sem.at[k])

        def x_copy(k):
            return cut(x_ref, xv_ref, at_ref[0], k, x_sem)

        def c_copy(k):
            return cut(c_ref, cs_ref, 1 - at_ref[0], k, c_sem)

        def v_copy(k, i, j):
            return copy(v_ref.at[at_block(k, tk), :], vv[i].at[at_block(j, tk), :], v_sem.at[k])

        for k in range(n):
            x_copy(k).start()
            v_copy(k, k // each, k % each).start()
        for k in range(n):
            c_copy(k).start()
        acc[...] = jnp.zeros_like(acc)
        for i in range(VPARTS):

            @pl.loop(0, each)
            def _(j):
                k = i * each + j
                x_copy(k).wait()
                v_copy(k, i, j).wait()
                acc[...] += jnp.dot(xv_ref[:, at_block(k, tk)], vv[i][at_block(j, tk), :], preferred_element_type=F32)

        p_ref[...] = acc[...].astype(BF)
        for k in range(n):
            c_copy(k).wait()

    return call(
        body,
        "project_own",
        [(x, "h"), (v, "h"), (c, "h")],
        [((rows, rank), BF, "v"), ((rows, half), BF, "v"), ((rows, half), BF, "v")] + [((part, rank), BF, "v")] * VPARTS,
        [pltpu.VMEM((rows, rank), F32)] + [dma(n)] * 3,
        flops=2 * rows * half * rank,
        mib=8,
        after=after,
    )


def write_halves(at_ref, total, outs):
    if len(outs) == 1:
        outs[0][...] = total(slice(None))
        return
    each = outs[0].shape[0]
    bit = at_ref[1] & 1
    for i, o_ref in ((bit, outs[0]), (1 - bit, outs[1])):
        o_ref[...] = total(at_block(i, each)).astype(BF)


def halves_of(rows, rank, direct):
    return [((rows // 2, rank), BF, "v")] * 2 if direct else [((rows, rank), F32, "v")]


def project_other(x_o, vs, theirs, direct):
    rows, half = x_o.shape
    tk, rank = vs[0].shape

    def body(at_ref, x_ref, t_ref, *refs):
        vv, outs, acc = refs[:VPARTS], refs[VPARTS:-1], refs[-1]
        for k in range(VPARTS):
            part = jnp.dot(x_ref[:, k * tk : (k + 1) * tk], vv[k][...], preferred_element_type=F32)
            acc[...] = part + (acc[...] if k else t_ref[...].astype(F32))
        write_halves(at_ref, lambda here: acc[here, :], outs)

    return call(
        body,
        "project_other",
        [(x_o, "v"), (theirs, "v")] + [(a, "v") for a in vs],
        halves_of(rows, rank, direct),
        [pltpu.VMEM((rows, rank), F32)],
        flops=2 * rows * half * rank,
        mib=6,
    )


def fetch_first(c, u, after=()):
    rows, part = c.shape[0], u.shape[0] // 2

    def body(at_ref, c_ref, cv_ref, c_sem, fetch):
        first_c = copy(c_ref.at[:, at_block(2 * at_ref[0], part)], cv_ref, c_sem.at[0])
        fetch()
        first_c.start()
        first_c.wait()

    return call(
        body, "fetch_first", [(c, "h")], [((rows, part), BF, "v")], [dma(1)], ahead=[(u, 0, part // 2)], after=after, us=2.8
    )


def hidden(c, x):
    return (c.astype(F32) * x.astype(F32)).astype(BF)


def back_project(s, x, x_o, c, c_o, u, u_first, so_far, c_all=None, after=()):
    rows, (half, rank) = x.shape[0], u.shape
    part = half // 2
    tk = u_first.shape[0]
    n = part // tk
    first = so_far is None
    n_outs = 2 if first else 3

    def body(at_ref, x_ref, xo_ref, c_ref, co_ref, u_ref, uf_ref, *refs, fetch=nothing):
        if first:
            all_ref, acc_ref, b_ref, next_ref, uv, h, u_sem, c_sem = refs
            src = all_ref.at[:, pl.ds(pl.multiple_of(at_ref[0] * half + part, part), part)]
            next_c = copy(src, next_ref, c_sem.at[0])
        else:
            so_ref, own_ref, oth_ref, b_ref, uv, h, u_sem = refs

        def u_copy(k):
            return copy(u_ref.at[pl.ds(s * part + k * tk, tk), :], uv.at[k - 1], u_sem.at[k - 1])

        for k in range(1, n):
            u_copy(k).start()
        if first:
            next_c.start()
        fetch()
        for k in range(n):
            here = pl.ds(k * tk, tk)
            there = pl.ds(s * part + k * tk, tk)
            own = hidden(c_ref[:, here], x_ref[:, there])
            oth = hidden(co_ref[:, there], xo_ref[:, there])
            h[k, :rows, :] = own
            h[k, rows:, :] = oth
            b_ref[:, here] = jnp.sum(own.astype(F32), axis=0, keepdims=True) + jnp.sum(oth.astype(F32), axis=0, keepdims=True)
        for k in range(1, n):
            u_copy(k).wait()

        @pl.loop(0, 2)
        def _(i):
            at_rows = at_block(i, rows)
            total = None if first else so_ref[at_rows, :]
            for k in range(n):
                term = jnp.dot(h[k, at_rows, :], uv[k - 1] if k else uf_ref[...], preferred_element_type=F32)
                total = term if total is None else total + term
            if first:
                acc_ref[at_rows, :] = total
            else:

                @pl.when(i == 0)
                def _():
                    own_ref[...] = total.astype(BF)

                @pl.when(i == 1)
                def _():
                    oth_ref[...] = total

        if first:
            next_c.wait()

    outs = [((2 * rows, rank), F32, "v")] if first else [((rows, rank), BF, "v"), ((rows, rank), F32, "v")]
    outs += [((1, part), F32, "v")] + ([((rows, part), BF, "v")] if first else [])
    return call(
        body,
        "back_project",
        [(x, "v"), (x_o, "v"), (c, "v"), (c_o, "v"), (u, "h"), (u_first, "v"), (c_all, "h") if first else (so_far, "v")],
        outs,
        [pltpu.VMEM((max(1, n - 1), tk, rank), BF), pltpu.VMEM((n, 2 * rows, tk), BF), dma(max(1, n - 1))]
        + ([dma(1)] if first else []),
        flops=2 * rows * half * rank,
        mib=16,
        after=after,
        ahead=[(u, part, tk)] if first else [],
    )


def turn_x(x, x_o, after=()):
    rows, half = x.shape
    tw = min(512, half)
    n = half // tw

    def body(at_ref, x_ref, xo_ref, o_ref, stage, sems):
        def out(k):
            here = at_block(k, tw)
            return copy(stage.at[here, :], o_ref.at[here, :], sems.at[k])

        @pl.loop(0, n)
        def _(k):
            here = at_block(k, tw)
            stage[here, :rows] = x_ref[:, here].T
            stage[here, rows:] = xo_ref[:, here].T
            out(k).start()

        @pl.loop(0, n)
        def _(k):
            out(k).wait()

    return call(
        body,
        "turn_x",
        [(x, "v"), (x_o, "v")],
        [((half, 2 * rows), BF, "h")],
        [pltpu.VMEM((half, 2 * rows), BF), dma(n)],
        after=after,
        us=3.6,
        mib=12,
    )[0]


def turn_hidden(s, x, x_o, c, c_o, after=(), carry=()):
    rows, half = x.shape
    part = half // 2
    tw = min(512, part)

    def body(at_ref, x_ref, xo_ref, c_ref, co_ref, o_ref):
        @pl.loop(0, part // tw)
        def _(k):
            here = at_block(k, tw)
            there = pl.ds(pl.multiple_of(s * part + k * tw, tw), tw)
            o_ref[here, :rows] = hidden(c_ref[:, here], x_ref[:, there]).T
            o_ref[here, rows:] = hidden(co_ref[:, there], xo_ref[:, there]).T

    return call(
        body,
        "turn_hidden",
        [(a, "v") for a in (x, x_o, c, c_o)],
        [((part, 2 * rows), BF, "v")],
        mib=6,
        after=after,
        us=1.8,
        carry=carry,
    )


def fill(at_ref, both, refs):
    if len(refs) == 2:
        rows = refs[0].shape[0]
        both[:rows, :] = refs[0][...]
        both[rows:, :] = refs[1][...]
        return
    each = refs[0].shape[0]
    bit = at_ref[1] & 1
    for i, (keep, other) in enumerate((refs[:2], refs[2:])):
        both[at_block(2 * i + bit, each), :] = keep[...]
        both[at_block(2 * i + 1 - bit, each), :] = other[...]


def factor_grad(name, s, half, turned, p, so_far, placed=None, after=(), ahead=(), work=1):
    rows2, rank = turned.shape[1], p[0].shape[1]
    part = half // 2
    tw = min(512, part // 2)
    n = part // tw
    far = turned.shape[0] == half
    np_ = len(p)
    recv, full = ([placed[0]], placed[1]) if placed else ((), None)
    nr = len(recv)
    ins = [(turned, "h" if far else "v")] + [(a, "v") for a in p]
    aliases = {}
    if so_far is not None:
        aliases[len(ins)] = 0
        ins.append((so_far, "h"))
    if placed:
        ins += [(a, "v") for a in recv]
        aliases[len(ins)] = 1
        ins.append((full, "h"))

    def body(at_ref, t_ref, *refs, fetch=nothing):
        p_refs, refs = refs[:np_], refs[np_ + (so_far is not None) :]
        r_refs, refs = refs[:nr], refs[nr + (nr > 0) :]
        o_ref, refs = refs[0], refs[1:]
        if nr:
            f_ref, refs = refs[0], refs[1:]
        stage, both, sems, put_sem, *refs = refs

        def left_copy(k):
            src = t_ref.at[pl.ds(pl.multiple_of(s * part + k * tw, tw), tw), :]
            return copy(src, refs[0].at[at_block(k, tw), :], refs[1].at[k])

        def put(i):
            w = recv[i].shape[1]
            there = pl.ds(pl.multiple_of((1 - at_ref[0]) * half + s * w, w), w)
            return copy(r_refs[i], f_ref.at[:, there], put_sem.at[i])

        def out(k):
            slot = lax.rem(k, 4)
            there = pl.ds(pl.multiple_of(s * part + k * tw, tw), tw)
            return copy(stage.at[slot], o_ref.at[there, :], sems.at[slot])

        if far:
            for k in range(n):
                left_copy(k).start()
        for i in range(nr):
            put(i).start()
        fetch()
        fill(at_ref, both, p_refs)

        @pl.loop(0, n // 2)
        def _(kk):
            if far:
                left_copy(2 * kk).wait()
                left_copy(2 * kk + 1).wait()

            @pl.when(kk >= 2)
            def _():
                out(2 * kk - 4).wait()
                out(2 * kk - 3).wait()

            for i in range(2):
                k = 2 * kk + i
                left = refs[0][at_block(k, tw), :] if far else t_ref[at_block(k, tw), :]
                stage[lax.rem(k, 4)] = jnp.dot(left, both[...], preferred_element_type=F32).astype(BF)
                out(k).start()

        for k in range(max(0, n - 4), n):
            out(k).wait()
        for i in range(nr):
            put(i).wait()

    outs = [((half, rank), BF, "h")] + ([(full.shape, BF, "h")] if placed else [])
    return call(
        body,
        name,
        ins,
        outs,
        [pltpu.VMEM((4, tw, rank), BF), pltpu.VMEM((rows2, rank), BF), dma(4), dma(max(1, nr))]
        + ([pltpu.VMEM((part, rows2), BF), dma(n)] if far else []),
        flops=work * rows2 * half * rank,
        aliases=aliases,
        mib=18 if far else 12,
        after=after,
        ahead=ahead,
    )


def expand(s, u, u_first, p, after=(), ahead=()):
    half, rank = u.shape
    rows2 = sum(a.shape[0] for a in p)
    part = half // 2
    tw = u_first.shape[0]
    n = part // tw

    def body(at_ref, u_ref, uf_ref, *refs, fetch=nothing):
        o_ref, uv, both, u_sem = refs[len(p) :]

        def u_copy(k):
            src = u_ref.at[pl.ds(pl.multiple_of(s * part + k * tw, tw), tw), :]
            return copy(src, uv.at[k - 1], u_sem.at[k - 1])

        for k in range(1, n):
            u_copy(k).start()
        fetch()
        fill(at_ref, both, refs[: len(p)])
        o_ref[:, :tw] = lax.dot_general(both[...], uf_ref[...], NT, preferred_element_type=F32)

        @pl.loop(1, n)
        def _(k):
            u_copy(k).wait()
            o_ref[:, at_block(k, tw)] = lax.dot_general(both[...], uv[k - 1], NT, preferred_element_type=F32)

    return call(
        body,
        "expand",
        [(u, "h"), (u_first, "v")] + [(a, "v") for a in p],
        [((rows2, part), F32, "v")],
        [pltpu.VMEM((max(1, n - 1), tw, rank), BF), pltpu.VMEM((rows2, rank), BF), dma(max(1, n - 1))],
        flops=rows2 * half * rank,
        mib=11,
        after=after,
        ahead=ahead,
    )


def input_grad(s, c, c_o, ex, v, v_first, bias, g, so_far, width, after=(), ahead=()):
    rows, half = c_o.shape
    rank = v.shape[1]
    part = half // 2
    tw = v_first.shape[0]
    n = part // tw
    slots = max(1, min(2, n - 1))
    ng = len(g)

    def body(at_ref, c_ref, co_ref, ex_ref, v_ref, vf_ref, b_ref, *refs, fetch=nothing):
        g_refs, refs = refs[:ng], refs[ng + (so_far is not None) :]
        own_ref, oth_ref, stage, vv, both, sems, v_sem = refs

        def v_copy(k):
            src = v_ref.at[pl.ds(pl.multiple_of(s * part + k * tw, tw), tw), :]
            slot = lax.rem(k - 1, slots)
            return copy(src, vv.at[slot], v_sem.at[slot])

        def columns(k):
            return pl.ds(pl.multiple_of(at_ref[0] * half + s * part + k * tw, tw), tw)

        def out(k):
            slot = lax.rem(k, 2)
            return copy(stage.at[slot], own_ref.at[:, columns(k)], sems.at[slot])

        def block(k, v_block):
            here = at_block(k, tw)
            there = pl.ds(pl.multiple_of(s * part + k * tw, tw), tw)
            bk = lax.dot_general(both[...], v_block, NT, preferred_element_type=F32)
            b = b_ref[:, columns(k)].astype(F32)
            cf, cof = c_ref[:, here].astype(F32), co_ref[:, there].astype(F32)
            stage[lax.rem(k, 2)] = (cf * (ex_ref[:rows, here] + b) + cf + bk[:rows]).astype(BF)
            oth_ref[:, here] = (cof * (ex_ref[rows:, here] + b) + cof + bk[rows:]).astype(BF)
            out(k).start()

        for k in range(1, min(n, slots + 1)):
            v_copy(k).start()
        fetch()
        fill(at_ref, both, g_refs)
        block(0, vf_ref[...])

        @pl.loop(1, n)
        def _(k):
            v_copy(k).wait()

            @pl.when(k >= 2)
            def _():
                out(k - 2).wait()

            block(k, vv[lax.rem(k - 1, slots)])

            @pl.when(k + slots < n)
            def _():
                v_copy(k + slots).start()

        for k in range(max(0, n - 2), n):
            out(k).wait()

    ins = [(c, "v"), (c_o, "v"), (ex, "v"), (v, "h"), (v_first, "v"), (bias, "v")] + [(a, "v") for a in g]
    aliases = {}
    if so_far is not None:
        aliases = {len(ins): 0}
        ins.append((so_far, "h"))
    return call(
        body,
        "input_grad",
        ins,
        [((rows, width), BF, "h"), ((rows, part), BF, "v")],
        [
            pltpu.VMEM((2, rows, tw), BF),
            pltpu.VMEM((slots, tw, rank), BF),
            pltpu.VMEM((2 * rows, rank), BF),
            dma(2),
            dma(slots),
        ],
        flops=2 * rows * half * rank,
        aliases=aliases,
        mib=14,
        after=after,
        ahead=ahead,
    )


def plus(a, b):
    return a.astype(F32) + b.astype(F32)


def pair_halves(a, b, direct, after=()):
    rows, rank = a.shape

    def body(at_ref, a_ref, b_ref, *outs):
        write_halves(at_ref, lambda here: plus(a_ref[here, :], b_ref[here, :]), outs)

    return call(body, "pair_halves", [(a, "v"), (b, "v")], halves_of(rows, rank, direct), after=after)


def pieces_of(a, b, m, after=(), carry=()):
    rows, rank = a.shape
    each = rows // m

    def body(at_ref, a_ref, b_ref, *outs):
        for d in range(m):
            here = at_block((at_ref[1] >> 1) ^ d, each)
            outs[d][...] = plus(a_ref[here, :], b_ref[here, :]).astype(BF)

    return call(body, "pieces_of", [(a, "v"), (b, "v")], [((each, rank), BF, "v")] * m, after=after, carry=carry)


def add_pieces(parts, after=(), carry=()):
    def body(at_ref, *refs):
        total = refs[0][...].astype(F32)
        for r in refs[1:-1]:
            total += r[...].astype(F32)
        refs[-1][...] = total.astype(BF)

    return call(body, "add_pieces", [(a, "v") for a in parts], [(parts[0].shape, BF, "v")], after=after, carry=carry)


def join_pieces(parts, after=()):
    m = len(parts)
    each, rank = parts[0].shape

    def body(at_ref, *refs):
        for d in range(m):
            refs[-1][at_block((at_ref[1] >> 1) ^ d, each), :] = refs[d][...]

    return call(body, "join_pieces", [(a, "v") for a in parts], [((m * each, rank), BF, "v")], after=after)[0]


def hold(a, after):
    def body(at_ref, a_ref, o_ref):
        pass

    return call(body, "hold", [(a, "v")], [(a.shape, a.dtype, "v")], aliases={0: 0}, after=after, mib=9)[0]


def solution(mesh):
    n = mesh.shape["col"]
    m = n // 2
    swap = [(0, 1), (1, 0)]

    def trade(a):
        return lax.ppermute(a, "batch", swap)

    def to(a, d):
        return lax.ppermute(a, "col", [(i, i ^ d) for i in range(n)])

    def spread(parts):
        return [parts[0]] + [to(parts[d], 2 * d) for d in range(1, m)]

    def local(x, c, u, v, bias):
        half, width = u.shape[0], x.shape[1]
        direct = x.shape[0] % (16 * n) == 0 and n & (n - 1) == 0 and n > 2

        def plain(total):
            total = lax.psum(total, "col").astype(BF)
            return [trade(total), total]

        part = half // 2
        tw = min(1024, part)
        x_s = cut_half(x, half)
        x_o = trade(x_s)
        own, x_own, c_s, *v_in = project_own(x, v, c, [x_s])
        theirs = trade(own)
        c_o = trade(hold(c_s, [theirs]))
        sums = project_other(x_o, v_in, theirs, direct)
        c0, u0 = fetch_first(c, u, [sums[0]])
        acc, b0, c1, u1 = back_project(0, x_own, x_o, c0, c_o, u, u0, None, c)
        if direct:
            parts = pieces_of(sums[0], to(sums[1], 1), m, [acc])
            own_g, mine_g, b1 = back_project(1, x_own, x_o, c1, c_o, u, u1, acc, after=[parts[0]])
            total, own_g = add_pieces(spread(parts), carry=[own_g])
            (h_t0,) = turn_hidden(0, x_own, x_o, c0, c_o, [total])
            sums_g = pair_halves(mine_g, trade(own_g), direct, [h_t0])
            (h_t1,) = turn_hidden(1, x_own, x_o, c1, c_o, [sums_g[0]])
            half_p = join_pieces(spread([total] * m), [h_t1])
            other_p = to(half_p, 1)
            x_t = turn_x(x_own, x_o, [half_p])
            other_p = hold(other_p, [(x_t, "h")])
            p = [trade(half_p), trade(other_p), half_p, other_p]
            (grad_u,) = factor_grad("u_grad", 0, half, h_t0, p, None, after=[(x_t, "h")])
            parts_g = pieces_of(sums_g[0], to(sums_g[1], 1), m, [(grad_u, "h")])
            grad_u, u0 = factor_grad("u_grad", 1, half, h_t1, p, grad_u, after=[parts_g[0]], ahead=[(u, 0, tw)])
            (total_g,) = add_pieces(spread(parts_g), [(grad_u, "h")])
            ex0, u1 = expand(0, u, u0, p, [total_g], [(u, part, tw)])
            half_g = join_pieces(spread([total_g] * m), [ex0])
            other_g = to(half_g, 1)
            ex1, v0 = expand(1, u, u1, p, [half_g], [(v, 0, tw)])
            other_g = hold(other_g, [ex1])
            g = [trade(half_g), trade(other_g), half_g, other_g]
        else:
            own_g, mine_g, b1 = back_project(1, x_own, x_o, c1, c_o, u, u1, acc)
            (sums_g,) = pair_halves(mine_g, trade(own_g), direct)
            p, g = plain(sums[0]), plain(sums_g)
            x_t = turn_x(x_own, x_o)
            (h_t0,) = turn_hidden(0, x_own, x_o, c0, c_o)
            (h_t1,) = turn_hidden(1, x_own, x_o, c1, c_o)
            (grad_u,) = factor_grad("u_grad", 0, half, h_t0, p, None)
            grad_u, u0 = factor_grad("u_grad", 1, half, h_t1, p, grad_u, ahead=[(u, 0, tw)])
            ex0, u1 = expand(0, u, u0, p, ahead=[(u, part, tw)])
            ex1, v0 = expand(1, u, u1, p, ahead=[(v, 0, tw)])
        bias = bias[None, :]
        out, oth0, v1 = input_grad(0, c0, c_o, ex0, v, v0, bias, g, None, width, [ex1], [(v, part, tw)])
        out, oth1 = input_grad(1, c1, c_o, ex1, v, v1, bias, g, out, width)
        back0, back1 = trade(oth0), trade(oth1)
        grad_v, out = factor_grad("v_grad", 0, half, x_t, g, None, (back0, out), work=0)
        grad_v, out = factor_grad("v_grad", 1, half, x_t, g, grad_v, (back1, out))
        return out, grad_u, grad_v, jnp.concatenate([b0[0], b1[0]])

    return jax.shard_map(
        local,
        mesh=mesh,
        in_specs=(
            P(("group", "batch"), "col"),
            P(("group", "batch"), "col"),
            P(("col", "batch"), None),
            P(("col", "batch"), None),
            P("col"),
        ),
        out_specs=(
            P(("group", "batch"), "col"),
            P(("group", "col", "batch"), None),
            P(("group", "col", "batch"), None),
            P(("group", "col", "batch")),
        ),
        check_vma=False,
    )
```

```python
import jax
import jax.numpy as jnp
from jax import lax
from jax.experimental import pallas as pl
from jax.experimental.pallas import tpu as pltpu
from jax.sharding import PartitionSpec as P

BF, F32 = jnp.bfloat16, jnp.float32
MIB = 1 << 20
NT = (((1,), (1,)), ((), ()))


class Place:
    def __getitem__(self, i):
        return lax.axis_index(("batch", "col")[i])


def call(body, name, ins, outs, scratch=(), flops=0, aliases=None, mib=4, after=(), us=0.3, carry=(), ahead=()):
    specs = {"v": pl.BlockSpec(memory_space=pltpu.VMEM), "h": pl.BlockSpec(memory_space=pl.ANY)}
    spaces = {"v": pltpu.VMEM, "h": pltpu.HBM}
    n_ins, n_ahead, n_outs, n_after = len(ins), len(ahead), len(outs), len(after)
    aliases = dict(aliases or {})
    aliases.update({n_ins + n_ahead + i: n_outs + n_ahead + i for i in range(len(carry))})
    ins = list(ins) + [(a, "h") for a, _, _ in ahead] + [(a, "v") for a in carry]
    ins += [a if isinstance(a, tuple) else (a, "v") for a in after]
    outs = list(outs) + [((rows, a.shape[1]), a.dtype, "v") for a, _, rows in ahead] + [(a.shape, a.dtype, "v") for a in carry]
    args = [pltpu.with_memory_space_constraint(a, spaces[w]) for a, w in ins]

    def whole(*refs):
        first = len(ins)
        sems = refs[-1] if n_ahead else None
        scratch_refs = refs[first + len(outs) : len(refs) - (n_ahead > 0)]
        fetches = [
            pltpu.make_async_copy(refs[n_ins + i].at[pl.ds(row, rows), :], refs[first + n_outs + i], sems.at[i])
            for i, (_, row, rows) in enumerate(ahead)
        ]
        body(Place(), *refs[:n_ins], *refs[first : first + n_outs], *scratch_refs, fetch=lambda: [f.start() for f in fetches])
        for f in fetches:
            f.wait()

    return pl.pallas_call(
        whole if n_ahead else lambda *refs: body(Place(), *refs[:n_ins], *refs[len(ins) : len(ins) + n_outs], *refs[len(ins) + len(outs) :]),
        out_shape=tuple(spaces[w](dims, dtype) for dims, dtype, w in outs),
        in_specs=[specs[w] for _, w in ins],
        out_specs=tuple(specs[w] for _, _, w in outs),
        scratch_shapes=list(scratch) + ([pltpu.SemaphoreType.DMA((n_ahead,))] if n_ahead else []),
        input_output_aliases=aliases,
        compiler_params=pltpu.CompilerParams(vmem_limit_bytes=mib * MIB),
        cost_estimate=pl.CostEstimate(flops=int(1.7 * flops + us * 1.15e9), bytes_accessed=0, transcendentals=0),
        name=name,
    )(*args)


def nothing():
    pass


def at_block(i, size):
    return pl.ds(pl.multiple_of(i * size, size), size)


def dma(n):
    return pltpu.SemaphoreType.DMA((n,))


def copy(src, dst, sem):
    return pltpu.make_async_copy(src, dst, sem)


def cut_half(x, half, after=()):
    rows = x.shape[0]
    n = 8
    step = rows // n

    def body(at_ref, x_ref, o_ref, sems):
        def cut(i):
            here = pl.ds(i * step, step)
            return copy(x_ref.at[here, at_block(1 - at_ref[0], half)], o_ref.at[here, :], sems.at[i])

        for i in range(n):
            cut(i).start()
        for i in range(n):
            cut(i).wait()

    return call(body, "cut_half", [(x, "h")], [((rows, half), BF, "v")], [dma(n)], us=2.2, after=after)[0]


VPARTS = 4


def project_own(x, v, c, after=()):
    rows, (half, rank) = x.shape[0], v.shape
    part = half // VPARTS
    tk = min(1024, part)
    n = half // tk
    each = part // tk

    def body(at_ref, x_ref, v_ref, c_ref, p_ref, xv_ref, cs_ref, *refs):
        vv, (acc, x_sem, v_sem, c_sem) = refs[:VPARTS], refs[VPARTS:]

        def cut(ref, dst, core, k, sem):
            src = ref.at[:, pl.ds(pl.multiple_of(core * half + k * tk, tk), tk)]
            return copy(src, dst.at[:, at_block(k, tk)], sem.at[k])

        def x_copy(k):
            return cut(x_ref, xv_ref, at_ref[0], k, x_sem)

        def c_copy(k):
            return cut(c_ref, cs_ref, 1 - at_ref[0], k, c_sem)

        def v_copy(k, i, j):
            return copy(v_ref.at[at_block(k, tk), :], vv[i].at[at_block(j, tk), :], v_sem.at[k])

        for k in range(n):
            x_copy(k).start()
            v_copy(k, k // each, k % each).start()
        for k in range(n):
            c_copy(k).start()
        acc[...] = jnp.zeros_like(acc)
        for i in range(VPARTS):

            @pl.loop(0, each)
            def _(j):
                k = i * each + j
                x_copy(k).wait()
                v_copy(k, i, j).wait()
                acc[...] += jnp.dot(xv_ref[:, at_block(k, tk)], vv[i][at_block(j, tk), :], preferred_element_type=F32)

        p_ref[...] = acc[...].astype(BF)
        for k in range(n):
            c_copy(k).wait()

    return call(
        body,
        "project_own",
        [(x, "h"), (v, "h"), (c, "h")],
        [((rows, rank), BF, "v"), ((rows, half), BF, "v"), ((rows, half), BF, "v")] + [((part, rank), BF, "v")] * VPARTS,
        [pltpu.VMEM((rows, rank), F32)] + [dma(n)] * 3,
        flops=2 * rows * half * rank,
        mib=8,
        after=after,
    )


def write_halves(at_ref, total, outs):
    if len(outs) == 1:
        outs[0][...] = total(slice(None))
        return
    each = outs[0].shape[0]
    bit = at_ref[1] & 1
    for i, o_ref in ((bit, outs[0]), (1 - bit, outs[1])):
        o_ref[...] = total(at_block(i, each)).astype(BF)


def halves_of(rows, rank, direct):
    return [((rows // 2, rank), BF, "v")] * 2 if direct else [((rows, rank), F32, "v")]


def project_other(x_o, vs, theirs, c, u, direct):
    rows, half = x_o.shape
    tk, rank = vs[0].shape
    first = half // 2

    def body(at_ref, x_ref, t_ref, c_ref, *refs, fetch):
        vv, outs, cv_ref, acc, c_sem = refs[:VPARTS], refs[VPARTS:-3], refs[-3], refs[-2], refs[-1]
        first_c = copy(c_ref.at[:, at_block(2 * at_ref[0], first)], cv_ref, c_sem.at[0])
        fetch()
        first_c.start()
        for k in range(VPARTS):
            part = jnp.dot(x_ref[:, k * tk : (k + 1) * tk], vv[k][...], preferred_element_type=F32)
            acc[...] = part + (acc[...] if k else t_ref[...].astype(F32))
        write_halves(at_ref, lambda here: acc[here, :], outs)
        first_c.wait()

    return call(
        body,
        "project_other",
        [(x_o, "v"), (theirs, "v"), (c, "h")] + [(a, "v") for a in vs],
        halves_of(rows, rank, direct) + [((rows, first), BF, "v")],
        [pltpu.VMEM((rows, rank), F32), dma(1)],
        flops=2 * rows * half * rank,
        mib=6,
        ahead=[(u, 0, first // 4)],
    )


def hidden(c, x):
    return (c.astype(F32) * x.astype(F32)).astype(BF)


def back_project(s, x, x_o, c, c_o, u, u_first, so_far, c_all=None, after=()):
    rows, (half, rank) = x.shape[0], u.shape
    part = half // 2
    tk = u_first.shape[0]
    n = part // tk
    first = so_far is None
    n_outs = 2 if first else 3

    def body(at_ref, x_ref, xo_ref, c_ref, co_ref, u_ref, uf_ref, *refs, fetch=nothing):
        if first:
            all_ref, acc_ref, b_ref, next_ref, uv, h, u_sem, c_sem = refs
            src = all_ref.at[:, pl.ds(pl.multiple_of(at_ref[0] * half + part, part), part)]
            next_c = copy(src, next_ref, c_sem.at[0])
        else:
            so_ref, own_ref, oth_ref, b_ref, uv, h, u_sem = refs

        def u_copy(k):
            return copy(u_ref.at[pl.ds(s * part + k * tk, tk), :], uv.at[k - 1], u_sem.at[k - 1])

        for k in range(1, n):
            u_copy(k).start()
        if first:
            next_c.start()
        fetch()
        for k in range(n):
            here = pl.ds(k * tk, tk)
            there = pl.ds(s * part + k * tk, tk)
            own = hidden(c_ref[:, here], x_ref[:, there])
            oth = hidden(co_ref[:, there], xo_ref[:, there])
            h[k, :rows, :] = own
            h[k, rows:, :] = oth
            b_ref[:, here] = jnp.sum(own.astype(F32), axis=0, keepdims=True) + jnp.sum(oth.astype(F32), axis=0, keepdims=True)
        @pl.loop(0, 2)
        def _(i):
            at_rows = at_block(i, rows)
            total = None if first else so_ref[at_rows, :]
            for k in range(n):
                if k:

                    @pl.when(i == 0)
                    def _():
                        u_copy(k).wait()

                term = jnp.dot(h[k, at_rows, :], uv[k - 1] if k else uf_ref[...], preferred_element_type=F32)
                total = term if total is None else total + term
            if first:
                acc_ref[at_rows, :] = total
            else:

                @pl.when(i == 0)
                def _():
                    own_ref[...] = total.astype(BF)

                @pl.when(i == 1)
                def _():
                    oth_ref[...] = total

        if first:
            next_c.wait()

    outs = [((2 * rows, rank), F32, "v")] if first else [((rows, rank), BF, "v"), ((rows, rank), F32, "v")]
    outs += [((1, part), F32, "v")] + ([((rows, part), BF, "v")] if first else [])
    return call(
        body,
        "back_project",
        [(x, "v"), (x_o, "v"), (c, "v"), (c_o, "v"), (u, "h"), (u_first, "v"), (c_all, "h") if first else (so_far, "v")],
        outs,
        [pltpu.VMEM((max(1, n - 1), tk, rank), BF), pltpu.VMEM((n, 2 * rows, tk), BF), dma(max(1, n - 1))]
        + ([dma(1)] if first else []),
        flops=2 * rows * half * rank,
        mib=15,
        after=after,
        ahead=[(u, part, tk)] if first else [],
    )


def turn_x(x, x_o, after=()):
    rows, half = x.shape
    tw = min(512, half)
    n = half // tw

    def body(at_ref, x_ref, xo_ref, o_ref, stage, sems):
        def out(k):
            here = at_block(k, tw)
            return copy(stage.at[here, :], o_ref.at[here, :], sems.at[k])

        @pl.loop(0, n)
        def _(k):
            here = at_block(k, tw)
            stage[here, :rows] = x_ref[:, here].T
            stage[here, rows:] = xo_ref[:, here].T
            out(k).start()

        @pl.loop(0, n)
        def _(k):
            out(k).wait()

    return call(
        body,
        "turn_x",
        [(x, "v"), (x_o, "v")],
        [((half, 2 * rows), BF, "h")],
        [pltpu.VMEM((half, 2 * rows), BF), dma(n)],
        after=after,
        us=3.6,
        mib=12,
    )[0]


def turn_hidden(s, x, x_o, c, c_o, after=(), carry=()):
    rows, half = x.shape
    part = half // 2
    tw = min(512, part)

    def body(at_ref, x_ref, xo_ref, c_ref, co_ref, o_ref):
        @pl.loop(0, part // tw)
        def _(k):
            here = at_block(k, tw)
            there = pl.ds(pl.multiple_of(s * part + k * tw, tw), tw)
            o_ref[here, :rows] = hidden(c_ref[:, here], x_ref[:, there]).T
            o_ref[here, rows:] = hidden(co_ref[:, there], xo_ref[:, there]).T

    return call(
        body,
        "turn_hidden",
        [(a, "v") for a in (x, x_o, c, c_o)],
        [((part, 2 * rows), BF, "v")],
        mib=6,
        after=after,
        us=1.8,
        carry=carry,
    )


def fill(at_ref, both, refs):
    if len(refs) == 2:
        rows = refs[0].shape[0]
        both[:rows, :] = refs[0][...]
        both[rows:, :] = refs[1][...]
        return
    each = refs[0].shape[0]
    bit = at_ref[1] & 1
    for i, (keep, other) in enumerate((refs[:2], refs[2:])):
        both[at_block(2 * i + bit, each), :] = keep[...]
        both[at_block(2 * i + 1 - bit, each), :] = other[...]


def factor_grad(name, s, half, turned, p, so_far, placed=None, after=(), ahead=(), work=1):
    rows2, rank = turned.shape[1], p[0].shape[1]
    part = half // 2
    tw = min(512, part // 2)
    n = part // tw
    np_ = len(p)
    recv, full = ([placed[0]], placed[1]) if placed else ((), None)
    nr = len(recv)
    ins = [(turned, "v")] + [(a, "v") for a in p]
    aliases = {}
    if so_far is not None:
        aliases[len(ins)] = 0
        ins.append((so_far, "h"))
    if placed:
        ins += [(a, "v") for a in recv]
        aliases[len(ins)] = 1
        ins.append((full, "h"))

    def body(at_ref, t_ref, *refs, fetch=nothing):
        p_refs, refs = refs[:np_], refs[np_ + (so_far is not None) :]
        r_refs, refs = refs[:nr], refs[nr + (nr > 0) :]
        o_ref, refs = refs[0], refs[1:]
        if nr:
            f_ref, refs = refs[0], refs[1:]
        stage, both, sems, put_sem = refs

        def put(i):
            w = recv[i].shape[1]
            there = pl.ds(pl.multiple_of((1 - at_ref[0]) * half + s * w, w), w)
            return copy(r_refs[i], f_ref.at[:, there], put_sem.at[i])

        def out(k):
            slot = lax.rem(k, 4)
            there = pl.ds(pl.multiple_of(s * part + k * tw, tw), tw)
            return copy(stage.at[slot], o_ref.at[there, :], sems.at[slot])

        fetch()
        for i in range(nr):
            put(i).start()
        fill(at_ref, both, p_refs)

        @pl.loop(0, n // 2)
        def _(kk):
            @pl.when(kk >= 2)
            def _():
                out(2 * kk - 4).wait()
                out(2 * kk - 3).wait()

            for i in range(2):
                k = 2 * kk + i
                stage[lax.rem(k, 4)] = jnp.dot(t_ref[at_block(k, tw), :], both[...], preferred_element_type=F32).astype(BF)
                out(k).start()

        for k in range(max(0, n - 4), n):
            out(k).wait()
        for i in range(nr):
            put(i).wait()

    outs = [((half, rank), BF, "h")] + ([(full.shape, BF, "h")] if placed else [])
    return call(
        body,
        name,
        ins,
        outs,
        [pltpu.VMEM((4, tw, rank), BF), pltpu.VMEM((rows2, rank), BF), dma(4), dma(max(1, nr))],
        flops=work * rows2 * half * rank,
        aliases=aliases,
        mib=12,
        after=after,
        ahead=ahead,
    )


def expand(s, u, u_first, p, after=(), ahead=()):
    half, rank = u.shape
    rows2 = sum(a.shape[0] for a in p)
    part = half // 2
    tw = u_first.shape[0]
    n = part // tw

    def body(at_ref, u_ref, uf_ref, *refs, fetch=nothing):
        o_ref, uv, both, u_sem = refs[len(p) :]

        def u_copy(k):
            src = u_ref.at[pl.ds(pl.multiple_of(s * part + k * tw, tw), tw), :]
            return copy(src, uv.at[k - 1], u_sem.at[k - 1])

        for k in range(1, n):
            u_copy(k).start()
        fetch()
        fill(at_ref, both, refs[: len(p)])
        o_ref[:, :tw] = lax.dot_general(both[...], uf_ref[...], NT, preferred_element_type=F32)

        @pl.loop(1, n)
        def _(k):
            u_copy(k).wait()
            o_ref[:, at_block(k, tw)] = lax.dot_general(both[...], uv[k - 1], NT, preferred_element_type=F32)

    return call(
        body,
        "expand",
        [(u, "h"), (u_first, "v")] + [(a, "v") for a in p],
        [((rows2, part), F32, "v")],
        [pltpu.VMEM((max(1, n - 1), tw, rank), BF), pltpu.VMEM((rows2, rank), BF), dma(max(1, n - 1))],
        flops=rows2 * half * rank,
        mib=11,
        after=after,
        ahead=ahead,
    )


def input_grad(s, c, c_o, ex, v, v_first, bias, g, so_far, width, after=(), ahead=()):
    rows, half = c_o.shape
    rank = v.shape[1]
    part = half // 2
    tw = v_first.shape[0]
    n = part // tw
    slots = max(1, min(2, n - 1))
    ng = len(g)

    def body(at_ref, c_ref, co_ref, ex_ref, v_ref, vf_ref, b_ref, *refs, fetch=nothing):
        g_refs, refs = refs[:ng], refs[ng + (so_far is not None) :]
        own_ref, oth_ref, stage, vv, both, sems, v_sem = refs

        def v_copy(k):
            src = v_ref.at[pl.ds(pl.multiple_of(s * part + k * tw, tw), tw), :]
            slot = lax.rem(k - 1, slots)
            return copy(src, vv.at[slot], v_sem.at[slot])

        def columns(k):
            return pl.ds(pl.multiple_of(at_ref[0] * half + s * part + k * tw, tw), tw)

        def out(k):
            slot = lax.rem(k, 2)
            return copy(stage.at[slot], own_ref.at[:, columns(k)], sems.at[slot])

        def block(k, v_block):
            here = at_block(k, tw)
            there = pl.ds(pl.multiple_of(s * part + k * tw, tw), tw)
            bk = lax.dot_general(both[...], v_block, NT, preferred_element_type=F32)
            b = b_ref[:, columns(k)].astype(F32)
            cf, cof = c_ref[:, here].astype(F32), co_ref[:, there].astype(F32)
            stage[lax.rem(k, 2)] = (cf * (ex_ref[:rows, here] + b) + cf + bk[:rows]).astype(BF)
            oth_ref[:, here] = (cof * (ex_ref[rows:, here] + b) + cof + bk[rows:]).astype(BF)
            out(k).start()

        for k in range(1, min(n, slots + 1)):
            v_copy(k).start()
        fetch()
        fill(at_ref, both, g_refs)
        block(0, vf_ref[...])

        @pl.loop(1, n)
        def _(k):
            v_copy(k).wait()

            @pl.when(k >= 2)
            def _():
                out(k - 2).wait()

            block(k, vv[lax.rem(k - 1, slots)])

            @pl.when(k + slots < n)
            def _():
                v_copy(k + slots).start()

        for k in range(max(0, n - 2), n):
            out(k).wait()

    ins = [(c, "v"), (c_o, "v"), (ex, "v"), (v, "h"), (v_first, "v"), (bias, "v")] + [(a, "v") for a in g]
    aliases = {}
    if so_far is not None:
        aliases = {len(ins): 0}
        ins.append((so_far, "h"))
    return call(
        body,
        "input_grad",
        ins,
        [((rows, width), BF, "h"), ((rows, part), BF, "v")],
        [
            pltpu.VMEM((2, rows, tw), BF),
            pltpu.VMEM((slots, tw, rank), BF),
            pltpu.VMEM((2 * rows, rank), BF),
            dma(2),
            dma(slots),
        ],
        flops=2 * rows * half * rank,
        aliases=aliases,
        mib=13,
        after=after,
        ahead=ahead,
    )


def plus(a, b):
    return a.astype(F32) + b.astype(F32)


def pair_halves(a, b, direct, after=()):
    rows, rank = a.shape

    def body(at_ref, a_ref, b_ref, *outs):
        write_halves(at_ref, lambda here: plus(a_ref[here, :], b_ref[here, :]), outs)

    return call(body, "pair_halves", [(a, "v"), (b, "v")], halves_of(rows, rank, direct), after=after)


def pieces_of(a, b, m, after=(), carry=()):
    rows, rank = a.shape
    each = rows // m

    def body(at_ref, a_ref, b_ref, *outs):
        for d in range(m):
            here = at_block((at_ref[1] >> 1) ^ d, each)
            outs[d][...] = plus(a_ref[here, :], b_ref[here, :]).astype(BF)

    return call(body, "pieces_of", [(a, "v"), (b, "v")], [((each, rank), BF, "v")] * m, after=after, carry=carry)


def add_pieces(parts, after=(), carry=()):
    def body(at_ref, *refs):
        total = refs[0][...].astype(F32)
        for r in refs[1:-1]:
            total += r[...].astype(F32)
        refs[-1][...] = total.astype(BF)

    return call(body, "add_pieces", [(a, "v") for a in parts], [(parts[0].shape, BF, "v")], after=after, carry=carry)


def join_pieces(parts, after=()):
    m = len(parts)
    each, rank = parts[0].shape

    def body(at_ref, *refs):
        for d in range(m):
            refs[-1][at_block((at_ref[1] >> 1) ^ d, each), :] = refs[d][...]

    return call(body, "join_pieces", [(a, "v") for a in parts], [((m * each, rank), BF, "v")], after=after)[0]


def hold(a, after):
    def body(at_ref, a_ref, o_ref):
        pass

    return call(body, "hold", [(a, "v")], [(a.shape, a.dtype, "v")], aliases={0: 0}, after=after)[0]


def solution(mesh):
    n = mesh.shape["col"]
    m = n // 2
    swap = [(0, 1), (1, 0)]

    def trade(a):
        return lax.ppermute(a, "batch", swap)

    def to(a, d):
        return lax.ppermute(a, "col", [(i, i ^ d) for i in range(n)])

    def spread(parts):
        return [parts[0]] + [to(parts[d], 2 * d) for d in range(1, m)]

    def local(x, c, u, v, bias):
        half, width = u.shape[0], x.shape[1]
        direct = x.shape[0] % (16 * n) == 0 and n & (n - 1) == 0 and n > 2

        def plain(total):
            total = lax.psum(total, "col").astype(BF)
            return [trade(total), total]

        part = half // 2
        tw = min(1024, part)
        x_s = cut_half(x, half)
        x_o = trade(x_s)
        own, x_own, c_s, *v_in = project_own(x, v, c, [x_s])
        theirs = trade(own)
        c_o = trade(hold(c_s, [theirs]))
        *sums, c0, u0 = project_other(x_o, v_in, theirs, c, u, direct)
        acc, b0, c1, u1 = back_project(0, x_own, x_o, c0, c_o, u, u0, None, c)
        if direct:
            parts = pieces_of(sums[0], to(sums[1], 1), m, [acc])
            own_g, mine_g, b1 = back_project(1, x_own, x_o, c1, c_o, u, u1, acc, after=[parts[0]])
            total, own_g = add_pieces(spread(parts), carry=[own_g])
            (h_t0,) = turn_hidden(0, x_own, x_o, c0, c_o, [total])
            sums_g = pair_halves(mine_g, trade(own_g), direct, [h_t0])
            (h_t1,) = turn_hidden(1, x_own, x_o, c1, c_o, [sums_g[0]])
            half_p = join_pieces(spread([total] * m), [h_t1])
            other_p = to(half_p, 1)
            x_t = turn_x(x_own, x_o, [half_p])
            other_p = hold(other_p, [(x_t, "h")])
            grad_b = jnp.concatenate([b0[0], b1[0]])
            p = [trade(half_p), trade(other_p), half_p, other_p]
            (grad_u,) = factor_grad("u_grad", 0, half, h_t0, p, None, after=[(x_t, "h"), (grad_b, "h")])
            parts_g = pieces_of(sums_g[0], to(sums_g[1], 1), m, [(grad_u, "h")])
            grad_u, u0 = factor_grad("u_grad", 1, half, h_t1, p, grad_u, after=[parts_g[0]], ahead=[(u, 0, tw)])
            (total_g,) = add_pieces(spread(parts_g), [(grad_u, "h")])
            ex0, u1 = expand(0, u, u0, p, [total_g], [(u, part, tw)])
            half_g = join_pieces(spread([total_g] * m), [ex0])
            other_g = to(half_g, 1)
            ex1, v0 = expand(1, u, u1, p, [half_g], [(v, 0, tw)])
            other_g = hold(other_g, [ex1])
            g = [trade(half_g), trade(other_g), half_g, other_g]
        else:
            own_g, mine_g, b1 = back_project(1, x_own, x_o, c1, c_o, u, u1, acc)
            (sums_g,) = pair_halves(mine_g, trade(own_g), direct)
            p, g = plain(sums[0]), plain(sums_g)
            grad_b = jnp.concatenate([b0[0], b1[0]])
            x_t = turn_x(x_own, x_o)
            (h_t0,) = turn_hidden(0, x_own, x_o, c0, c_o)
            (h_t1,) = turn_hidden(1, x_own, x_o, c1, c_o)
            (grad_u,) = factor_grad("u_grad", 0, half, h_t0, p, None)
            grad_u, u0 = factor_grad("u_grad", 1, half, h_t1, p, grad_u, ahead=[(u, 0, tw)])
            ex0, u1 = expand(0, u, u0, p, ahead=[(u, part, tw)])
            ex1, v0 = expand(1, u, u1, p, ahead=[(v, 0, tw)])
        bias = bias[None, :]
        out, oth0, v1 = input_grad(0, c0, c_o, ex0, v, v0, bias, g, None, width, [ex1], [(v, part, tw)])
        out, oth1, x_t0 = input_grad(1, c1, c_o, ex1, v, v1, bias, g, out, width, ahead=[(x_t, 0, part)])
        back0, back1 = trade(oth0), trade(oth1)
        grad_v, out, x_t1 = factor_grad("v_grad", 0, half, x_t0, g, None, (back0, out), ahead=[(x_t, part, part)], work=0)
        grad_v, out = factor_grad("v_grad", 1, half, x_t1, g, grad_v, (back1, out))
        return out, grad_u, grad_v, grad_b

    return jax.shard_map(
        local,
        mesh=mesh,
        in_specs=(
            P(("group", "batch"), "col"),
            P(("group", "batch"), "col"),
            P(("col", "batch"), None),
            P(("col", "batch"), None),
            P("col"),
        ),
        out_specs=(
            P(("group", "batch"), "col"),
            P(("group", "col", "batch"), None),
            P(("group", "col", "batch"), None),
            P(("group", "col", "batch")),
        ),
        check_vma=False,
    )
```

```python
import jax
import jax.numpy as jnp
from jax import lax
from jax.experimental import pallas as pl
from jax.experimental.pallas import tpu as pltpu
from jax.sharding import PartitionSpec as P

BF, F32 = jnp.bfloat16, jnp.float32
MIB = 1 << 20
NT = (((1,), (1,)), ((), ()))


class Place:
    def __getitem__(self, i):
        return lax.axis_index(("batch", "col")[i])


def call(body, name, ins, outs, scratch=(), flops=0, aliases=None, mib=4, after=(), us=0.3, carry=(), ahead=()):
    specs = {"v": pl.BlockSpec(memory_space=pltpu.VMEM), "h": pl.BlockSpec(memory_space=pl.ANY)}
    spaces = {"v": pltpu.VMEM, "h": pltpu.HBM}
    n_ins, n_ahead, n_outs, n_after = len(ins), len(ahead), len(outs), len(after)
    aliases = dict(aliases or {})
    aliases.update({n_ins + n_ahead + i: n_outs + n_ahead + i for i in range(len(carry))})
    ins = list(ins) + [(a, "h") for a, _, _ in ahead] + [(a, "v") for a in carry]
    ins += [a if isinstance(a, tuple) else (a, "v") for a in after]
    outs = list(outs) + [((rows, a.shape[1]), a.dtype, "v") for a, _, rows in ahead] + [(a.shape, a.dtype, "v") for a in carry]
    args = [pltpu.with_memory_space_constraint(a, spaces[w]) for a, w in ins]

    def whole(*refs):
        first = len(ins)
        sems = refs[-1] if n_ahead else None
        scratch_refs = refs[first + len(outs) : len(refs) - (n_ahead > 0)]
        fetches = [
            pltpu.make_async_copy(refs[n_ins + i].at[pl.ds(row, rows), :], refs[first + n_outs + i], sems.at[i])
            for i, (_, row, rows) in enumerate(ahead)
        ]
        body(Place(), *refs[:n_ins], *refs[first : first + n_outs], *scratch_refs, fetch=lambda: [f.start() for f in fetches])
        for f in fetches:
            f.wait()

    return pl.pallas_call(
        whole if n_ahead else lambda *refs: body(Place(), *refs[:n_ins], *refs[len(ins) : len(ins) + n_outs], *refs[len(ins) + len(outs) :]),
        out_shape=tuple(spaces[w](dims, dtype) for dims, dtype, w in outs),
        in_specs=[specs[w] for _, w in ins],
        out_specs=tuple(specs[w] for _, _, w in outs),
        scratch_shapes=list(scratch) + ([pltpu.SemaphoreType.DMA((n_ahead,))] if n_ahead else []),
        input_output_aliases=aliases,
        compiler_params=pltpu.CompilerParams(vmem_limit_bytes=mib * MIB),
        cost_estimate=pl.CostEstimate(flops=int(1.7 * flops + us * 1.15e9), bytes_accessed=0, transcendentals=0),
        name=name,
    )(*args)


def nothing():
    pass


def at_block(i, size):
    return pl.ds(pl.multiple_of(i * size, size), size)


def dma(n):
    return pltpu.SemaphoreType.DMA((n,))


def copy(src, dst, sem):
    return pltpu.make_async_copy(src, dst, sem)


def cut_half(x, half, after=()):
    rows = x.shape[0]
    n = 8
    step = rows // n

    def body(at_ref, x_ref, o_ref, sems):
        def cut(i):
            here = pl.ds(i * step, step)
            return copy(x_ref.at[here, at_block(1 - at_ref[0], half)], o_ref.at[here, :], sems.at[i])

        for i in range(n):
            cut(i).start()
        for i in range(n):
            cut(i).wait()

    return call(body, "cut_half", [(x, "h")], [((rows, half), BF, "v")], [dma(n)], us=2.2, after=after)[0]


VPARTS = 4


def project_own(x, v, after=()):
    rows, (half, rank) = x.shape[0], v.shape
    part = half // VPARTS
    tk = min(1024, part)
    n = half // tk
    each = part // tk

    def body(at_ref, x_ref, v_ref, p_ref, xv_ref, *refs):
        vv, (acc, x_sem, v_sem) = refs[:VPARTS], refs[VPARTS:]

        def x_copy(k):
            src = x_ref.at[:, pl.ds(pl.multiple_of(at_ref[0] * half + k * tk, tk), tk)]
            return copy(src, xv_ref.at[:, at_block(k, tk)], x_sem.at[k])

        def v_copy(k, i, j):
            return copy(v_ref.at[at_block(k, tk), :], vv[i].at[at_block(j, tk), :], v_sem.at[k])

        for k in range(n):
            x_copy(k).start()
            v_copy(k, k // each, k % each).start()
        acc[...] = jnp.zeros_like(acc)
        for i in range(VPARTS):

            @pl.loop(0, each)
            def _(j):
                k = i * each + j
                x_copy(k).wait()
                v_copy(k, i, j).wait()
                acc[...] += jnp.dot(xv_ref[:, at_block(k, tk)], vv[i][at_block(j, tk), :], preferred_element_type=F32)

        p_ref[...] = acc[...].astype(BF)

    return call(
        body,
        "project_own",
        [(x, "h"), (v, "h")],
        [((rows, rank), BF, "v"), ((rows, half), BF, "v")] + [((part, rank), BF, "v")] * VPARTS,
        [pltpu.VMEM((rows, rank), F32)] + [dma(n)] * 2,
        flops=2 * rows * half * rank,
        mib=8,
        after=after,
    )


def write_halves(at_ref, total, outs):
    if len(outs) == 1:
        outs[0][...] = total(slice(None))
        return
    each = outs[0].shape[0]
    bit = at_ref[1] & 1
    for i, o_ref in ((bit, outs[0]), (1 - bit, outs[1])):
        o_ref[...] = total(at_block(i, each)).astype(BF)


def halves_of(rows, rank, direct):
    return [((rows // 2, rank), BF, "v")] * 2 if direct else [((rows, rank), F32, "v")]


def project_other(x_o, vs, theirs, c, u, direct):
    rows, half = x_o.shape
    tk, rank = vs[0].shape
    first = half // 2

    def body(at_ref, x_ref, t_ref, c_ref, *refs, fetch):
        vv, outs, cv_ref, acc, c_sem = refs[:VPARTS], refs[VPARTS:-3], refs[-3], refs[-2], refs[-1]
        first_c = copy(c_ref.at[:, at_block(2 * at_ref[0], first)], cv_ref, c_sem.at[0])
        fetch()
        first_c.start()
        for k in range(VPARTS):
            part = jnp.dot(x_ref[:, k * tk : (k + 1) * tk], vv[k][...], preferred_element_type=F32)
            acc[...] = part + (acc[...] if k else t_ref[...].astype(F32))
        write_halves(at_ref, lambda here: acc[here, :], outs)
        first_c.wait()

    return call(
        body,
        "project_other",
        [(x_o, "v"), (theirs, "v"), (c, "h")] + [(a, "v") for a in vs],
        halves_of(rows, rank, direct) + [((rows, first), BF, "v")],
        [pltpu.VMEM((rows, rank), F32), dma(1)],
        flops=2 * rows * half * rank,
        mib=6,
        ahead=[(u, 0, first // 4)],
    )


def hidden(c, x):
    return (c.astype(F32) * x.astype(F32)).astype(BF)


def back_project(s, x, x_o, c, c_o, u, u_first, so_far, c_all=None, after=()):
    rows, (half, rank) = x.shape[0], u.shape
    part = half // 2
    tk = u_first.shape[0]
    n = part // tk
    first = so_far is None
    n_outs = 2 if first else 3

    def body(at_ref, x_ref, xo_ref, c_ref, co_ref, u_ref, uf_ref, *refs, fetch=nothing):
        if first:
            all_ref, acc_ref, b_ref, next_ref, uv, h, u_sem, c_sem = refs
            src = all_ref.at[:, pl.ds(pl.multiple_of(at_ref[0] * half + part, part), part)]
            next_c = copy(src, next_ref, c_sem.at[0])
        else:
            so_ref, own_ref, oth_ref, b_ref, uv, h, u_sem = refs

        def u_copy(k):
            return copy(u_ref.at[pl.ds(s * part + k * tk, tk), :], uv.at[k - 1], u_sem.at[k - 1])

        for k in range(1, n):
            u_copy(k).start()
        if first:
            next_c.start()
        fetch()
        for k in range(n):
            here = pl.ds(k * tk, tk)
            there = pl.ds(s * part + k * tk, tk)
            own = hidden(c_ref[:, here], x_ref[:, there])
            oth = hidden(co_ref[:, there], xo_ref[:, there])
            h[k, :rows, :] = own
            h[k, rows:, :] = oth
            b_ref[:, here] = jnp.sum(own.astype(F32), axis=0, keepdims=True) + jnp.sum(oth.astype(F32), axis=0, keepdims=True)
        @pl.loop(0, 2)
        def _(i):
            at_rows = at_block(i, rows)
            total = None if first else so_ref[at_rows, :]
            for k in range(n):
                if k:

                    @pl.when(i == 0)
                    def _():
                        u_copy(k).wait()

                term = jnp.dot(h[k, at_rows, :], uv[k - 1] if k else uf_ref[...], preferred_element_type=F32)
                total = term if total is None else total + term
            if first:
                acc_ref[at_rows, :] = total
            else:

                @pl.when(i == 0)
                def _():
                    own_ref[...] = total.astype(BF)

                @pl.when(i == 1)
                def _():
                    oth_ref[...] = total

        if first:
            next_c.wait()

    outs = [((2 * rows, rank), F32, "v")] if first else [((rows, rank), BF, "v"), ((rows, rank), F32, "v")]
    outs += [((1, part), F32, "v")] + ([((rows, part), BF, "v")] if first else [])
    return call(
        body,
        "back_project",
        [(x, "v"), (x_o, "v"), (c, "v"), (c_o, "v"), (u, "h"), (u_first, "v"), (c_all, "h") if first else (so_far, "v")],
        outs,
        [pltpu.VMEM((max(1, n - 1), tk, rank), BF), pltpu.VMEM((n, 2 * rows, tk), BF), dma(max(1, n - 1))]
        + ([dma(1)] if first else []),
        flops=2 * rows * half * rank,
        mib=15,
        after=after,
        ahead=[(u, part, tk)] if first else [],
    )


def turn_x(x, x_o, after=()):
    rows, half = x.shape
    tw = min(512, half)
    n = half // tw

    def body(at_ref, x_ref, xo_ref, o_ref, stage, sems):
        def out(k):
            here = at_block(k, tw)
            return copy(stage.at[here, :], o_ref.at[here, :], sems.at[k])

        @pl.loop(0, n)
        def _(k):
            here = at_block(k, tw)
            stage[here, :rows] = x_ref[:, here].T
            stage[here, rows:] = xo_ref[:, here].T
            out(k).start()

        @pl.loop(0, n)
        def _(k):
            out(k).wait()

    return call(
        body,
        "turn_x",
        [(x, "v"), (x_o, "v")],
        [((half, 2 * rows), BF, "h")],
        [pltpu.VMEM((half, 2 * rows), BF), dma(n)],
        after=after,
        us=3.6,
        mib=12,
    )[0]


def turn_hidden(s, x, x_o, c, c_o, after=(), carry=()):
    rows, half = x.shape
    part = half // 2
    tw = min(512, part)

    def body(at_ref, x_ref, xo_ref, c_ref, co_ref, o_ref):
        @pl.loop(0, part // tw)
        def _(k):
            here = at_block(k, tw)
            there = pl.ds(pl.multiple_of(s * part + k * tw, tw), tw)
            o_ref[here, :rows] = hidden(c_ref[:, here], x_ref[:, there]).T
            o_ref[here, rows:] = hidden(co_ref[:, there], xo_ref[:, there]).T

    return call(
        body,
        "turn_hidden",
        [(a, "v") for a in (x, x_o, c, c_o)],
        [((part, 2 * rows), BF, "v")],
        mib=6,
        after=after,
        us=1.8,
        carry=carry,
    )


def fill(at_ref, both, refs):
    if len(refs) == 2:
        rows = refs[0].shape[0]
        both[:rows, :] = refs[0][...]
        both[rows:, :] = refs[1][...]
        return
    each = refs[0].shape[0]
    bit = at_ref[1] & 1
    for i, (keep, other) in enumerate((refs[:2], refs[2:])):
        both[at_block(2 * i + bit, each), :] = keep[...]
        both[at_block(2 * i + 1 - bit, each), :] = other[...]


def factor_grad(name, s, half, turned, p, so_far, placed=None, after=(), ahead=(), work=1):
    rows2, rank = turned.shape[1], p[0].shape[1]
    part = half // 2
    tw = min(512, part // 2)
    n = part // tw
    np_ = len(p)
    recv, full = ([placed[0]], placed[1]) if placed else ((), None)
    nr = len(recv)
    ins = [(turned, "v")] + [(a, "v") for a in p]
    aliases = {}
    if so_far is not None:
        aliases[len(ins)] = 0
        ins.append((so_far, "h"))
    if placed:
        ins += [(a, "v") for a in recv]
        aliases[len(ins)] = 1
        ins.append((full, "h"))

    def body(at_ref, t_ref, *refs, fetch=nothing):
        p_refs, refs = refs[:np_], refs[np_ + (so_far is not None) :]
        r_refs, refs = refs[:nr], refs[nr + (nr > 0) :]
        o_ref, refs = refs[0], refs[1:]
        if nr:
            f_ref, refs = refs[0], refs[1:]
        stage, both, sems, put_sem = refs

        def put(i):
            w = recv[i].shape[1]
            there = pl.ds(pl.multiple_of((1 - at_ref[0]) * half + s * w, w), w)
            return copy(r_refs[i], f_ref.at[:, there], put_sem.at[i])

        def out(k):
            slot = lax.rem(k, 4)
            there = pl.ds(pl.multiple_of(s * part + k * tw, tw), tw)
            return copy(stage.at[slot], o_ref.at[there, :], sems.at[slot])

        fetch()
        for i in range(nr):
            put(i).start()
        fill(at_ref, both, p_refs)

        @pl.loop(0, n // 2)
        def _(kk):
            @pl.when(kk >= 2)
            def _():
                out(2 * kk - 4).wait()
                out(2 * kk - 3).wait()

            for i in range(2):
                k = 2 * kk + i
                stage[lax.rem(k, 4)] = jnp.dot(t_ref[at_block(k, tw), :], both[...], preferred_element_type=F32).astype(BF)
                out(k).start()

        for k in range(max(0, n - 4), n):
            out(k).wait()
        for i in range(nr):
            put(i).wait()

    outs = [((half, rank), BF, "h")] + ([(full.shape, BF, "h")] if placed else [])
    return call(
        body,
        name,
        ins,
        outs,
        [pltpu.VMEM((4, tw, rank), BF), pltpu.VMEM((rows2, rank), BF), dma(4), dma(max(1, nr))],
        flops=work * rows2 * half * rank,
        aliases=aliases,
        mib=12,
        after=after,
        ahead=ahead,
    )


def expand(s, u, u_first, p, after=(), ahead=()):
    half, rank = u.shape
    rows2 = sum(a.shape[0] for a in p)
    part = half // 2
    tw = u_first.shape[0]
    n = part // tw

    def body(at_ref, u_ref, uf_ref, *refs, fetch=nothing):
        o_ref, uv, both, u_sem = refs[len(p) :]

        def u_copy(k):
            src = u_ref.at[pl.ds(pl.multiple_of(s * part + k * tw, tw), tw), :]
            return copy(src, uv.at[k - 1], u_sem.at[k - 1])

        for k in range(1, n):
            u_copy(k).start()
        fetch()
        fill(at_ref, both, refs[: len(p)])
        o_ref[:, :tw] = lax.dot_general(both[...], uf_ref[...], NT, preferred_element_type=F32)

        @pl.loop(1, n)
        def _(k):
            u_copy(k).wait()
            o_ref[:, at_block(k, tw)] = lax.dot_general(both[...], uv[k - 1], NT, preferred_element_type=F32)

    return call(
        body,
        "expand",
        [(u, "h"), (u_first, "v")] + [(a, "v") for a in p],
        [((rows2, part), F32, "v")],
        [pltpu.VMEM((max(1, n - 1), tw, rank), BF), pltpu.VMEM((rows2, rank), BF), dma(max(1, n - 1))],
        flops=rows2 * half * rank,
        mib=11,
        after=after,
        ahead=ahead,
    )


def input_grad(s, c, c_o, ex, v, v_first, bias, g, so_far, width, after=(), ahead=()):
    rows, half = c_o.shape
    rank = v.shape[1]
    part = half // 2
    tw = v_first.shape[0]
    n = part // tw
    slots = max(1, min(2, n - 1))
    ng = len(g)

    def body(at_ref, c_ref, co_ref, ex_ref, v_ref, vf_ref, b_ref, *refs, fetch=nothing):
        g_refs, refs = refs[:ng], refs[ng + (so_far is not None) :]
        own_ref, oth_ref, stage, vv, both, sems, v_sem = refs

        def v_copy(k):
            src = v_ref.at[pl.ds(pl.multiple_of(s * part + k * tw, tw), tw), :]
            slot = lax.rem(k - 1, slots)
            return copy(src, vv.at[slot], v_sem.at[slot])

        def columns(k):
            return pl.ds(pl.multiple_of(at_ref[0] * half + s * part + k * tw, tw), tw)

        def out(k):
            slot = lax.rem(k, 2)
            return copy(stage.at[slot], own_ref.at[:, columns(k)], sems.at[slot])

        def block(k, v_block):
            here = at_block(k, tw)
            there = pl.ds(pl.multiple_of(s * part + k * tw, tw), tw)
            bk = lax.dot_general(both[...], v_block, NT, preferred_element_type=F32)
            b = b_ref[:, columns(k)].astype(F32)
            cf, cof = c_ref[:, here].astype(F32), co_ref[:, there].astype(F32)
            stage[lax.rem(k, 2)] = (cf * (ex_ref[:rows, here] + b) + cf + bk[:rows]).astype(BF)
            oth_ref[:, here] = (cof * (ex_ref[rows:, here] + b) + cof + bk[rows:]).astype(BF)
            out(k).start()

        for k in range(1, min(n, slots + 1)):
            v_copy(k).start()
        fetch()
        fill(at_ref, both, g_refs)
        block(0, vf_ref[...])

        @pl.loop(1, n)
        def _(k):
            v_copy(k).wait()

            @pl.when(k >= 2)
            def _():
                out(k - 2).wait()

            block(k, vv[lax.rem(k - 1, slots)])

            @pl.when(k + slots < n)
            def _():
                v_copy(k + slots).start()

        for k in range(max(0, n - 2), n):
            out(k).wait()

    ins = [(c, "v"), (c_o, "v"), (ex, "v"), (v, "h"), (v_first, "v"), (bias, "v")] + [(a, "v") for a in g]
    aliases = {}
    if so_far is not None:
        aliases = {len(ins): 0}
        ins.append((so_far, "h"))
    return call(
        body,
        "input_grad",
        ins,
        [((rows, width), BF, "h"), ((rows, part), BF, "v")],
        [
            pltpu.VMEM((2, rows, tw), BF),
            pltpu.VMEM((slots, tw, rank), BF),
            pltpu.VMEM((2 * rows, rank), BF),
            dma(2),
            dma(slots),
        ],
        flops=2 * rows * half * rank,
        aliases=aliases,
        mib=13,
        after=after,
        ahead=ahead,
    )


def plus(a, b):
    return a.astype(F32) + b.astype(F32)


def pair_halves(a, b, direct, after=()):
    rows, rank = a.shape

    def body(at_ref, a_ref, b_ref, *outs):
        write_halves(at_ref, lambda here: plus(a_ref[here, :], b_ref[here, :]), outs)

    return call(body, "pair_halves", [(a, "v"), (b, "v")], halves_of(rows, rank, direct), after=after)


def pieces_of(a, b, m, after=(), carry=()):
    rows, rank = a.shape
    each = rows // m

    def body(at_ref, a_ref, b_ref, *outs):
        for d in range(m):
            here = at_block((at_ref[1] >> 1) ^ d, each)
            outs[d][...] = plus(a_ref[here, :], b_ref[here, :]).astype(BF)

    return call(body, "pieces_of", [(a, "v"), (b, "v")], [((each, rank), BF, "v")] * m, after=after, carry=carry)


def add_pieces(parts, after=(), carry=()):
    def body(at_ref, *refs):
        total = refs[0][...].astype(F32)
        for r in refs[1:-1]:
            total += r[...].astype(F32)
        refs[-1][...] = total.astype(BF)

    return call(body, "add_pieces", [(a, "v") for a in parts], [(parts[0].shape, BF, "v")], after=after, carry=carry)


def join_pieces(parts, after=()):
    m = len(parts)
    each, rank = parts[0].shape

    def body(at_ref, *refs):
        for d in range(m):
            refs[-1][at_block((at_ref[1] >> 1) ^ d, each), :] = refs[d][...]

    return call(body, "join_pieces", [(a, "v") for a in parts], [((m * each, rank), BF, "v")], after=after)[0]


def hold(a, after):
    def body(at_ref, a_ref, o_ref):
        pass

    return call(body, "hold", [(a, "v")], [(a.shape, a.dtype, "v")], aliases={0: 0}, after=after)[0]


def solution(mesh):
    n = mesh.shape["col"]
    m = n // 2
    swap = [(0, 1), (1, 0)]

    def trade(a):
        return lax.ppermute(a, "batch", swap)

    def to(a, d):
        return lax.ppermute(a, "col", [(i, i ^ d) for i in range(n)])

    def spread(parts):
        return [parts[0]] + [to(parts[d], 2 * d) for d in range(1, m)]

    def local(x, c, u, v, bias):
        half, width = u.shape[0], x.shape[1]
        direct = x.shape[0] % (16 * n) == 0 and n & (n - 1) == 0 and n > 2

        def plain(total):
            total = lax.psum(total, "col").astype(BF)
            return [trade(total), total]

        part = half // 2
        tw = min(1024, part)
        x_s = cut_half(x, half)
        x_o = trade(x_s)
        own, x_own, *v_in = project_own(x, v, [x_s])
        theirs = trade(own)
        c_o = trade(hold(cut_half(c, half, [own]), [theirs]))
        *sums, c0, u0 = project_other(x_o, v_in, theirs, c, u, direct)
        acc, b0, c1, u1 = back_project(0, x_own, x_o, c0, c_o, u, u0, None, c)
        if direct:
            parts = pieces_of(sums[0], to(sums[1], 1), m, [acc])
            own_g, mine_g, b1 = back_project(1, x_own, x_o, c1, c_o, u, u1, acc, after=[parts[0]])
            total, own_g = add_pieces(spread(parts), carry=[own_g])
            (h_t0,) = turn_hidden(0, x_own, x_o, c0, c_o, [total])
            sums_g = pair_halves(mine_g, trade(own_g), direct, [h_t0])
            (h_t1,) = turn_hidden(1, x_own, x_o, c1, c_o, [sums_g[0]])
            half_p = join_pieces(spread([total] * m), [h_t1])
            other_p = to(half_p, 1)
            x_t = turn_x(x_own, x_o, [half_p])
            other_p = hold(other_p, [(x_t, "h")])
            grad_b = jnp.concatenate([b0[0], b1[0]])
            p = [trade(half_p), trade(other_p), half_p, other_p]
            (grad_u,) = factor_grad("u_grad", 0, half, h_t0, p, None, after=[(x_t, "h")])
            parts_g = pieces_of(sums_g[0], to(sums_g[1], 1), m, [(grad_u, "h")])
            grad_u, u0 = factor_grad("u_grad", 1, half, h_t1, p, grad_u, after=[parts_g[0]], ahead=[(u, 0, tw)])
            (total_g,) = add_pieces(spread(parts_g), [(grad_u, "h")])
            ex0, u1 = expand(0, u, u0, p, [total_g], [(u, part, tw)])
            half_g = join_pieces(spread([total_g] * m), [ex0])
            other_g = to(half_g, 1)
            ex1, v0 = expand(1, u, u1, p, [half_g], [(v, 0, tw)])
            other_g = hold(other_g, [ex1])
            g = [trade(half_g), trade(other_g), half_g, other_g]
        else:
            own_g, mine_g, b1 = back_project(1, x_own, x_o, c1, c_o, u, u1, acc)
            (sums_g,) = pair_halves(mine_g, trade(own_g), direct)
            p, g = plain(sums[0]), plain(sums_g)
            grad_b = jnp.concatenate([b0[0], b1[0]])
            x_t = turn_x(x_own, x_o)
            (h_t0,) = turn_hidden(0, x_own, x_o, c0, c_o)
            (h_t1,) = turn_hidden(1, x_own, x_o, c1, c_o)
            (grad_u,) = factor_grad("u_grad", 0, half, h_t0, p, None)
            grad_u, u0 = factor_grad("u_grad", 1, half, h_t1, p, grad_u, ahead=[(u, 0, tw)])
            ex0, u1 = expand(0, u, u0, p, ahead=[(u, part, tw)])
            ex1, v0 = expand(1, u, u1, p, ahead=[(v, 0, tw)])
        bias = bias[None, :]
        out, oth0, v1 = input_grad(0, c0, c_o, ex0, v, v0, bias, g, None, width, [ex1, (grad_b, "h")], [(v, part, tw)])
        out, oth1, x_t0 = input_grad(1, c1, c_o, ex1, v, v1, bias, g, out, width, ahead=[(x_t, 0, part)])
        back0, back1 = trade(oth0), trade(oth1)
        grad_v, out, x_t1 = factor_grad("v_grad", 0, half, x_t0, g, None, (back0, out), ahead=[(x_t, part, part)], work=0)
        grad_v, out = factor_grad("v_grad", 1, half, x_t1, g, grad_v, (back1, out))
        return out, grad_u, grad_v, grad_b

    return jax.shard_map(
        local,
        mesh=mesh,
        in_specs=(
            P(("group", "batch"), "col"),
            P(("group", "batch"), "col"),
            P(("col", "batch"), None),
            P(("col", "batch"), None),
            P("col"),
        ),
        out_specs=(
            P(("group", "batch"), "col"),
            P(("group", "col", "batch"), None),
            P(("group", "col", "batch"), None),
            P(("group", "col", "batch")),
        ),
        check_vma=False,
    )
```

```python
import jax
import jax.numpy as jnp
from jax import lax
from jax.experimental import pallas as pl
from jax.experimental.pallas import tpu as pltpu
from jax.sharding import PartitionSpec as P

BF, F32 = jnp.bfloat16, jnp.float32
MIB = 1 << 20
NT = (((1,), (1,)), ((), ()))


class Place:
    def __getitem__(self, i):
        return lax.axis_index(("batch", "col")[i])


def call(body, name, ins, outs, scratch=(), flops=0, aliases=None, mib=4, after=(), us=0.3, carry=(), ahead=()):
    specs = {"v": pl.BlockSpec(memory_space=pltpu.VMEM), "h": pl.BlockSpec(memory_space=pl.ANY)}
    spaces = {"v": pltpu.VMEM, "h": pltpu.HBM}
    n_ins, n_ahead, n_outs, n_after = len(ins), len(ahead), len(outs), len(after)
    aliases = dict(aliases or {})
    aliases.update({n_ins + n_ahead + i: n_outs + n_ahead + i for i in range(len(carry))})
    ins = list(ins) + [(a, "h") for a, _, _ in ahead] + [(a, "v") for a in carry]
    ins += [a if isinstance(a, tuple) else (a, "v") for a in after]
    outs = list(outs) + [((rows, a.shape[1]), a.dtype, "v") for a, _, rows in ahead] + [(a.shape, a.dtype, "v") for a in carry]
    args = [pltpu.with_memory_space_constraint(a, spaces[w]) for a, w in ins]

    def whole(*refs):
        first = len(ins)
        sems = refs[-1] if n_ahead else None
        scratch_refs = refs[first + len(outs) : len(refs) - (n_ahead > 0)]
        fetches = [
            pltpu.make_async_copy(refs[n_ins + i].at[pl.ds(row, rows), :], refs[first + n_outs + i], sems.at[i])
            for i, (_, row, rows) in enumerate(ahead)
        ]
        body(Place(), *refs[:n_ins], *refs[first : first + n_outs], *scratch_refs, fetch=lambda: [f.start() for f in fetches])
        for f in fetches:
            f.wait()

    return pl.pallas_call(
        whole if n_ahead else lambda *refs: body(Place(), *refs[:n_ins], *refs[len(ins) : len(ins) + n_outs], *refs[len(ins) + len(outs) :]),
        out_shape=tuple(spaces[w](dims, dtype) for dims, dtype, w in outs),
        in_specs=[specs[w] for _, w in ins],
        out_specs=tuple(specs[w] for _, _, w in outs),
        scratch_shapes=list(scratch) + ([pltpu.SemaphoreType.DMA((n_ahead,))] if n_ahead else []),
        input_output_aliases=aliases,
        compiler_params=pltpu.CompilerParams(vmem_limit_bytes=mib * MIB),
        cost_estimate=pl.CostEstimate(flops=int(1.7 * flops + us * 1.15e9), bytes_accessed=0, transcendentals=0),
        name=name,
    )(*args)


def nothing():
    pass


def at_block(i, size):
    return pl.ds(pl.multiple_of(i * size, size), size)


def dma(n):
    return pltpu.SemaphoreType.DMA((n,))


def copy(src, dst, sem):
    return pltpu.make_async_copy(src, dst, sem)


def cut_half(x, half, after=()):
    rows = x.shape[0]
    n = 8
    step = rows // n

    def body(at_ref, x_ref, o_ref, sems):
        def cut(i):
            here = pl.ds(i * step, step)
            return copy(x_ref.at[here, at_block(1 - at_ref[0], half)], o_ref.at[here, :], sems.at[i])

        for i in range(n):
            cut(i).start()
        for i in range(n):
            cut(i).wait()

    return call(body, "cut_half", [(x, "h")], [((rows, half), BF, "v")], [dma(n)], us=2.2, after=after)[0]


VPARTS = 4


def project_own(x, v, after=()):
    rows, (half, rank) = x.shape[0], v.shape
    part = half // VPARTS
    tk = min(1024, part)
    n = half // tk
    each = part // tk

    def body(at_ref, x_ref, v_ref, p_ref, xv_ref, *refs):
        vv, (acc, x_sem, v_sem) = refs[:VPARTS], refs[VPARTS:]

        def x_copy(k):
            src = x_ref.at[:, pl.ds(pl.multiple_of(at_ref[0] * half + k * tk, tk), tk)]
            return copy(src, xv_ref.at[:, at_block(k, tk)], x_sem.at[k])

        def v_copy(k, i, j):
            return copy(v_ref.at[at_block(k, tk), :], vv[i].at[at_block(j, tk), :], v_sem.at[k])

        for k in range(n):
            x_copy(k).start()
            v_copy(k, k // each, k % each).start()
        acc[...] = jnp.zeros_like(acc)
        for i in range(VPARTS):

            @pl.loop(0, each)
            def _(j):
                k = i * each + j
                x_copy(k).wait()
                v_copy(k, i, j).wait()
                acc[...] += jnp.dot(xv_ref[:, at_block(k, tk)], vv[i][at_block(j, tk), :], preferred_element_type=F32)

        p_ref[...] = acc[...].astype(BF)

    return call(
        body,
        "project_own",
        [(x, "h"), (v, "h")],
        [((rows, rank), BF, "v"), ((rows, half), BF, "v")] + [((part, rank), BF, "v")] * VPARTS,
        [pltpu.VMEM((rows, rank), F32)] + [dma(n)] * 2,
        flops=2 * rows * half * rank,
        mib=8,
        after=after,
    )


def write_halves(at_ref, total, outs):
    if len(outs) == 1:
        outs[0][...] = total(slice(None))
        return
    each = outs[0].shape[0]
    bit = at_ref[1] & 1
    for i, o_ref in ((bit, outs[0]), (1 - bit, outs[1])):
        o_ref[...] = total(at_block(i, each)).astype(BF)


def halves_of(rows, rank, direct):
    return [((rows // 2, rank), BF, "v")] * 2 if direct else [((rows, rank), F32, "v")]


def project_other(x_o, vs, theirs, c, u, direct):
    rows, half = x_o.shape
    tk, rank = vs[0].shape
    first = half // 2

    def body(at_ref, x_ref, t_ref, c_ref, *refs, fetch):
        vv, outs, cv_ref, acc, c_sem = refs[:VPARTS], refs[VPARTS:-3], refs[-3], refs[-2], refs[-1]
        first_c = copy(c_ref.at[:, at_block(2 * at_ref[0], first)], cv_ref, c_sem.at[0])
        fetch()
        first_c.start()
        for k in range(VPARTS):
            part = jnp.dot(x_ref[:, k * tk : (k + 1) * tk], vv[k][...], preferred_element_type=F32)
            acc[...] = part + (acc[...] if k else t_ref[...].astype(F32))
        write_halves(at_ref, lambda here: acc[here, :], outs)
        first_c.wait()

    return call(
        body,
        "project_other",
        [(x_o, "v"), (theirs, "v"), (c, "h")] + [(a, "v") for a in vs],
        halves_of(rows, rank, direct) + [((rows, first), BF, "v")],
        [pltpu.VMEM((rows, rank), F32), dma(1)],
        flops=2 * rows * half * rank,
        mib=6,
        ahead=[(u, 0, first // 4)],
    )


def hidden(c, x):
    return (c.astype(F32) * x.astype(F32)).astype(BF)


def back_project(lo, n, x, x_o, c, c_o, u, u_first, so_far, c_all=None, after=()):
    rows, (half, rank) = x.shape[0], u.shape
    part = c.shape[1]
    tk = u_first.shape[0]
    shift = lo * tk % part
    first, last = so_far is None, (lo + n) * tk == half

    def body(at_ref, x_ref, xo_ref, c_ref, co_ref, u_ref, uf_ref, *refs, fetch=nothing):
        if first:
            all_ref, acc_ref, b_ref, next_ref, uv, h, u_sem, c_sem = refs
            src = all_ref.at[:, pl.ds(pl.multiple_of(at_ref[0] * half + part, part), part)]
            next_c = copy(src, next_ref, c_sem.at[0])
        elif last:
            so_ref, own_ref, oth_ref, b_ref, uv, h, u_sem = refs
        else:
            so_ref, acc_ref, b_ref, uv, h, u_sem = refs

        def u_copy(k):
            return copy(u_ref.at[pl.ds((lo + k) * tk, tk), :], uv.at[k - 1], u_sem.at[k - 1])

        for k in range(1, n):
            u_copy(k).start()
        if first:
            next_c.start()
        fetch()
        for k in range(n):
            here = pl.ds(k * tk, tk)
            there = pl.ds((lo + k) * tk, tk)
            own = hidden(c_ref[:, pl.ds(shift + k * tk, tk)], x_ref[:, there])
            oth = hidden(co_ref[:, there], xo_ref[:, there])
            h[k, :rows, :] = own
            h[k, rows:, :] = oth
            b_ref[:, here] = jnp.sum(own.astype(F32), axis=0, keepdims=True) + jnp.sum(oth.astype(F32), axis=0, keepdims=True)

        @pl.loop(0, 2)
        def _(i):
            at_rows = at_block(i, rows)
            total = None if first else so_ref[at_rows, :]
            for k in range(n):
                if k:

                    @pl.when(i == 0)
                    def _():
                        u_copy(k).wait()

                term = jnp.dot(h[k, at_rows, :], uv[k - 1] if k else uf_ref[...], preferred_element_type=F32)
                total = term if total is None else total + term
            if not last:
                acc_ref[at_rows, :] = total
            else:

                @pl.when(i == 0)
                def _():
                    own_ref[...] = total.astype(BF)

                @pl.when(i == 1)
                def _():
                    oth_ref[...] = total

        if first:
            next_c.wait()

    outs = [((rows, rank), BF, "v"), ((rows, rank), F32, "v")] if last else [((2 * rows, rank), F32, "v")]
    outs += [((1, n * tk), F32, "v")] + ([((rows, part), BF, "v")] if first else [])
    return call(
        body,
        "back_project",
        [(x, "v"), (x_o, "v"), (c, "v"), (c_o, "v"), (u, "h"), (u_first, "v"), (c_all, "h") if first else (so_far, "v")],
        outs,
        [pltpu.VMEM((max(1, n - 1), tk, rank), BF), pltpu.VMEM((n, 2 * rows, tk), BF), dma(max(1, n - 1))]
        + ([dma(1)] if first else []),
        flops=4 * rows * n * tk * rank,
        mib=15 if first else 12,
        after=after,
        ahead=[] if last else [(u, (lo + n) * tk, tk)],
    )


def turn_x(x, x_o, after=()):
    rows, half = x.shape
    tw = min(512, half)
    n = half // tw

    def body(at_ref, x_ref, xo_ref, o_ref, stage, sems):
        def out(k):
            here = at_block(k, tw)
            return copy(stage.at[here, :], o_ref.at[here, :], sems.at[k])

        @pl.loop(0, n)
        def _(k):
            here = at_block(k, tw)
            stage[here, :rows] = x_ref[:, here].T
            stage[here, rows:] = xo_ref[:, here].T
            out(k).start()

        @pl.loop(0, n)
        def _(k):
            out(k).wait()

    return call(
        body,
        "turn_x",
        [(x, "v"), (x_o, "v")],
        [((half, 2 * rows), BF, "h")],
        [pltpu.VMEM((half, 2 * rows), BF), dma(n)],
        after=after,
        us=3.6,
        mib=12,
    )[0]


def turn_hidden(s, x, x_o, c, c_o, after=(), carry=()):
    rows, half = x.shape
    part = half // 2
    tw = min(512, part)

    def body(at_ref, x_ref, xo_ref, c_ref, co_ref, o_ref):
        @pl.loop(0, part // tw)
        def _(k):
            here = at_block(k, tw)
            there = pl.ds(pl.multiple_of(s * part + k * tw, tw), tw)
            o_ref[here, :rows] = hidden(c_ref[:, here], x_ref[:, there]).T
            o_ref[here, rows:] = hidden(co_ref[:, there], xo_ref[:, there]).T

    return call(
        body,
        "turn_hidden",
        [(a, "v") for a in (x, x_o, c, c_o)],
        [((part, 2 * rows), BF, "v")],
        mib=6,
        after=after,
        us=1.8,
        carry=carry,
    )


def fill(at_ref, both, refs):
    if len(refs) == 2:
        rows = refs[0].shape[0]
        both[:rows, :] = refs[0][...]
        both[rows:, :] = refs[1][...]
        return
    each = refs[0].shape[0]
    bit = at_ref[1] & 1
    for i, (keep, other) in enumerate((refs[:2], refs[2:])):
        both[at_block(2 * i + bit, each), :] = keep[...]
        both[at_block(2 * i + 1 - bit, each), :] = other[...]


def factor_grad(name, s, half, turned, p, so_far, placed=None, after=(), ahead=(), work=1):
    rows2, rank = turned.shape[1], p[0].shape[1]
    part = half // 2
    tw = min(512, part // 2)
    n = part // tw
    np_ = len(p)
    recv, full = ([placed[0]], placed[1]) if placed else ((), None)
    nr = len(recv)
    ins = [(turned, "v")] + [(a, "v") for a in p]
    aliases = {}
    if so_far is not None:
        aliases[len(ins)] = 0
        ins.append((so_far, "h"))
    if placed:
        ins += [(a, "v") for a in recv]
        aliases[len(ins)] = 1
        ins.append((full, "h"))

    def body(at_ref, t_ref, *refs, fetch=nothing):
        p_refs, refs = refs[:np_], refs[np_ + (so_far is not None) :]
        r_refs, refs = refs[:nr], refs[nr + (nr > 0) :]
        o_ref, refs = refs[0], refs[1:]
        if nr:
            f_ref, refs = refs[0], refs[1:]
        stage, both, sems, put_sem = refs

        def put(i):
            w = recv[i].shape[1]
            there = pl.ds(pl.multiple_of((1 - at_ref[0]) * half + s * w, w), w)
            return copy(r_refs[i], f_ref.at[:, there], put_sem.at[i])

        def out(k):
            slot = lax.rem(k, 4)
            there = pl.ds(pl.multiple_of(s * part + k * tw, tw), tw)
            return copy(stage.at[slot], o_ref.at[there, :], sems.at[slot])

        fetch()
        for i in range(nr):
            put(i).start()
        fill(at_ref, both, p_refs)

        @pl.loop(0, n // 2)
        def _(kk):
            @pl.when(kk >= 2)
            def _():
                out(2 * kk - 4).wait()
                out(2 * kk - 3).wait()

            for i in range(2):
                k = 2 * kk + i
                stage[lax.rem(k, 4)] = jnp.dot(t_ref[at_block(k, tw), :], both[...], preferred_element_type=F32).astype(BF)
                out(k).start()

        for k in range(max(0, n - 4), n):
            out(k).wait()
        for i in range(nr):
            put(i).wait()

    outs = [((half, rank), BF, "h")] + ([(full.shape, BF, "h")] if placed else [])
    return call(
        body,
        name,
        ins,
        outs,
        [pltpu.VMEM((4, tw, rank), BF), pltpu.VMEM((rows2, rank), BF), dma(4), dma(max(1, nr))],
        flops=work * rows2 * half * rank,
        aliases=aliases,
        mib=12,
        after=after,
        ahead=ahead,
    )


def expand(s, u, u_first, p, after=(), ahead=()):
    half, rank = u.shape
    rows2 = sum(a.shape[0] for a in p)
    part = half // 2
    tw = u_first.shape[0]
    n = part // tw

    def body(at_ref, u_ref, uf_ref, *refs, fetch=nothing):
        o_ref, uv, both, u_sem = refs[len(p) :]

        def u_copy(k):
            src = u_ref.at[pl.ds(pl.multiple_of(s * part + k * tw, tw), tw), :]
            return copy(src, uv.at[k - 1], u_sem.at[k - 1])

        for k in range(1, n):
            u_copy(k).start()
        fetch()
        fill(at_ref, both, refs[: len(p)])
        o_ref[:, :tw] = lax.dot_general(both[...], uf_ref[...], NT, preferred_element_type=F32)

        @pl.loop(1, n)
        def _(k):
            u_copy(k).wait()
            o_ref[:, at_block(k, tw)] = lax.dot_general(both[...], uv[k - 1], NT, preferred_element_type=F32)

    return call(
        body,
        "expand",
        [(u, "h"), (u_first, "v")] + [(a, "v") for a in p],
        [((rows2, part), F32, "v")],
        [pltpu.VMEM((max(1, n - 1), tw, rank), BF), pltpu.VMEM((rows2, rank), BF), dma(max(1, n - 1))],
        flops=rows2 * half * rank,
        mib=11,
        after=after,
        ahead=ahead,
    )


def input_grad(s, c, c_o, ex, v, v_first, bias, g, so_far, width, after=(), ahead=()):
    rows, half = c_o.shape
    rank = v.shape[1]
    part = half // 2
    tw = v_first.shape[0]
    n = part // tw
    slots = max(1, min(2, n - 1))
    ng = len(g)

    def body(at_ref, c_ref, co_ref, ex_ref, v_ref, vf_ref, b_ref, *refs, fetch=nothing):
        g_refs, refs = refs[:ng], refs[ng + (so_far is not None) :]
        own_ref, oth_ref, stage, vv, both, sems, v_sem = refs

        def v_copy(k):
            src = v_ref.at[pl.ds(pl.multiple_of(s * part + k * tw, tw), tw), :]
            slot = lax.rem(k - 1, slots)
            return copy(src, vv.at[slot], v_sem.at[slot])

        def columns(k):
            return pl.ds(pl.multiple_of(at_ref[0] * half + s * part + k * tw, tw), tw)

        def out(k):
            slot = lax.rem(k, 2)
            return copy(stage.at[slot], own_ref.at[:, columns(k)], sems.at[slot])

        def block(k, v_block):
            here = at_block(k, tw)
            there = pl.ds(pl.multiple_of(s * part + k * tw, tw), tw)
            bk = lax.dot_general(both[...], v_block, NT, preferred_element_type=F32)
            b = b_ref[:, columns(k)].astype(F32)
            cf, cof = c_ref[:, here].astype(F32), co_ref[:, there].astype(F32)
            stage[lax.rem(k, 2)] = (cf * (ex_ref[:rows, here] + b) + cf + bk[:rows]).astype(BF)
            oth_ref[:, here] = (cof * (ex_ref[rows:, here] + b) + cof + bk[rows:]).astype(BF)
            out(k).start()

        for k in range(1, min(n, slots + 1)):
            v_copy(k).start()
        fetch()
        fill(at_ref, both, g_refs)
        block(0, vf_ref[...])

        @pl.loop(1, n)
        def _(k):
            v_copy(k).wait()

            @pl.when(k >= 2)
            def _():
                out(k - 2).wait()

            block(k, vv[lax.rem(k - 1, slots)])

            @pl.when(k + slots < n)
            def _():
                v_copy(k + slots).start()

        for k in range(max(0, n - 2), n):
            out(k).wait()

    ins = [(c, "v"), (c_o, "v"), (ex, "v"), (v, "h"), (v_first, "v"), (bias, "v")] + [(a, "v") for a in g]
    aliases = {}
    if so_far is not None:
        aliases = {len(ins): 0}
        ins.append((so_far, "h"))
    return call(
        body,
        "input_grad",
        ins,
        [((rows, width), BF, "h"), ((rows, part), BF, "v")],
        [
            pltpu.VMEM((2, rows, tw), BF),
            pltpu.VMEM((slots, tw, rank), BF),
            pltpu.VMEM((2 * rows, rank), BF),
            dma(2),
            dma(slots),
        ],
        flops=2 * rows * half * rank,
        aliases=aliases,
        mib=13,
        after=after,
        ahead=ahead,
    )


def plus(a, b):
    return a.astype(F32) + b.astype(F32)


def pair_halves(a, b, direct, after=()):
    rows, rank = a.shape

    def body(at_ref, a_ref, b_ref, *outs):
        write_halves(at_ref, lambda here: plus(a_ref[here, :], b_ref[here, :]), outs)

    return call(body, "pair_halves", [(a, "v"), (b, "v")], halves_of(rows, rank, direct), after=after)


def pieces_of(a, b, m, after=(), carry=()):
    rows, rank = a.shape
    each = rows // m

    def body(at_ref, a_ref, b_ref, *outs):
        for d in range(m):
            here = at_block((at_ref[1] >> 1) ^ d, each)
            outs[d][...] = plus(a_ref[here, :], b_ref[here, :]).astype(BF)

    return call(body, "pieces_of", [(a, "v"), (b, "v")], [((each, rank), BF, "v")] * m, after=after, carry=carry)


def add_pieces(parts, after=(), carry=()):
    def body(at_ref, *refs):
        total = refs[0][...].astype(F32)
        for r in refs[1:-1]:
            total += r[...].astype(F32)
        refs[-1][...] = total.astype(BF)

    return call(body, "add_pieces", [(a, "v") for a in parts], [(parts[0].shape, BF, "v")], after=after, carry=carry)


def join_pieces(parts, after=(), carry=()):
    m = len(parts)
    each, rank = parts[0].shape

    def body(at_ref, *refs):
        for d in range(m):
            refs[-1][at_block((at_ref[1] >> 1) ^ d, each), :] = refs[d][...]

    return call(body, "join_pieces", [(a, "v") for a in parts], [((m * each, rank), BF, "v")], after=after, carry=carry)


def hold(a, after):
    def body(at_ref, a_ref, o_ref):
        pass

    return call(body, "hold", [(a, "v")], [(a.shape, a.dtype, "v")], aliases={0: 0}, after=after)[0]


def solution(mesh):
    n = mesh.shape["col"]
    m = n // 2
    swap = [(0, 1), (1, 0)]

    def trade(a):
        return lax.ppermute(a, "batch", swap)

    def to(a, d):
        return lax.ppermute(a, "col", [(i, i ^ d) for i in range(n)])

    def spread(parts):
        return [parts[0]] + [to(parts[d], 2 * d) for d in range(1, m)]

    def local(x, c, u, v, bias):
        half, width = u.shape[0], x.shape[1]
        direct = x.shape[0] % (16 * n) == 0 and n & (n - 1) == 0 and n > 2

        def plain(total):
            total = lax.psum(total, "col").astype(BF)
            return [trade(total), total]

        part = half // 2
        tw = min(1024, part)
        x_s = cut_half(x, half)
        x_o = trade(x_s)
        own, x_own, *v_in = project_own(x, v, [x_s])
        theirs = trade(own)
        c_o = trade(hold(cut_half(c, half, [own]), [theirs]))
        *sums, c0, u0 = project_other(x_o, v_in, theirs, c, u, direct)
        acc, b0, c1, u1 = back_project(0, 4, x_own, x_o, c0, c_o, u, u0, None, c)
        if direct:
            parts = pieces_of(sums[0], to(sums[1], 1), m, [acc])
            acc, b1, u1 = back_project(4, 2, x_own, x_o, c1, c_o, u, u1, acc, after=[parts[0]])
            (h_t0,) = turn_hidden(0, x_own, x_o, c0, c_o, [acc])
            (total,) = add_pieces(spread(parts), [h_t0])
            own_g, mine_g, b2 = back_project(6, 2, x_own, x_o, c1, c_o, u, u1, acc, after=[total])
            (h_t1,) = turn_hidden(1, x_own, x_o, c1, c_o, [mine_g])
            half_p, own_g = join_pieces(spread([total] * m), [h_t1], [own_g])
            other_p = to(half_p, 1)
            x_t = turn_x(x_own, x_o, [half_p])
            sums_g = pair_halves(mine_g, trade(own_g), direct, [(x_t, "h")])
            other_p = hold(other_p, [(x_t, "h")])
            grad_b = jnp.concatenate([b0[0], b1[0], b2[0]])
            p = [trade(half_p), trade(other_p), half_p, other_p]
            (grad_u,) = factor_grad("u_grad", 0, half, h_t0, p, None, after=[(x_t, "h")])
            parts_g = pieces_of(sums_g[0], to(sums_g[1], 1), m, [(grad_u, "h")])
            grad_u, u0 = factor_grad("u_grad", 1, half, h_t1, p, grad_u, after=[parts_g[0]], ahead=[(u, 0, tw)])
            (total_g,) = add_pieces(spread(parts_g), [(grad_u, "h")])
            ex0, u1 = expand(0, u, u0, p, [total_g], [(u, part, tw)])
            (half_g,) = join_pieces(spread([total_g] * m), [ex0])
            other_g = to(half_g, 1)
            ex1, v0 = expand(1, u, u1, p, [half_g], [(v, 0, tw)])
            other_g = hold(other_g, [ex1])
            g = [trade(half_g), trade(other_g), half_g, other_g]
        else:
            acc, b1, u1 = back_project(4, 2, x_own, x_o, c1, c_o, u, u1, acc)
            own_g, mine_g, b2 = back_project(6, 2, x_own, x_o, c1, c_o, u, u1, acc)
            (sums_g,) = pair_halves(mine_g, trade(own_g), direct)
            p, g = plain(sums[0]), plain(sums_g)
            grad_b = jnp.concatenate([b0[0], b1[0], b2[0]])
            x_t = turn_x(x_own, x_o)
            (h_t0,) = turn_hidden(0, x_own, x_o, c0, c_o)
            (h_t1,) = turn_hidden(1, x_own, x_o, c1, c_o)
            (grad_u,) = factor_grad("u_grad", 0, half, h_t0, p, None)
            grad_u, u0 = factor_grad("u_grad", 1, half, h_t1, p, grad_u, ahead=[(u, 0, tw)])
            ex0, u1 = expand(0, u, u0, p, ahead=[(u, part, tw)])
            ex1, v0 = expand(1, u, u1, p, ahead=[(v, 0, tw)])
        bias = bias[None, :]
        out, oth0, v1 = input_grad(0, c0, c_o, ex0, v, v0, bias, g, None, width, [ex1, (grad_b, "h")], [(v, part, tw)])
        out, oth1, x_t0 = input_grad(1, c1, c_o, ex1, v, v1, bias, g, out, width, ahead=[(x_t, 0, part)])
        back0, back1 = trade(oth0), trade(oth1)
        grad_v, out, x_t1 = factor_grad("v_grad", 0, half, x_t0, g, None, (back0, out), ahead=[(x_t, part, part)], work=0)
        grad_v, out = factor_grad("v_grad", 1, half, x_t1, g, grad_v, (back1, out))
        return out, grad_u, grad_v, grad_b

    return jax.shard_map(
        local,
        mesh=mesh,
        in_specs=(
            P(("group", "batch"), "col"),
            P(("group", "batch"), "col"),
            P(("col", "batch"), None),
            P(("col", "batch"), None),
            P("col"),
        ),
        out_specs=(
            P(("group", "batch"), "col"),
            P(("group", "col", "batch"), None),
            P(("group", "col", "batch"), None),
            P(("group", "col", "batch")),
        ),
        check_vma=False,
    )
```

```python
import jax
import jax.numpy as jnp
from jax import lax
from jax.experimental import pallas as pl
from jax.experimental.pallas import tpu as pltpu
from jax.sharding import PartitionSpec as P

BF, F32 = jnp.bfloat16, jnp.float32
MIB = 1 << 20
NT = (((1,), (1,)), ((), ()))


class Place:
    def __getitem__(self, i):
        return lax.axis_index(("batch", "col")[i])


def call(body, name, ins, outs, scratch=(), flops=0, aliases=None, mib=4, after=(), us=0.3, carry=(), ahead=()):
    specs = {"v": pl.BlockSpec(memory_space=pltpu.VMEM), "h": pl.BlockSpec(memory_space=pl.ANY)}
    spaces = {"v": pltpu.VMEM, "h": pltpu.HBM}
    n_ins, n_ahead, n_outs, n_after = len(ins), len(ahead), len(outs), len(after)
    aliases = dict(aliases or {})
    aliases.update({n_ins + n_ahead + i: n_outs + n_ahead + i for i in range(len(carry))})
    ins = list(ins) + [(a, "h") for a, _, _ in ahead] + [(a, "v") for a in carry]
    ins += [a if isinstance(a, tuple) else (a, "v") for a in after]
    outs = list(outs) + [((rows, a.shape[1]), a.dtype, "v") for a, _, rows in ahead] + [(a.shape, a.dtype, "v") for a in carry]
    args = [pltpu.with_memory_space_constraint(a, spaces[w]) for a, w in ins]

    def whole(*refs):
        first = len(ins)
        sems = refs[-1] if n_ahead else None
        scratch_refs = refs[first + len(outs) : len(refs) - (n_ahead > 0)]
        fetches = [
            pltpu.make_async_copy(refs[n_ins + i].at[pl.ds(row, rows), :], refs[first + n_outs + i], sems.at[i])
            for i, (_, row, rows) in enumerate(ahead)
        ]
        body(Place(), *refs[:n_ins], *refs[first : first + n_outs], *scratch_refs, fetch=lambda: [f.start() for f in fetches])
        for f in fetches:
            f.wait()

    return pl.pallas_call(
        whole if n_ahead else lambda *refs: body(Place(), *refs[:n_ins], *refs[len(ins) : len(ins) + n_outs], *refs[len(ins) + len(outs) :]),
        out_shape=tuple(spaces[w](dims, dtype) for dims, dtype, w in outs),
        in_specs=[specs[w] for _, w in ins],
        out_specs=tuple(specs[w] for _, _, w in outs),
        scratch_shapes=list(scratch) + ([pltpu.SemaphoreType.DMA((n_ahead,))] if n_ahead else []),
        input_output_aliases=aliases,
        compiler_params=pltpu.CompilerParams(vmem_limit_bytes=mib * MIB),
        cost_estimate=pl.CostEstimate(flops=int(1.7 * flops + us * 1.15e9), bytes_accessed=0, transcendentals=0),
        name=name,
    )(*args)


def nothing():
    pass


def at_block(i, size):
    return pl.ds(pl.multiple_of(i * size, size), size)


def dma(n):
    return pltpu.SemaphoreType.DMA((n,))


def copy(src, dst, sem):
    return pltpu.make_async_copy(src, dst, sem)


def cut_half(x, half, after=()):
    rows = x.shape[0]
    n = 8
    step = rows // n

    def body(at_ref, x_ref, o_ref, sems):
        def cut(i):
            here = pl.ds(i * step, step)
            return copy(x_ref.at[here, at_block(1 - at_ref[0], half)], o_ref.at[here, :], sems.at[i])

        for i in range(n):
            cut(i).start()
        for i in range(n):
            cut(i).wait()

    return call(body, "cut_half", [(x, "h")], [((rows, half), BF, "v")], [dma(n)], us=2.2, after=after)[0]


VPARTS = 4


def project_own(x, v, after=()):
    rows, (half, rank) = x.shape[0], v.shape
    part = half // VPARTS
    tk = min(1024, part)
    n = half // tk
    each = part // tk

    def body(at_ref, x_ref, v_ref, p_ref, xv_ref, *refs):
        vv, (acc, x_sem, v_sem) = refs[:VPARTS], refs[VPARTS:]

        def x_copy(k):
            src = x_ref.at[:, pl.ds(pl.multiple_of(at_ref[0] * half + k * tk, tk), tk)]
            return copy(src, xv_ref.at[:, at_block(k, tk)], x_sem.at[k])

        def v_copy(k, i, j):
            return copy(v_ref.at[at_block(k, tk), :], vv[i].at[at_block(j, tk), :], v_sem.at[k])

        for k in range(n):
            x_copy(k).start()
            v_copy(k, k // each, k % each).start()
        acc[...] = jnp.zeros_like(acc)
        for i in range(VPARTS):

            @pl.loop(0, each)
            def _(j):
                k = i * each + j
                x_copy(k).wait()
                v_copy(k, i, j).wait()
                acc[...] += jnp.dot(xv_ref[:, at_block(k, tk)], vv[i][at_block(j, tk), :], preferred_element_type=F32)

        p_ref[...] = acc[...].astype(BF)

    return call(
        body,
        "project_own",
        [(x, "h"), (v, "h")],
        [((rows, rank), BF, "v"), ((rows, half), BF, "v")] + [((part, rank), BF, "v")] * VPARTS,
        [pltpu.VMEM((rows, rank), F32)] + [dma(n)] * 2,
        flops=2 * rows * half * rank,
        mib=8,
        after=after,
    )


def write_halves(at_ref, total, outs):
    if len(outs) == 1:
        outs[0][...] = total(slice(None))
        return
    each = outs[0].shape[0]
    bit = at_ref[1] & 1
    for i, o_ref in ((bit, outs[0]), (1 - bit, outs[1])):
        o_ref[...] = total(at_block(i, each)).astype(o_ref.dtype)


def halves_of(rows, rank, direct):
    return [((rows // 2, rank), F32, "v"), ((rows // 2, rank), BF, "v")] if direct else [((rows, rank), F32, "v")]


def project_other(x_o, vs, theirs, c, u, direct):
    rows, half = x_o.shape
    tk, rank = vs[0].shape
    first = half // 2

    def body(at_ref, x_ref, t_ref, c_ref, *refs, fetch):
        vv, outs, cv_ref, acc, c_sem = refs[:VPARTS], refs[VPARTS:-3], refs[-3], refs[-2], refs[-1]
        first_c = copy(c_ref.at[:, at_block(2 * at_ref[0], first)], cv_ref, c_sem.at[0])
        fetch()
        first_c.start()
        for k in range(VPARTS):
            part = jnp.dot(x_ref[:, k * tk : (k + 1) * tk], vv[k][...], preferred_element_type=F32)
            acc[...] = part + (acc[...] if k else t_ref[...].astype(F32))
        write_halves(at_ref, lambda here: acc[here, :], outs)
        first_c.wait()

    return call(
        body,
        "project_other",
        [(x_o, "v"), (theirs, "v"), (c, "h")] + [(a, "v") for a in vs],
        halves_of(rows, rank, direct) + [((rows, first), BF, "v")],
        [pltpu.VMEM((rows, rank), F32), dma(1)],
        flops=2 * rows * half * rank,
        mib=6,
        ahead=[(u, 0, first // 4)],
    )


def hidden(c, x):
    return (c.astype(F32) * x.astype(F32)).astype(BF)


def back_project(lo, n, x, x_o, c, c_o, u, u_first, so_far, c_all=None, after=()):
    rows, (half, rank) = x.shape[0], u.shape
    part = c.shape[1]
    tk = u_first.shape[0]
    shift = lo * tk % part
    first, last = so_far is None, (lo + n) * tk == half

    def body(at_ref, x_ref, xo_ref, c_ref, co_ref, u_ref, uf_ref, *refs, fetch=nothing):
        if first:
            all_ref, acc_ref, b_ref, next_ref, uv, h, u_sem, c_sem = refs
            src = all_ref.at[:, pl.ds(pl.multiple_of(at_ref[0] * half + part, part), part)]
            next_c = copy(src, next_ref, c_sem.at[0])
        elif last:
            so_ref, own_ref, oth_ref, b_ref, uv, h, u_sem = refs
        else:
            so_ref, acc_ref, b_ref, uv, h, u_sem = refs

        def u_copy(k):
            return copy(u_ref.at[pl.ds((lo + k) * tk, tk), :], uv.at[k - 1], u_sem.at[k - 1])

        for k in range(1, n):
            u_copy(k).start()
        if first:
            next_c.start()
        fetch()
        for k in range(n):
            here = pl.ds(k * tk, tk)
            there = pl.ds((lo + k) * tk, tk)
            own = hidden(c_ref[:, pl.ds(shift + k * tk, tk)], x_ref[:, there])
            oth = hidden(co_ref[:, there], xo_ref[:, there])
            h[k, :rows, :] = own
            h[k, rows:, :] = oth
            b_ref[:, here] = jnp.sum(own.astype(F32), axis=0, keepdims=True) + jnp.sum(oth.astype(F32), axis=0, keepdims=True)

        @pl.loop(0, 2)
        def _(i):
            at_rows = at_block(i, rows)
            total = None if first else so_ref[at_rows, :]
            for k in range(n):
                if k:

                    @pl.when(i == 0)
                    def _():
                        u_copy(k).wait()

                term = jnp.dot(h[k, at_rows, :], uv[k - 1] if k else uf_ref[...], preferred_element_type=F32)
                total = term if total is None else total + term
            if not last:
                acc_ref[at_rows, :] = total
            else:

                @pl.when(i == 0)
                def _():
                    own_ref[...] = total.astype(BF)

                @pl.when(i == 1)
                def _():
                    oth_ref[...] = total

        if first:
            next_c.wait()

    outs = [((rows, rank), BF, "v"), ((rows, rank), F32, "v")] if last else [((2 * rows, rank), F32, "v")]
    outs += [((1, n * tk), F32, "v")] + ([((rows, part), BF, "v")] if first else [])
    return call(
        body,
        "back_project",
        [(x, "v"), (x_o, "v"), (c, "v"), (c_o, "v"), (u, "h"), (u_first, "v"), (c_all, "h") if first else (so_far, "v")],
        outs,
        [pltpu.VMEM((max(1, n - 1), tk, rank), BF), pltpu.VMEM((n, 2 * rows, tk), BF), dma(max(1, n - 1))]
        + ([dma(1)] if first else []),
        flops=4 * rows * n * tk * rank,
        mib=15 if first else 12,
        after=after,
        ahead=[] if last else [(u, (lo + n) * tk, tk)],
    )


def turn_x(x, x_o, after=()):
    rows, half = x.shape
    tw = min(512, half)
    n = half // tw

    def body(at_ref, x_ref, xo_ref, o_ref, stage, sems):
        def out(k):
            here = at_block(k, tw)
            return copy(stage.at[here, :], o_ref.at[here, :], sems.at[k])

        @pl.loop(0, n)
        def _(k):
            here = at_block(k, tw)
            stage[here, :rows] = x_ref[:, here].T
            stage[here, rows:] = xo_ref[:, here].T
            out(k).start()

        @pl.loop(0, n)
        def _(k):
            out(k).wait()

    return call(
        body,
        "turn_x",
        [(x, "v"), (x_o, "v")],
        [((half, 2 * rows), BF, "h")],
        [pltpu.VMEM((half, 2 * rows), BF), dma(n)],
        after=after,
        us=3.6,
        mib=12,
    )[0]


def turn_hidden(s, x, x_o, c, c_o, after=(), carry=()):
    rows, half = x.shape
    part = half // 2
    tw = min(512, part)

    def body(at_ref, x_ref, xo_ref, c_ref, co_ref, o_ref):
        @pl.loop(0, part // tw)
        def _(k):
            here = at_block(k, tw)
            there = pl.ds(pl.multiple_of(s * part + k * tw, tw), tw)
            o_ref[here, :rows] = hidden(c_ref[:, here], x_ref[:, there]).T
            o_ref[here, rows:] = hidden(co_ref[:, there], xo_ref[:, there]).T

    return call(
        body,
        "turn_hidden",
        [(a, "v") for a in (x, x_o, c, c_o)],
        [((part, 2 * rows), BF, "v")],
        mib=6,
        after=after,
        us=1.8,
        carry=carry,
    )


def fill(at_ref, both, refs):
    if len(refs) == 2:
        rows = refs[0].shape[0]
        both[:rows, :] = refs[0][...]
        both[rows:, :] = refs[1][...]
        return
    each = refs[0].shape[0]
    bit = at_ref[1] & 1
    for i, (keep, other) in enumerate((refs[:2], refs[2:])):
        both[at_block(2 * i + bit, each), :] = keep[...]
        both[at_block(2 * i + 1 - bit, each), :] = other[...]


def factor_grad(name, s, half, turned, p, so_far, placed=None, after=(), ahead=(), work=1):
    rows2, rank = turned.shape[1], p[0].shape[1]
    part = half // 2
    tw = min(512, part // 2)
    n = part // tw
    np_ = len(p)
    recv, full = ([placed[0]], placed[1]) if placed else ((), None)
    nr = len(recv)
    ins = [(turned, "v")] + [(a, "v") for a in p]
    aliases = {}
    if so_far is not None:
        aliases[len(ins)] = 0
        ins.append((so_far, "h"))
    if placed:
        ins += [(a, "v") for a in recv]
        aliases[len(ins)] = 1
        ins.append((full, "h"))

    def body(at_ref, t_ref, *refs, fetch=nothing):
        p_refs, refs = refs[:np_], refs[np_ + (so_far is not None) :]
        r_refs, refs = refs[:nr], refs[nr + (nr > 0) :]
        o_ref, refs = refs[0], refs[1:]
        if nr:
            f_ref, refs = refs[0], refs[1:]
        stage, both, sems, put_sem = refs

        def put(i):
            w = recv[i].shape[1]
            there = pl.ds(pl.multiple_of((1 - at_ref[0]) * half + s * w, w), w)
            return copy(r_refs[i], f_ref.at[:, there], put_sem.at[i])

        def out(k):
            slot = lax.rem(k, 4)
            there = pl.ds(pl.multiple_of(s * part + k * tw, tw), tw)
            return copy(stage.at[slot], o_ref.at[there, :], sems.at[slot])

        fetch()
        for i in range(nr):
            put(i).start()
        fill(at_ref, both, p_refs)

        @pl.loop(0, n // 2)
        def _(kk):
            @pl.when(kk >= 2)
            def _():
                out(2 * kk - 4).wait()
                out(2 * kk - 3).wait()

            for i in range(2):
                k = 2 * kk + i
                stage[lax.rem(k, 4)] = jnp.dot(t_ref[at_block(k, tw), :], both[...], preferred_element_type=F32).astype(BF)
                out(k).start()

        for k in range(max(0, n - 4), n):
            out(k).wait()
        for i in range(nr):
            put(i).wait()

    outs = [((half, rank), BF, "h")] + ([(full.shape, BF, "h")] if placed else [])
    return call(
        body,
        name,
        ins,
        outs,
        [pltpu.VMEM((4, tw, rank), BF), pltpu.VMEM((rows2, rank), BF), dma(4), dma(max(1, nr))],
        flops=work * rows2 * half * rank,
        aliases=aliases,
        mib=12,
        after=after,
        ahead=ahead,
    )


def expand(s, u, u_first, p, after=(), ahead=()):
    half, rank = u.shape
    rows2 = sum(a.shape[0] for a in p)
    part = half // 2
    tw = u_first.shape[0]
    n = part // tw

    def body(at_ref, u_ref, uf_ref, *refs, fetch=nothing):
        o_ref, uv, both, u_sem = refs[len(p) :]

        def u_copy(k):
            src = u_ref.at[pl.ds(pl.multiple_of(s * part + k * tw, tw), tw), :]
            return copy(src, uv.at[k - 1], u_sem.at[k - 1])

        for k in range(1, n):
            u_copy(k).start()
        fetch()
        fill(at_ref, both, refs[: len(p)])
        o_ref[:, :tw] = lax.dot_general(both[...], uf_ref[...], NT, preferred_element_type=F32)

        @pl.loop(1, n)
        def _(k):
            u_copy(k).wait()
            o_ref[:, at_block(k, tw)] = lax.dot_general(both[...], uv[k - 1], NT, preferred_element_type=F32)

    return call(
        body,
        "expand",
        [(u, "h"), (u_first, "v")] + [(a, "v") for a in p],
        [((rows2, part), F32, "v")],
        [pltpu.VMEM((max(1, n - 1), tw, rank), BF), pltpu.VMEM((rows2, rank), BF), dma(max(1, n - 1))],
        flops=rows2 * half * rank,
        mib=11,
        after=after,
        ahead=ahead,
    )


def input_grad(s, c, c_o, ex, v, v_first, bias, g, so_far, width, after=(), ahead=()):
    rows, half = c_o.shape
    rank = v.shape[1]
    part = half // 2
    tw = v_first.shape[0]
    n = part // tw
    slots = max(1, min(2, n - 1))
    ng = len(g)

    def body(at_ref, c_ref, co_ref, ex_ref, v_ref, vf_ref, b_ref, *refs, fetch=nothing):
        g_refs, refs = refs[:ng], refs[ng + (so_far is not None) :]
        own_ref, oth_ref, stage, vv, both, sems, v_sem = refs

        def v_copy(k):
            src = v_ref.at[pl.ds(pl.multiple_of(s * part + k * tw, tw), tw), :]
            slot = lax.rem(k - 1, slots)
            return copy(src, vv.at[slot], v_sem.at[slot])

        def columns(k):
            return pl.ds(pl.multiple_of(at_ref[0] * half + s * part + k * tw, tw), tw)

        def out(k):
            slot = lax.rem(k, 2)
            return copy(stage.at[slot], own_ref.at[:, columns(k)], sems.at[slot])

        def block(k, v_block):
            here = at_block(k, tw)
            there = pl.ds(pl.multiple_of(s * part + k * tw, tw), tw)
            bk = lax.dot_general(both[...], v_block, NT, preferred_element_type=F32)
            b = b_ref[:, columns(k)].astype(F32)
            cf, cof = c_ref[:, here].astype(F32), co_ref[:, there].astype(F32)
            stage[lax.rem(k, 2)] = (cf * (ex_ref[:rows, here] + b) + cf + bk[:rows]).astype(BF)
            oth_ref[:, here] = (cof * (ex_ref[rows:, here] + b) + cof + bk[rows:]).astype(BF)
            out(k).start()

        for k in range(1, min(n, slots + 1)):
            v_copy(k).start()
        fetch()
        fill(at_ref, both, g_refs)
        block(0, vf_ref[...])

        @pl.loop(1, n)
        def _(k):
            v_copy(k).wait()

            @pl.when(k >= 2)
            def _():
                out(k - 2).wait()

            block(k, vv[lax.rem(k - 1, slots)])

            @pl.when(k + slots < n)
            def _():
                v_copy(k + slots).start()

        for k in range(max(0, n - 2), n):
            out(k).wait()

    ins = [(c, "v"), (c_o, "v"), (ex, "v"), (v, "h"), (v_first, "v"), (bias, "v")] + [(a, "v") for a in g]
    aliases = {}
    if so_far is not None:
        aliases = {len(ins): 0}
        ins.append((so_far, "h"))
    return call(
        body,
        "input_grad",
        ins,
        [((rows, width), BF, "h"), ((rows, part), BF, "v")],
        [
            pltpu.VMEM((2, rows, tw), BF),
            pltpu.VMEM((slots, tw, rank), BF),
            pltpu.VMEM((2 * rows, rank), BF),
            dma(2),
            dma(slots),
        ],
        flops=2 * rows * half * rank,
        aliases=aliases,
        mib=13,
        after=after,
        ahead=ahead,
    )


def plus(a, b):
    return a.astype(F32) + b.astype(F32)


def pair_halves(a, b, direct, after=()):
    rows, rank = a.shape

    def body(at_ref, a_ref, b_ref, *outs):
        write_halves(at_ref, lambda here: plus(a_ref[here, :], b_ref[here, :]), outs)

    return call(body, "pair_halves", [(a, "v"), (b, "v")], halves_of(rows, rank, direct), after=after)


def pieces_of(a, b, m, after=(), carry=()):
    rows, rank = a.shape
    each = rows // m

    def body(at_ref, a_ref, b_ref, *outs):
        for d in range(m):
            here = at_block((at_ref[1] >> 1) ^ d, each)
            outs[d][...] = plus(a_ref[here, :], b_ref[here, :]).astype(outs[d].dtype)

    return call(body, "pieces_of", [(a, "v"), (b, "v")], [((each, rank), F32 if d == 0 else BF, "v") for d in range(m)], after=after, carry=carry)


def add_pieces(parts, after=(), carry=()):
    def body(at_ref, *refs):
        total = refs[0][...].astype(F32)
        for r in refs[1:-1]:
            total += r[...].astype(F32)
        refs[-1][...] = total.astype(BF)

    return call(body, "add_pieces", [(a, "v") for a in parts], [(parts[0].shape, BF, "v")], after=after, carry=carry)


def join_pieces(parts, after=(), carry=()):
    m = len(parts)
    each, rank = parts[0].shape

    def body(at_ref, *refs):
        for d in range(m):
            refs[-1][at_block((at_ref[1] >> 1) ^ d, each), :] = refs[d][...]

    return call(body, "join_pieces", [(a, "v") for a in parts], [((m * each, rank), BF, "v")], after=after, carry=carry)


def hold(a, after):
    def body(at_ref, a_ref, o_ref):
        pass

    return call(body, "hold", [(a, "v")], [(a.shape, a.dtype, "v")], aliases={0: 0}, after=after)[0]


def solution(mesh):
    n = mesh.shape["col"]
    m = n // 2
    swap = [(0, 1), (1, 0)]

    def trade(a):
        return lax.ppermute(a, "batch", swap)

    def to(a, d):
        return lax.ppermute(a, "col", [(i, i ^ d) for i in range(n)])

    def spread(parts):
        return [parts[0]] + [to(parts[d], 2 * d) for d in range(1, m)]

    def local(x, c, u, v, bias):
        half, width = u.shape[0], x.shape[1]
        direct = x.shape[0] % (16 * n) == 0 and n & (n - 1) == 0 and n > 2

        def plain(total):
            total = lax.psum(total, "col").astype(BF)
            return [trade(total), total]

        part = half // 2
        tw = min(1024, part)
        x_s = cut_half(x, half)
        x_o = trade(x_s)
        own, x_own, *v_in = project_own(x, v, [x_s])
        theirs = trade(own)
        c_o = trade(hold(cut_half(c, half, [own]), [theirs]))
        *sums, c0, u0 = project_other(x_o, v_in, theirs, c, u, direct)
        acc, b0, c1, u1 = back_project(0, 4, x_own, x_o, c0, c_o, u, u0, None, c)
        if direct:
            parts = pieces_of(sums[0], to(sums[1], 1), m, [acc])
            acc, b1, u1 = back_project(4, 2, x_own, x_o, c1, c_o, u, u1, acc, after=[parts[0]])
            (h_t0,) = turn_hidden(0, x_own, x_o, c0, c_o, [acc])
            (total,) = add_pieces(spread(parts), [h_t0])
            own_g, mine_g, b2 = back_project(6, 2, x_own, x_o, c1, c_o, u, u1, acc, after=[total])
            (h_t1,) = turn_hidden(1, x_own, x_o, c1, c_o, [mine_g])
            half_p, own_g = join_pieces(spread([total] * m), [h_t1], [own_g])
            other_p = to(half_p, 1)
            x_t = turn_x(x_own, x_o, [half_p])
            sums_g = pair_halves(mine_g, trade(own_g), direct, [(x_t, "h")])
            other_p = hold(other_p, [(x_t, "h")])
            grad_b = jnp.concatenate([b0[0], b1[0], b2[0]])
            p = [trade(half_p), trade(other_p), half_p, other_p]
            (grad_u,) = factor_grad("u_grad", 0, half, h_t0, p, None, after=[(x_t, "h")])
            parts_g = pieces_of(sums_g[0], to(sums_g[1], 1), m, [(grad_u, "h")])
            grad_u, u0 = factor_grad("u_grad", 1, half, h_t1, p, grad_u, after=[parts_g[0]], ahead=[(u, 0, tw)])
            (total_g,) = add_pieces(spread(parts_g), [(grad_u, "h")])
            ex0, u1 = expand(0, u, u0, p, [total_g], [(u, part, tw)])
            (half_g,) = join_pieces(spread([total_g] * m), [ex0])
            other_g = to(half_g, 1)
            ex1, v0 = expand(1, u, u1, p, [half_g], [(v, 0, tw)])
            other_g = hold(other_g, [ex1])
            g = [trade(half_g), trade(other_g), half_g, other_g]
        else:
            acc, b1, u1 = back_project(4, 2, x_own, x_o, c1, c_o, u, u1, acc)
            own_g, mine_g, b2 = back_project(6, 2, x_own, x_o, c1, c_o, u, u1, acc)
            (sums_g,) = pair_halves(mine_g, trade(own_g), direct)
            p, g = plain(sums[0]), plain(sums_g)
            grad_b = jnp.concatenate([b0[0], b1[0], b2[0]])
            x_t = turn_x(x_own, x_o)
            (h_t0,) = turn_hidden(0, x_own, x_o, c0, c_o)
            (h_t1,) = turn_hidden(1, x_own, x_o, c1, c_o)
            (grad_u,) = factor_grad("u_grad", 0, half, h_t0, p, None)
            grad_u, u0 = factor_grad("u_grad", 1, half, h_t1, p, grad_u, ahead=[(u, 0, tw)])
            ex0, u1 = expand(0, u, u0, p, ahead=[(u, part, tw)])
            ex1, v0 = expand(1, u, u1, p, ahead=[(v, 0, tw)])
        bias = bias[None, :]
        out, oth0, v1 = input_grad(0, c0, c_o, ex0, v, v0, bias, g, None, width, [ex1, (grad_b, "h")], [(v, part, tw)])
        out, oth1, x_t0 = input_grad(1, c1, c_o, ex1, v, v1, bias, g, out, width, ahead=[(x_t, 0, part)])
        back0, back1 = trade(oth0), trade(oth1)
        grad_v, out, x_t1 = factor_grad("v_grad", 0, half, x_t0, g, None, (back0, out), ahead=[(x_t, part, part)], work=0)
        grad_v, out = factor_grad("v_grad", 1, half, x_t1, g, grad_v, (back1, out))
        return out, grad_u, grad_v, grad_b

    return jax.shard_map(
        local,
        mesh=mesh,
        in_specs=(
            P(("group", "batch"), "col"),
            P(("group", "batch"), "col"),
            P(("col", "batch"), None),
            P(("col", "batch"), None),
            P("col"),
        ),
        out_specs=(
            P(("group", "batch"), "col"),
            P(("group", "col", "batch"), None),
            P(("group", "col", "batch"), None),
            P(("group", "col", "batch")),
        ),
        check_vma=False,
    )
```

```python
import jax
import jax.numpy as jnp
from jax import lax
from jax.experimental import pallas as pl
from jax.experimental.pallas import tpu as pltpu
from jax.sharding import PartitionSpec as P

BF, F32 = jnp.bfloat16, jnp.float32
MIB = 1 << 20
NT = (((1,), (1,)), ((), ()))


class Place:
    def __getitem__(self, i):
        return lax.axis_index(("batch", "col")[i])


def call(body, name, ins, outs, scratch=(), flops=0, aliases=None, mib=4, after=(), us=0.3, carry=(), ahead=()):
    specs = {"v": pl.BlockSpec(memory_space=pltpu.VMEM), "h": pl.BlockSpec(memory_space=pl.ANY)}
    spaces = {"v": pltpu.VMEM, "h": pltpu.HBM}
    n_ins, n_ahead, n_outs, n_after = len(ins), len(ahead), len(outs), len(after)
    aliases = dict(aliases or {})
    aliases.update({n_ins + n_ahead + i: n_outs + n_ahead + i for i in range(len(carry))})
    ins = list(ins) + [(a, "h") for a, _, _ in ahead] + [(a, "v") for a in carry]
    ins += [a if isinstance(a, tuple) else (a, "v") for a in after]
    outs = list(outs) + [((rows, a.shape[1]), a.dtype, "v") for a, _, rows in ahead] + [(a.shape, a.dtype, "v") for a in carry]
    args = [pltpu.with_memory_space_constraint(a, spaces[w]) for a, w in ins]

    def whole(*refs):
        first = len(ins)
        sems = refs[-1] if n_ahead else None
        scratch_refs = refs[first + len(outs) : len(refs) - (n_ahead > 0)]
        fetches = [
            pltpu.make_async_copy(refs[n_ins + i].at[pl.ds(row, rows), :], refs[first + n_outs + i], sems.at[i])
            for i, (_, row, rows) in enumerate(ahead)
        ]
        body(Place(), *refs[:n_ins], *refs[first : first + n_outs], *scratch_refs, fetch=lambda: [f.start() for f in fetches])
        for f in fetches:
            f.wait()

    return pl.pallas_call(
        whole if n_ahead else lambda *refs: body(Place(), *refs[:n_ins], *refs[len(ins) : len(ins) + n_outs], *refs[len(ins) + len(outs) :]),
        out_shape=tuple(spaces[w](dims, dtype) for dims, dtype, w in outs),
        in_specs=[specs[w] for _, w in ins],
        out_specs=tuple(specs[w] for _, _, w in outs),
        scratch_shapes=list(scratch) + ([pltpu.SemaphoreType.DMA((n_ahead,))] if n_ahead else []),
        input_output_aliases=aliases,
        compiler_params=pltpu.CompilerParams(vmem_limit_bytes=mib * MIB),
        cost_estimate=pl.CostEstimate(flops=int(1.7 * flops + us * 1.15e9), bytes_accessed=0, transcendentals=0),
        name=name,
    )(*args)


def nothing():
    pass


def at_block(i, size):
    return pl.ds(pl.multiple_of(i * size, size), size)


def dma(n):
    return pltpu.SemaphoreType.DMA((n,))


def copy(src, dst, sem):
    return pltpu.make_async_copy(src, dst, sem)


def cut_half(x, half, after=()):
    rows = x.shape[0]
    n = 8
    step = rows // n

    def body(at_ref, x_ref, o_ref, sems):
        def cut(i):
            here = pl.ds(i * step, step)
            return copy(x_ref.at[here, at_block(1 - at_ref[0], half)], o_ref.at[here, :], sems.at[i])

        for i in range(n):
            cut(i).start()
        for i in range(n):
            cut(i).wait()

    return call(body, "cut_half", [(x, "h")], [((rows, half), BF, "v")], [dma(n)], us=2.2, after=after)[0]


VPARTS = 4


def project_own(x, v, after=()):
    rows, (half, rank) = x.shape[0], v.shape
    part = half // VPARTS
    tk = min(1024, part)
    n = half // tk
    each = part // tk

    def body(at_ref, x_ref, v_ref, p_ref, xv_ref, *refs):
        vv, (acc, x_sem, v_sem) = refs[:VPARTS], refs[VPARTS:]

        def x_copy(k):
            src = x_ref.at[:, pl.ds(pl.multiple_of(at_ref[0] * half + k * tk, tk), tk)]
            return copy(src, xv_ref.at[:, at_block(k, tk)], x_sem.at[k])

        def v_copy(k, i, j):
            return copy(v_ref.at[at_block(k, tk), :], vv[i].at[at_block(j, tk), :], v_sem.at[k])

        for k in range(n):
            x_copy(k).start()
            v_copy(k, k // each, k % each).start()
        acc[...] = jnp.zeros_like(acc)
        for i in range(VPARTS):

            @pl.loop(0, each)
            def _(j):
                k = i * each + j
                x_copy(k).wait()
                v_copy(k, i, j).wait()
                acc[...] += jnp.dot(xv_ref[:, at_block(k, tk)], vv[i][at_block(j, tk), :], preferred_element_type=F32)

        p_ref[...] = acc[...].astype(BF)

    return call(
        body,
        "project_own",
        [(x, "h"), (v, "h")],
        [((rows, rank), BF, "v"), ((rows, half), BF, "v")] + [((part, rank), BF, "v")] * VPARTS,
        [pltpu.VMEM((rows, rank), F32)] + [dma(n)] * 2,
        flops=2 * rows * half * rank,
        mib=8,
        after=after,
    )


def write_halves(at_ref, total, outs):
    if len(outs) == 1:
        outs[0][...] = total(slice(None))
        return
    each = outs[0].shape[0]
    bit = at_ref[1] & 1
    for i, o_ref in ((bit, outs[0]), (1 - bit, outs[1])):
        o_ref[...] = total(at_block(i, each)).astype(o_ref.dtype)


def halves_of(rows, rank, direct):
    return [((rows // 2, rank), F32, "v"), ((rows // 2, rank), BF, "v")] if direct else [((rows, rank), F32, "v")]


def project_other(x_o, vs, theirs, c, u, direct):
    rows, half = x_o.shape
    tk, rank = vs[0].shape
    first = half // 2

    def body(at_ref, x_ref, t_ref, c_ref, *refs, fetch):
        vv, outs, cv_ref, acc, c_sem = refs[:VPARTS], refs[VPARTS:-3], refs[-3], refs[-2], refs[-1]
        first_c = copy(c_ref.at[:, at_block(2 * at_ref[0], first)], cv_ref, c_sem.at[0])
        fetch()
        first_c.start()
        for k in range(VPARTS):
            part = jnp.dot(x_ref[:, k * tk : (k + 1) * tk], vv[k][...], preferred_element_type=F32)
            acc[...] = part + (acc[...] if k else t_ref[...].astype(F32))
        write_halves(at_ref, lambda here: acc[here, :], outs)
        first_c.wait()

    return call(
        body,
        "project_other",
        [(x_o, "v"), (theirs, "v"), (c, "h")] + [(a, "v") for a in vs],
        halves_of(rows, rank, direct) + [((rows, first), BF, "v")],
        [pltpu.VMEM((rows, rank), F32), dma(1)],
        flops=2 * rows * half * rank,
        mib=6,
        ahead=[(u, 0, first // 4)],
    )


def hidden(c, x):
    return (c.astype(F32) * x.astype(F32)).astype(BF)


def back_project(lo, n, x, x_o, c, c_o, u, u_first, so_far, c_all=None, after=()):
    rows, (half, rank) = x.shape[0], u.shape
    part = c.shape[1]
    tk = u_first.shape[0]
    shift = lo * tk % part
    first, last = so_far is None, (lo + n) * tk == half

    def body(at_ref, x_ref, xo_ref, c_ref, co_ref, u_ref, uf_ref, *refs, fetch=nothing):
        if first:
            all_ref, acc_ref, b_ref, next_ref, uv, h, u_sem, c_sem = refs
            src = all_ref.at[:, pl.ds(pl.multiple_of(at_ref[0] * half + part, part), part)]
            next_c = copy(src, next_ref, c_sem.at[0])
        elif last:
            so_ref, own_ref, oth_ref, b_ref, uv, h, u_sem = refs
        else:
            so_ref, acc_ref, b_ref, uv, h, u_sem = refs

        def u_copy(k):
            return copy(u_ref.at[pl.ds((lo + k) * tk, tk), :], uv.at[k - 1], u_sem.at[k - 1])

        for k in range(1, n):
            u_copy(k).start()
        if first:
            next_c.start()
        fetch()
        for k in range(n):
            here = pl.ds(k * tk, tk)
            there = pl.ds((lo + k) * tk, tk)
            own = hidden(c_ref[:, pl.ds(shift + k * tk, tk)], x_ref[:, there])
            oth = hidden(co_ref[:, there], xo_ref[:, there])
            h[k, :rows, :] = own
            h[k, rows:, :] = oth
            b_ref[:, here] = jnp.sum(own.astype(F32), axis=0, keepdims=True) + jnp.sum(oth.astype(F32), axis=0, keepdims=True)

        @pl.loop(0, 2)
        def _(i):
            at_rows = at_block(i, rows)
            total = None if first else so_ref[at_rows, :]
            for k in range(n):
                if k:

                    @pl.when(i == 0)
                    def _():
                        u_copy(k).wait()

                term = jnp.dot(h[k, at_rows, :], uv[k - 1] if k else uf_ref[...], preferred_element_type=F32)
                total = term if total is None else total + term
            if not last:
                acc_ref[at_rows, :] = total
            else:

                @pl.when(i == 0)
                def _():
                    own_ref[...] = total.astype(BF)

                @pl.when(i == 1)
                def _():
                    oth_ref[...] = total

        if first:
            next_c.wait()

    outs = [((rows, rank), BF, "v"), ((rows, rank), F32, "v")] if last else [((2 * rows, rank), F32, "v")]
    outs += [((1, n * tk), F32, "v")] + ([((rows, part), BF, "v")] if first else [])
    return call(
        body,
        "back_project",
        [(x, "v"), (x_o, "v"), (c, "v"), (c_o, "v"), (u, "h"), (u_first, "v"), (c_all, "h") if first else (so_far, "v")],
        outs,
        [pltpu.VMEM((max(1, n - 1), tk, rank), BF), pltpu.VMEM((n, 2 * rows, tk), BF), dma(max(1, n - 1))]
        + ([dma(1)] if first else []),
        flops=4 * rows * n * tk * rank,
        mib=15 if first else 12,
        after=after,
        ahead=[] if last else [(u, (lo + n) * tk, tk)],
    )


def turn_x(x, x_o, after=()):
    rows, half = x.shape
    tw = min(512, half)
    n = half // tw

    def body(at_ref, x_ref, xo_ref, o_ref, stage, sems):
        def out(k):
            here = at_block(k, tw)
            return copy(stage.at[here, :], o_ref.at[here, :], sems.at[k])

        @pl.loop(0, n)
        def _(k):
            here = at_block(k, tw)
            stage[here, :rows] = x_ref[:, here].T
            stage[here, rows:] = xo_ref[:, here].T
            out(k).start()

        @pl.loop(0, n)
        def _(k):
            out(k).wait()

    return call(
        body,
        "turn_x",
        [(x, "v"), (x_o, "v")],
        [((half, 2 * rows), BF, "h")],
        [pltpu.VMEM((half, 2 * rows), BF), dma(n)],
        after=after,
        us=3.6,
        mib=12,
    )[0]


def turn_hidden(s, x, x_o, c, c_o, after=(), carry=()):
    rows, half = x.shape
    part = half // 2
    tw = min(512, part)

    def body(at_ref, x_ref, xo_ref, c_ref, co_ref, o_ref):
        @pl.loop(0, part // tw)
        def _(k):
            here = at_block(k, tw)
            there = pl.ds(pl.multiple_of(s * part + k * tw, tw), tw)
            o_ref[here, :rows] = hidden(c_ref[:, here], x_ref[:, there]).T
            o_ref[here, rows:] = hidden(co_ref[:, there], xo_ref[:, there]).T

    return call(
        body,
        "turn_hidden",
        [(a, "v") for a in (x, x_o, c, c_o)],
        [((part, 2 * rows), BF, "v")],
        mib=6,
        after=after,
        us=1.8,
        carry=carry,
    )


def fill(at_ref, both, refs):
    if len(refs) == 2:
        rows = refs[0].shape[0]
        both[:rows, :] = refs[0][...]
        both[rows:, :] = refs[1][...]
        return
    each = refs[0].shape[0]
    bit = at_ref[1] & 1
    for i, (keep, other) in enumerate((refs[:2], refs[2:])):
        both[at_block(2 * i + bit, each), :] = keep[...]
        both[at_block(2 * i + 1 - bit, each), :] = other[...]


def factor_grad(name, s, half, turned, p, so_far, placed=None, after=(), ahead=(), work=1):
    rows2, rank = turned.shape[1], p[0].shape[1]
    part = half // 2
    tw = min(256, part // 2)
    n = part // tw
    group = min(4, n)
    slots = 2 * group
    np_ = len(p)
    recv, full = ([placed[0]], placed[1]) if placed else ((), None)
    nr = len(recv)
    ins = [(turned, "v")] + [(a, "v") for a in p]
    aliases = {}
    if so_far is not None:
        aliases[len(ins)] = 0
        ins.append((so_far, "h"))
    if placed:
        ins += [(a, "v") for a in recv]
        aliases[len(ins)] = 1
        ins.append((full, "h"))

    def body(at_ref, t_ref, *refs, fetch=nothing):
        p_refs, refs = refs[:np_], refs[np_ + (so_far is not None) :]
        r_refs, refs = refs[:nr], refs[nr + (nr > 0) :]
        o_ref, refs = refs[0], refs[1:]
        if nr:
            f_ref, refs = refs[0], refs[1:]
        stage, both, sems, put_sem = refs

        def put(i):
            w = recv[i].shape[1]
            there = pl.ds(pl.multiple_of((1 - at_ref[0]) * half + s * w, w), w)
            return copy(r_refs[i], f_ref.at[:, there], put_sem.at[i])

        def out(k):
            slot = lax.rem(k, slots)
            there = pl.ds(pl.multiple_of(s * part + k * tw, tw), tw)
            return copy(stage.at[slot], o_ref.at[there, :], sems.at[slot])

        fetch()
        for i in range(nr):
            put(i).start()
        fill(at_ref, both, p_refs)

        @pl.loop(0, n // group)
        def _(kk):
            @pl.when(kk >= 2)
            def _():
                for i in range(group):
                    out(group * kk + i - slots).wait()

            for i in range(group):
                k = group * kk + i
                stage[lax.rem(k, slots)] = jnp.dot(t_ref[at_block(k, tw), :], both[...], preferred_element_type=F32).astype(BF)
                out(k).start()

        for k in range(max(0, n - slots), n):
            out(k).wait()
        for i in range(nr):
            put(i).wait()

    outs = [((half, rank), BF, "h")] + ([(full.shape, BF, "h")] if placed else [])
    return call(
        body,
        name,
        ins,
        outs,
        [pltpu.VMEM((slots, tw, rank), BF), pltpu.VMEM((rows2, rank), BF), dma(slots), dma(max(1, nr))],
        flops=work * rows2 * half * rank,
        aliases=aliases,
        mib=12,
        after=after,
        ahead=ahead,
    )


def expand(s, u, u_first, p, after=(), ahead=()):
    half, rank = u.shape
    rows2 = sum(a.shape[0] for a in p)
    part = half // 2
    tw = u_first.shape[0]
    n = part // tw

    def body(at_ref, u_ref, uf_ref, *refs, fetch=nothing):
        o_ref, uv, both, u_sem = refs[len(p) :]

        def u_copy(k):
            src = u_ref.at[pl.ds(pl.multiple_of(s * part + k * tw, tw), tw), :]
            return copy(src, uv.at[k - 1], u_sem.at[k - 1])

        for k in range(1, n):
            u_copy(k).start()
        fetch()
        fill(at_ref, both, refs[: len(p)])
        o_ref[:, :tw] = lax.dot_general(both[...], uf_ref[...], NT, preferred_element_type=F32)

        @pl.loop(1, n)
        def _(k):
            u_copy(k).wait()
            o_ref[:, at_block(k, tw)] = lax.dot_general(both[...], uv[k - 1], NT, preferred_element_type=F32)

    return call(
        body,
        "expand",
        [(u, "h"), (u_first, "v")] + [(a, "v") for a in p],
        [((rows2, part), F32, "v")],
        [pltpu.VMEM((max(1, n - 1), tw, rank), BF), pltpu.VMEM((rows2, rank), BF), dma(max(1, n - 1))],
        flops=rows2 * half * rank,
        mib=11,
        after=after,
        ahead=ahead,
    )


def input_grad(s, c, c_o, ex, v, v_first, bias, g, so_far, width, after=(), ahead=()):
    rows, half = c_o.shape
    rank = v.shape[1]
    part = half // 2
    tw = v_first.shape[0]
    n = part // tw
    slots = max(1, min(2, n - 1))
    ng = len(g)

    def body(at_ref, c_ref, co_ref, ex_ref, v_ref, vf_ref, b_ref, *refs, fetch=nothing):
        g_refs, refs = refs[:ng], refs[ng + (so_far is not None) :]
        own_ref, oth_ref, stage, vv, both, sems, v_sem = refs

        def v_copy(k):
            src = v_ref.at[pl.ds(pl.multiple_of(s * part + k * tw, tw), tw), :]
            slot = lax.rem(k - 1, slots)
            return copy(src, vv.at[slot], v_sem.at[slot])

        def columns(k):
            return pl.ds(pl.multiple_of(at_ref[0] * half + s * part + k * tw, tw), tw)

        def out(k):
            slot = lax.rem(k, 2)
            return copy(stage.at[slot], own_ref.at[:, columns(k)], sems.at[slot])

        def block(k, v_block):
            here = at_block(k, tw)
            there = pl.ds(pl.multiple_of(s * part + k * tw, tw), tw)
            bk = lax.dot_general(both[...], v_block, NT, preferred_element_type=F32)
            b = b_ref[:, columns(k)].astype(F32)
            cf, cof = c_ref[:, here].astype(F32), co_ref[:, there].astype(F32)
            stage[lax.rem(k, 2)] = (cf * (ex_ref[:rows, here] + b) + cf + bk[:rows]).astype(BF)
            oth_ref[:, here] = (cof * (ex_ref[rows:, here] + b) + cof + bk[rows:]).astype(BF)
            out(k).start()

        for k in range(1, min(n, slots + 1)):
            v_copy(k).start()
        fetch()
        fill(at_ref, both, g_refs)
        block(0, vf_ref[...])

        @pl.loop(1, n)
        def _(k):
            v_copy(k).wait()

            @pl.when(k >= 2)
            def _():
                out(k - 2).wait()

            block(k, vv[lax.rem(k - 1, slots)])

            @pl.when(k + slots < n)
            def _():
                v_copy(k + slots).start()

        for k in range(max(0, n - 2), n):
            out(k).wait()

    ins = [(c, "v"), (c_o, "v"), (ex, "v"), (v, "h"), (v_first, "v"), (bias, "v")] + [(a, "v") for a in g]
    aliases = {}
    if so_far is not None:
        aliases = {len(ins): 0}
        ins.append((so_far, "h"))
    return call(
        body,
        "input_grad",
        ins,
        [((rows, width), BF, "h"), ((rows, part), BF, "v")],
        [
            pltpu.VMEM((2, rows, tw), BF),
            pltpu.VMEM((slots, tw, rank), BF),
            pltpu.VMEM((2 * rows, rank), BF),
            dma(2),
            dma(slots),
        ],
        flops=2 * rows * half * rank,
        aliases=aliases,
        mib=13,
        after=after,
        ahead=ahead,
    )


def plus(a, b):
    return a.astype(F32) + b.astype(F32)


def pair_halves(a, b, direct, after=()):
    rows, rank = a.shape

    def body(at_ref, a_ref, b_ref, *outs):
        write_halves(at_ref, lambda here: plus(a_ref[here, :], b_ref[here, :]), outs)

    return call(body, "pair_halves", [(a, "v"), (b, "v")], halves_of(rows, rank, direct), after=after)


def pieces_of(a, b, m, after=(), carry=()):
    rows, rank = a.shape
    each = rows // m

    def body(at_ref, a_ref, b_ref, *outs):
        for d in range(m):
            here = at_block((at_ref[1] >> 1) ^ d, each)
            outs[d][...] = plus(a_ref[here, :], b_ref[here, :]).astype(outs[d].dtype)

    return call(body, "pieces_of", [(a, "v"), (b, "v")], [((each, rank), F32 if d == 0 else BF, "v") for d in range(m)], after=after, carry=carry)


def add_pieces(parts, after=(), carry=()):
    def body(at_ref, *refs):
        total = refs[0][...].astype(F32)
        for r in refs[1:-1]:
            total += r[...].astype(F32)
        refs[-1][...] = total.astype(BF)

    return call(body, "add_pieces", [(a, "v") for a in parts], [(parts[0].shape, BF, "v")], after=after, carry=carry)


def join_pieces(parts, after=(), carry=()):
    m = len(parts)
    each, rank = parts[0].shape

    def body(at_ref, *refs):
        for d in range(m):
            refs[-1][at_block((at_ref[1] >> 1) ^ d, each), :] = refs[d][...]

    return call(body, "join_pieces", [(a, "v") for a in parts], [((m * each, rank), BF, "v")], after=after, carry=carry)


def hold(a, after):
    def body(at_ref, a_ref, o_ref):
        pass

    return call(body, "hold", [(a, "v")], [(a.shape, a.dtype, "v")], aliases={0: 0}, after=after)[0]


def solution(mesh):
    n = mesh.shape["col"]
    m = n // 2
    swap = [(0, 1), (1, 0)]

    def trade(a):
        return lax.ppermute(a, "batch", swap)

    def to(a, d):
        return lax.ppermute(a, "col", [(i, i ^ d) for i in range(n)])

    def spread(parts):
        return [parts[0]] + [to(parts[d], 2 * d) for d in range(1, m)]

    def local(x, c, u, v, bias):
        half, width = u.shape[0], x.shape[1]
        direct = x.shape[0] % (16 * n) == 0 and n & (n - 1) == 0 and n > 2

        def plain(total):
            total = lax.psum(total, "col").astype(BF)
            return [trade(total), total]

        part = half // 2
        tw = min(1024, part)
        x_s = cut_half(x, half)
        x_o = trade(x_s)
        own, x_own, *v_in = project_own(x, v, [x_s])
        theirs = trade(own)
        c_o = trade(hold(cut_half(c, half, [own]), [theirs]))
        *sums, c0, u0 = project_other(x_o, v_in, theirs, c, u, direct)
        acc, b0, c1, u1 = back_project(0, 4, x_own, x_o, c0, c_o, u, u0, None, c)
        if direct:
            parts = pieces_of(sums[0], to(sums[1], 1), m, [acc])
            acc, b1, u1 = back_project(4, 2, x_own, x_o, c1, c_o, u, u1, acc, after=[parts[0]])
            (h_t0,) = turn_hidden(0, x_own, x_o, c0, c_o, [acc])
            (total,) = add_pieces(spread(parts), [h_t0])
            own_g, mine_g, b2 = back_project(6, 2, x_own, x_o, c1, c_o, u, u1, acc, after=[total])
            (h_t1,) = turn_hidden(1, x_own, x_o, c1, c_o, [mine_g])
            half_p, own_g = join_pieces(spread([total] * m), [h_t1], [own_g])
            other_p = to(half_p, 1)
            x_t = turn_x(x_own, x_o, [half_p])
            sums_g = pair_halves(mine_g, trade(own_g), direct, [(x_t, "h")])
            other_p = hold(other_p, [(x_t, "h")])
            grad_b = jnp.concatenate([b0[0], b1[0], b2[0]])
            p = [trade(half_p), trade(other_p), half_p, other_p]
            (grad_u,) = factor_grad("u_grad", 0, half, h_t0, p, None, after=[(x_t, "h")])
            parts_g = pieces_of(sums_g[0], to(sums_g[1], 1), m, [(grad_u, "h")])
            grad_u, u0 = factor_grad("u_grad", 1, half, h_t1, p, grad_u, after=[parts_g[0]], ahead=[(u, 0, tw)])
            (total_g,) = add_pieces(spread(parts_g), [(grad_u, "h")])
            ex0, u1 = expand(0, u, u0, p, [total_g], [(u, part, tw)])
            (half_g,) = join_pieces(spread([total_g] * m), [ex0])
            other_g = to(half_g, 1)
            ex1, v0 = expand(1, u, u1, p, [half_g], [(v, 0, tw)])
            other_g = hold(other_g, [ex1])
            g = [trade(half_g), trade(other_g), half_g, other_g]
        else:
            acc, b1, u1 = back_project(4, 2, x_own, x_o, c1, c_o, u, u1, acc)
            own_g, mine_g, b2 = back_project(6, 2, x_own, x_o, c1, c_o, u, u1, acc)
            (sums_g,) = pair_halves(mine_g, trade(own_g), direct)
            p, g = plain(sums[0]), plain(sums_g)
            grad_b = jnp.concatenate([b0[0], b1[0], b2[0]])
            x_t = turn_x(x_own, x_o)
            (h_t0,) = turn_hidden(0, x_own, x_o, c0, c_o)
            (h_t1,) = turn_hidden(1, x_own, x_o, c1, c_o)
            (grad_u,) = factor_grad("u_grad", 0, half, h_t0, p, None)
            grad_u, u0 = factor_grad("u_grad", 1, half, h_t1, p, grad_u, ahead=[(u, 0, tw)])
            ex0, u1 = expand(0, u, u0, p, ahead=[(u, part, tw)])
            ex1, v0 = expand(1, u, u1, p, ahead=[(v, 0, tw)])
        bias = bias[None, :]
        out, oth0, v1 = input_grad(0, c0, c_o, ex0, v, v0, bias, g, None, width, [ex1, (grad_b, "h")], [(v, part, tw)])
        out, oth1, x_t0 = input_grad(1, c1, c_o, ex1, v, v1, bias, g, out, width, ahead=[(x_t, 0, part)])
        back0, back1 = trade(oth0), trade(oth1)
        grad_v, out, x_t1 = factor_grad("v_grad", 0, half, x_t0, g, None, (back0, out), ahead=[(x_t, part, part)], work=0)
        grad_v, out = factor_grad("v_grad", 1, half, x_t1, g, grad_v, (back1, out))
        return out, grad_u, grad_v, grad_b

    return jax.shard_map(
        local,
        mesh=mesh,
        in_specs=(
            P(("group", "batch"), "col"),
            P(("group", "batch"), "col"),
            P(("col", "batch"), None),
            P(("col", "batch"), None),
            P("col"),
        ),
        out_specs=(
            P(("group", "batch"), "col"),
            P(("group", "col", "batch"), None),
            P(("group", "col", "batch"), None),
            P(("group", "col", "batch")),
        ),
        check_vma=False,
    )
```
